32 devices in a mesh: req: 8 (over z, x), head: 4 (over y, core).
Axes of the slice: x: 2, y: 2, z: 4, core: 2. Of those that a mesh axis runs over, the one named last changes fastest.
Arguments:
- token_ids: int32 [256, 4], P('req'), may hold values from 0 to 31999
- state_perm: int32 [256], P('req'), may hold values from 0 to 255, as said below
- token_count: int32 [256], P('req'), may hold values from 1 to 4
- tenant_bounds: int32 [5], replicated, may hold values from 0 to 256, as said below
- old_states: bfloat16 [256, 16, 128, 128], P('req', 'head'), may hold values from -6 to 6
- embedding: bfloat16 [32000, 2048], P('req', 'head'), may hold values from -6 to 6
- mixer_gain: float32 [2048], replicated, may hold values from 0.5 to 1.5
- query_weight: bfloat16 [2048, 2048], P(None, 'head'), may hold values from -0.125 to 0.125
- forget_weight: bfloat16 [2048, 2048], P(None, 'head'), may hold values from -0.125 to 0.125
- input_weight: bfloat16 [2048, 2048], P(None, 'head'), may hold values from -0.125 to 0.125
- forget_floor: float32 [2048], P('head'), may hold values from 0 to 0.9
- group_gain: float32 [2048], P('head'), may hold values from 0.5 to 1.5
- output_weight: bfloat16 [2048, 2048], P('head'), may hold values from -0.125 to 0.125
- feed_gain: float32 [2048], replicated, may hold values from 0.5 to 1.5
- gate_weight: bfloat16 [2048, 5632], P('head', 'req'), may hold values from -0.125 to 0.125
- up_weight: bfloat16 [2048, 5632], P('head', 'req'), may hold values from -0.125 to 0.125
- down_weight: bfloat16 [5632, 2048], P('req', 'head'), may hold values from -0.078125 to 0.078125
- final_gain: float32 [2048], P('head'), may hold values from 0.5 to 1.5
- tenant_gain: float32 [4, 2048], P(None, 'head'), may hold values from 0.1 to 1.9
- vocab_weight: bfloat16 [2048, 32000], P(None, ('req', 'head')), may hold values from -0.3984375 to 0.3984375
Outputs:
- hidden: float32 [256, 4, 2048], P('req', None, 'head')
- new_states: bfloat16 [256, 16, 128, 128], P('req', 'head')
- last_norm: float32 [256], P('req')
- greatest: float32 [256], P('req')
The draws below stay inside these ranges and needn't reach their ends.
Inputs may be any that keep to these rules, and one draw needn't show every extreme that they name: A permutation of the 256 slots: new slot n takes the state of old slot state_perm[n]. The 32 new slots k * 32 to k * 32 + 31 take exactly 4 old slots from each aligned block of 32 old slots. `tenant_bounds`: entry 0 is 0, entry 4 is 256, and the entries rise strictly.
All inputs are finite; a program needn't handle non-finite values.
Results may differ from the reference program's by a relative error of at most 0.018.
Values may be sent and summed in bfloat16 or wider, within the bound.
No kernel may reach another device: no remote copies, remote signals or barrier semaphores. Data moves between devices by JAX's collectives and lax.ppermute only.
A program may use at most 128 MiB of HBM per device.

```python
import math
from functools import partial
import jax
import jax.numpy as jnp
import numpy as np
from jax import lax

D = 2048
HEADS = 16
HEAD_DIM = 128
FF = 5632
VOCAB = 32000
RDEV = 32
POS = 4
TENANTS = 4
REQUESTS = 256
SENDS = 4
TOKENS = 1024
N_REQ = 8
N_HEAD = 4


def shuffle(one_key):
    return jax.random.permutation(one_key, RDEV)


def draw_state_perm(key, part):
    blocks = REQUESTS // RDEV
    source_key, dest_key = jax.random.split(jax.random.fold_in(key, 11))
    source_order = jax.vmap(shuffle)(jax.random.split(source_key, blocks))
    dest_order = jax.vmap(shuffle)(jax.random.split(dest_key, blocks))
    source_block = dest_order // SENDS
    within = dest_order % SENDS
    dest_block = jnp.arange(blocks)[:, None]
    local_slot = source_order[source_block, dest_block * SENDS + within]
    return (source_block * RDEV + local_slot).reshape(-1).astype(jnp.int32)


def draw_tenant_bounds(key, part):
    cuts = jax.random.permutation(jax.random.fold_in(key, 13), REQUESTS - 1)[:TENANTS - 1] + 1
    inner = jnp.sort(cuts).astype(jnp.int32)
    return jnp.concatenate([jnp.zeros((1,), jnp.int32), inner, jnp.full((1,), REQUESTS, jnp.int32)])


def with_ends(entries, key, smallest, top_value):
    longest = entries.shape.index(max(entries.shape))
    spots = []
    for shift in (0, 1):
        where = [jax.random.randint(jax.random.fold_in(key, axis), (), 0, length) for axis, length in enumerate(entries.shape)]
        where[longest] = (where[longest] + shift) % entries.shape[longest]
        spots.append(tuple(where))
    return entries.at[spots[0]].set(smallest).at[spots[1]].set(top_value)


def shard_levels(key, shape, pieces, smallest, largest):
    level, own = 1.0, jax.random.fold_in(key, 6)
    for axis_at, parts in pieces:
        draws = jnp.exp(jax.random.uniform(jax.random.fold_in(own, axis_at), (parts,), jnp.float32, smallest / len(pieces), largest / len(pieces)))
        level = level * jnp.repeat(draws, shape[axis_at] // parts).reshape([-1 if axis == axis_at else 1 for axis in range(len(shape))])
    return level


def cumulative_ranks(number_of, skew):
    loads = [(1 << 20) // math.isqrt(standing ** skew) + 1 for standing in range(1, number_of + 1)]
    spread = 1 + sum(loads) // (1 << 30)
    return np.cumsum(np.array([max(1, weight // spread) for weight in loads]))


def ranked_ids(own_key, dims, amount, lean):
    grid = cumulative_ranks(amount, lean)
    pick = jax.random.randint(jax.random.fold_in(own_key, 1), dims, 0, int(grid[amount - 1]))
    grade = jnp.searchsorted(jnp.asarray(grid, jnp.int32), pick, side="right")
    return jax.random.permutation(jax.random.fold_in(own_key, 2), amount)[grade].astype(jnp.int32)


def noise(key, dims, deviation, reach, shards=(), held_as=jnp.bfloat16):
    loudness = shard_levels(key, dims, shards, -0.22, 0.18) if shards else 1.0
    result = jax.random.normal(key, dims, jnp.float32) * deviation * loudness
    return jnp.minimum(jnp.maximum(result, -reach), reach).astype(held_as)


def setup_inputs(seed: int = 0) -> dict:
    splits = jax.random.split(jax.random.key(seed), 21)
    token_ids = with_ends(ranked_ids(splits[0], (REQUESTS, POS), VOCAB, 2), jax.random.fold_in(splits[0], 3), 0, VOCAB - 1).astype(jnp.int32)
    state_perm = draw_state_perm(jax.random.fold_in(splits[20], 71), 0)
    token_count = with_ends(jax.random.randint(splits[2], (REQUESTS,), 1, POS + 1), jax.random.fold_in(splits[2], 1), 1, POS).astype(jnp.int32)
    tenant_bounds = draw_tenant_bounds(jax.random.fold_in(splits[20], 71), 0)
    old_states = noise(splits[4], (REQUESTS, HEADS, HEAD_DIM, HEAD_DIM), 1.0, 6.0, ((0, 8), (1, 4)))
    embedding = noise(splits[5], (VOCAB, D), 1.0, 6.0, ((0, 8), (1, 4)))
    mixer_gain = jnp.clip(1.0 + 0.1 * jax.random.normal(splits[6], (D,), jnp.float32), 0.5, 1.5)
    query_weight = noise(splits[7], (D, D), D ** -0.5, 0.125, ((1, 4),))
    forget_weight = noise(splits[8], (D, D), D ** -0.5, 0.125, ((1, 4),))
    input_weight = noise(splits[9], (D, D), D ** -0.5, 0.125, ((1, 4),))
    forget_floor = jnp.clip(0.9 * jax.random.uniform(splits[10], (D,), jnp.float32) ** shard_levels(splits[10], (D,), ((0, 4),), -0.2, 0.2), 0.0, 0.9)
    group_gain = jnp.clip(1.0 + 0.1 * jax.random.normal(splits[11], (D,), jnp.float32), 0.5, 1.5)
    output_weight = noise(splits[12], (D, D), D ** -0.5, 0.125, ((0, 4),))
    feed_gain = jnp.clip(1.0 + 0.1 * jax.random.normal(splits[13], (D,), jnp.float32), 0.5, 1.5)
    gate_weight = noise(splits[14], (D, FF), D ** -0.5, 0.125, ((0, 4), (1, 8)))
    up_weight = noise(splits[15], (D, FF), D ** -0.5, 0.125, ((0, 4), (1, 8)))
    down_weight = noise(splits[16], (FF, D), FF ** -0.5, 0.078125, ((0, 8), (1, 4)))
    final_gain = jnp.clip(1.0 + 0.1 * jax.random.normal(splits[17], (D,), jnp.float32), 0.5, 1.5)
    tenant_gain = jnp.clip(1.0 + 0.18 * jax.random.normal(splits[18], (TENANTS, D), jnp.float32), 0.1, 1.9)
    vocab_weight = noise(splits[19], (D, VOCAB), 0.066, 0.3984375, ((1, 32),))
    return {"token_ids": token_ids, "state_perm": state_perm, "token_count": token_count, "tenant_bounds": tenant_bounds, "old_states": old_states, "embedding": embedding, "mixer_gain": mixer_gain, "query_weight": query_weight, "forget_weight": forget_weight, "input_weight": input_weight, "forget_floor": forget_floor, "group_gain": group_gain, "output_weight": output_weight, "feed_gain": feed_gain, "gate_weight": gate_weight, "up_weight": up_weight, "down_weight": down_weight, "final_gain": final_gain, "tenant_gain": tenant_gain, "vocab_weight": vocab_weight}


epsilon = 1e-06

def norm_scale(values):
    return lax.rsqrt(lax.optimization_barrier(jnp.mean(values * values, axis=-1, keepdims=True)) + epsilon)

def rounded(values):
    return lax.optimization_barrier(values.astype(jnp.bfloat16)).astype(jnp.float32)

def recur_block(block):
    start_state, query_act, forget_gate, key_part, value_part = block
    state_now = start_state.astype(jnp.float32)
    outputs = []
    for position in range(POS):
        state_now = forget_gate[:, position, :, :, None] * state_now + key_part[:, position, :, :, None] * value_part[:, position, :, None, :]
        outputs.append(jnp.einsum('rhk,rhkv->rhv', query_act[:, position], state_now, precision=lax.Precision.HIGHEST))
    return (jnp.stack(outputs, axis=1), state_now.astype(jnp.bfloat16))

def split_heads(values):
    return values.reshape(REQUESTS // RDEV, RDEV, POS, HEADS, HEAD_DIM)

def block_best(rows_block, vocab_weight):
    return lax.optimization_barrier(jnp.max(jnp.dot(rows_block, vocab_weight, preferred_element_type=jnp.float32), axis=1))

def reference(token_ids, state_perm, token_count, tenant_bounds, old_states, embedding, mixer_gain, query_weight, forget_weight, input_weight, forget_floor, group_gain, output_weight, feed_gain, gate_weight, up_weight, down_weight, final_gain, tenant_gain, vocab_weight):
    embedded = jnp.take(embedding, token_ids.reshape(-1).astype(jnp.int32), axis=0)
    stream = embedded.astype(jnp.float32)
    normed = (stream * norm_scale(stream) * mixer_gain).astype(jnp.bfloat16)
    query_raw = jnp.dot(normed, query_weight, preferred_element_type=jnp.float32)
    forget_raw = jnp.dot(normed, forget_weight, preferred_element_type=jnp.float32)
    value_part = jnp.dot(normed, input_weight, preferred_element_type=jnp.float32)
    query_act = query_raw * jax.nn.sigmoid(query_raw) * HEAD_DIM ** (-0.5)
    live_mask = (jnp.arange(POS)[None, :] < token_count[:, None]).reshape(TOKENS, 1)
    forget_gate = jnp.where(live_mask, forget_floor + (1.0 - forget_floor) * jax.nn.sigmoid(forget_raw), 1.0)
    key_part = 1.0 - forget_gate
    start_state = jnp.take(old_states, state_perm.astype(jnp.int32), axis=0).reshape(REQUESTS // RDEV, RDEV, HEADS, HEAD_DIM, HEAD_DIM)
    mixed_out, new_states = lax.map(recur_block, (start_state, split_heads(query_act), split_heads(forget_gate), split_heads(key_part), split_heads(value_part)))
    mixed_out = mixed_out.reshape(TOKENS, D)
    new_states = new_states.reshape(REQUESTS, HEADS, HEAD_DIM, HEAD_DIM)
    grouped = (mixed_out * norm_scale(mixed_out) * group_gain).astype(jnp.bfloat16)
    after_mixer = stream + jnp.dot(grouped, output_weight, preferred_element_type=jnp.float32)
    feed_in = (after_mixer * norm_scale(after_mixer) * feed_gain).astype(jnp.bfloat16)
    width_head = D // N_HEAD
    gate_sum = jnp.zeros((TOKENS, FF), jnp.float32)
    up_sum = jnp.zeros((TOKENS, FF), jnp.float32)
    for block_index in range(N_HEAD):
        rows_in = feed_in[:, block_index * width_head:(block_index + 1) * width_head]
        gate_sum = gate_sum + rounded(jnp.dot(rows_in, gate_weight[block_index * width_head:(block_index + 1) * width_head], preferred_element_type=jnp.float32))
        up_sum = up_sum + rounded(jnp.dot(rows_in, up_weight[block_index * width_head:(block_index + 1) * width_head], preferred_element_type=jnp.float32))
    activated = (jax.nn.silu(gate_sum) * up_sum).astype(jnp.bfloat16)
    width_units = FF // N_REQ
    feed_out = jnp.zeros((TOKENS, D), jnp.float32)
    for block_index in range(N_REQ):
        feed_out = feed_out + rounded(jnp.dot(activated[:, block_index * width_units:(block_index + 1) * width_units], down_weight[block_index * width_units:(block_index + 1) * width_units], preferred_element_type=jnp.float32))
    hidden = after_mixer + feed_out
    mean_square = lax.optimization_barrier(jnp.mean(hidden * hidden, axis=-1))
    tenant_index = lax.optimization_barrier(jnp.sum((jnp.arange(REQUESTS)[:, None] >= tenant_bounds[None, 1:TENANTS]).astype(jnp.int32), axis=1))
    token_gain = jnp.repeat(jnp.take(tenant_gain, tenant_index.astype(jnp.int32), axis=0), POS, axis=0)
    final_hidden = (hidden * lax.rsqrt(mean_square + epsilon)[:, None] * final_gain * token_gain).astype(jnp.bfloat16)
    last_pick = jnp.arange(POS)[None, :] == (token_count - 1)[:, None]
    last_norm = jnp.sqrt(lax.optimization_barrier(jnp.sum(jnp.where(last_pick, mean_square.reshape(REQUESTS, POS), 0.0), axis=1)) + epsilon)
    token_best = lax.map(partial(block_best, vocab_weight=vocab_weight), final_hidden.reshape(REQUESTS // RDEV, RDEV * POS, D))
    live_all = jnp.arange(POS)[None, :] < token_count[:, None]
    greatest = lax.optimization_barrier(jnp.max(jnp.where(live_all, token_best.reshape(REQUESTS, POS), -1e+30), axis=1))
    return (hidden.reshape(REQUESTS, POS, D), new_states, last_norm, greatest)
```

```python
import functools

import jax
import jax.numpy as jnp
import numpy as np
from jax import lax
from jax.experimental import pallas as pl
from jax.experimental.pallas import tpu as pltpu
from jax.sharding import PartitionSpec as P

D = 2048
HEAD_DIM = 128
epsilon = 1e-06
F32 = jnp.float32
BF16 = jnp.bfloat16
VMEM = pltpu.VMEM
SMEM = pltpu.SMEM


def swap(x, axis, size, offset):
    return lax.ppermute(x, axis, [(i, i ^ offset) for i in range(size)])


def bf16_parts(x):
    high = lax.reduce_precision(x, 8, 7)
    return high.astype(BF16), (x - high).astype(BF16)


def sort_kernel(sends, order_ref, old_ref, *rest):
    outs, sems = rest[:-1], rest[-1]
    copies = []
    for k, out in enumerate(outs):
        for rank in range(sends):
            at = k * sends + rank
            copies.append(
                pltpu.make_async_copy(old_ref.at[order_ref[at]], out.at[rank], sems.at[at])
            )
    for copy in copies:
        copy.start()
    for copy in copies:
        copy.wait()


def sort_states(order, old_states, owners):
    requests = old_states.shape[0]
    sends = requests // owners
    piece = jax.ShapeDtypeStruct((sends,) + old_states.shape[1:], old_states.dtype)
    return pl.pallas_call(
        functools.partial(sort_kernel, sends),
        out_shape=[piece] * owners,
        in_specs=[pl.BlockSpec(memory_space=SMEM), pl.BlockSpec(memory_space=pl.ANY)],
        out_specs=[pl.BlockSpec(memory_space=pl.ANY)] * owners,
        scratch_shapes=[pltpu.SemaphoreType.DMA((requests,))],
    )(order, old_states)


def roll(x, by):
    return pltpu.roll(x, by % x.shape[0], 0)


def mixer_kernel(
    owners, sends, heads, classes, steps,
    me_ref, emb_ref, live_ref, gain_ref, qw_ref, fw_ref, iw_ref, floor_ref, ggain_ref, ow_ref,
    *rest,
):
    states = rest[:owners]
    own_ref, parts, kv_ref = rest[owners], rest[owners + 1 : owners + 1 + classes], rest[owners + 1 + classes]
    qhi_ref, qlo_ref, mixed_ref, part_ref = rest[owners + 2 + classes :]
    tokens = live_ref.shape[0]
    requests = tokens // steps
    group = requests // classes
    rows = group * steps
    stream = emb_ref[0:tokens, :].astype(F32)
    scale = lax.rsqrt(jnp.mean(stream * stream, axis=1, keepdims=True) + epsilon)
    normed = (stream * scale * gain_ref[...]).astype(BF16)
    query = jnp.dot(normed, qw_ref[...], preferred_element_type=F32)
    query = query * jax.nn.sigmoid(query) * HEAD_DIM ** (-0.5)
    forget_raw = jnp.dot(normed, fw_ref[...], preferred_element_type=F32)
    value = jnp.dot(normed, iw_ref[...], preferred_element_type=F32)
    floor = floor_ref[...]
    forget = jnp.where(
        live_ref[...] > 0.0, floor + (1.0 - floor) * jax.nn.sigmoid(forget_raw), 1.0
    )
    key = 1.0 - forget
    step = lax.broadcasted_iota(jnp.int32, forget.shape, 0) % steps
    upto = forget * jnp.where(step >= 1, roll(forget, 1), 1.0)
    upto = upto * jnp.where(step >= 2, roll(upto, 2), 1.0)
    after = jnp.where(step <= steps - 2, roll(forget, -1), 1.0)
    after = after * jnp.where(step <= steps - 3, roll(forget, -2), 1.0)
    after = after * jnp.where(step <= steps - 4, roll(forget, -3), 1.0)
    carried = query * upto
    high = carried.astype(BF16).astype(F32)
    qhi_ref[...] = high
    qlo_ref[...] = carried - high
    lag_key, lag_value = key, value
    local = [jnp.zeros((tokens, HEAD_DIM), F32) for _ in range(heads)]
    for lag in range(steps):
        if lag:
            lag_key = roll(lag_key, 1) * forget
            lag_value = roll(lag_value, 1)
        product = jnp.where(step >= lag, query * lag_key, 0.0)
        for head in range(heads):
            cols = slice(head * HEAD_DIM, (head + 1) * HEAD_DIM)
            weight = jnp.sum(product[:, cols], axis=1, keepdims=True)
            local[head] = local[head] + weight * lag_value[:, cols]
    for head in range(heads):
        mixed_ref[:, head * HEAD_DIM : (head + 1) * HEAD_DIM] = local[head]
    upper = lax.broadcasted_iota(jnp.int32, (8, HEAD_DIM), 0) < steps
    for tile in range(tokens // 8):
        for head in range(heads):
            cols = slice(head * HEAD_DIM, (head + 1) * HEAD_DIM)
            at = slice(tile * 8, tile * 8 + 8)
            left = jnp.concatenate([qhi_ref[at, cols], qlo_ref[at, cols]], axis=0).astype(BF16)
            got = []
            for request in (2 * tile, 2 * tile + 1):
                place = (request % group) * classes + request // group
                old = states[place // sends][place % sends, head]
                product = jnp.dot(left, old, preferred_element_type=F32)
                got.append(product[0:8] + product[8:16])
            mixed_ref[at, cols] += jnp.where(upper, got[0], got[1])
    mixed = mixed_ref[...]
    square = jnp.sum(mixed * mixed, axis=1, keepdims=True)
    part_ref[:, 0:D] = jnp.dot(
        (mixed * ggain_ref[...]).astype(BF16), ow_ref[...], preferred_element_type=F32
    )
    square_high = square.astype(BF16).astype(F32)
    lane = lax.broadcasted_iota(jnp.int32, (tokens, 128), 1)
    part_ref[:, D : D + 128] = jnp.where(lane < 64, square_high, square - square_high)
    me = me_ref[0]
    for e in range(classes):
        first = pl.multiple_of((me ^ e) * rows, rows)
        parts[e][...] = part_ref[pl.ds(first, rows), :].astype(BF16)
    own_ref[...] = emb_ref[pl.ds(pl.multiple_of(me * rows, rows), rows), :]
    both = jnp.concatenate([(key * after).astype(BF16), value.astype(BF16)], axis=0)
    shape = (2 * tokens, 2 * tokens)
    target = lax.broadcasted_iota(jnp.int32, shape, 0)
    source = lax.broadcasted_iota(jnp.int32, shape, 1)
    place, within = target // (2 * steps), target % (2 * steps)
    request = (place % classes) * group + place // classes
    wanted = request * steps + within % steps + jnp.where(within >= steps, tokens, 0)
    pick = jnp.where(source == wanted, 1.0, 0.0).astype(BF16)
    kv_ref[...] = jnp.dot(pick, both, preferred_element_type=F32).astype(BF16)


def mixer(me, emb, live, gain, qw, fw, iw, floor, ggain, ow, states, steps, classes):
    tokens = live.shape[0]
    owners, sends, heads = len(states), states[0].shape[0], states[0].shape[1]
    width = qw.shape[1]
    rows = tokens // classes
    vmem = pl.BlockSpec(memory_space=VMEM)
    return pl.pallas_call(
        functools.partial(mixer_kernel, owners, sends, heads, classes, steps),
        out_shape=[jax.ShapeDtypeStruct((rows, D), BF16)]
        + [jax.ShapeDtypeStruct((rows, D + 128), BF16)] * classes
        + [jax.ShapeDtypeStruct((2 * tokens, width), BF16)],
        in_specs=[pl.BlockSpec(memory_space=SMEM)] + [vmem] * (9 + owners),
        out_specs=[vmem] * (classes + 2),
        scratch_shapes=[
            VMEM((tokens, width), F32),
            VMEM((tokens, width), F32),
            VMEM((tokens, width), F32),
            VMEM((tokens, D + 128), F32),
        ],
        compiler_params=pltpu.CompilerParams(vmem_limit_bytes=40 << 20),
    )(me, emb, live, gain, qw, fw, iw, floor, ggain, ow, *states)


def update_kernel(owners, sends, heads, steps, slot_ref, kv_ref, *rest):
    states, out_ref = rest[:owners], rest[owners]
    diagonal = lax.broadcasted_iota(jnp.int32, (HEAD_DIM, HEAD_DIM), 0) == lax.broadcasted_iota(
        jnp.int32, (HEAD_DIM, HEAD_DIM), 1
    )
    first = lax.broadcasted_iota(jnp.int32, (2 * steps, HEAD_DIM), 0) < steps
    for k in range(owners):
        for rank in range(sends):
            place = k * sends + rank
            slot = slot_ref[place]
            for head in range(heads):
                cols = slice(head * HEAD_DIM, (head + 1) * HEAD_DIM)
                both = kv_ref[place, :, cols]
                key = jnp.where(first, both, 0.0)
                value = jnp.where(first, roll(both, steps), 0.0)
                kept = 1.0 - jnp.sum(key, axis=0, keepdims=True)
                keep = jnp.where(diagonal, kept, 0.0).astype(BF16)
                fresh = lax.dot_general(
                    key, value, (((0,), (0,)), ((), ())), preferred_element_type=F32
                )
                old = jnp.dot(keep, states[k][rank, head], preferred_element_type=F32)
                out_ref[slot, head] = (old + fresh).astype(BF16)


def update_states(slots, kv, states, steps):
    owners, sends, heads = len(states), states[0].shape[0], states[0].shape[1]
    vmem = pl.BlockSpec(memory_space=VMEM)
    return pl.pallas_call(
        functools.partial(update_kernel, owners, sends, heads, steps),
        out_shape=jax.ShapeDtypeStruct((owners * sends,) + states[0].shape[1:], BF16),
        in_specs=[pl.BlockSpec(memory_space=SMEM)] + [vmem] * (1 + owners),
        out_specs=vmem,
        compiler_params=pltpu.CompilerParams(vmem_limit_bytes=40 << 20),
    )(slots, kv, *states)


def scatter_sum(blocks, n, cut):
    outer = n // 2
    blocks = blocks.reshape((outer, 2) + blocks.shape[1:])
    first, second = blocks[..., :cut], blocks[..., cut:]
    inner_got = swap(first[:, 1], "req", n, 1)
    outer_got = [swap(second[j], "req", n, 2 * j) for j in range(1, outer)]
    first = (first[:, 0].astype(F32) + inner_got.astype(F32)).astype(BF16)
    second = sum([got.astype(F32) for got in outer_got], second[0].astype(F32)).astype(BF16)
    outer_got = [swap(first[j], "req", n, 2 * j) for j in range(1, outer)]
    inner_got = swap(second[1], "req", n, 1)
    first = sum([got.astype(F32) for got in outer_got], first[0].astype(F32))
    second = second[0].astype(F32) + inner_got.astype(F32)
    return jnp.concatenate([first, second], axis=-1)


def exchange(block, dim, n, n_head):
    if dim == "outer":
        got = [swap(block, "req", n, 2 * j) for j in range(1, n // 2)]
    elif dim == "inner":
        got = [swap(block, "req", n, 1)]
    else:
        got = [swap(block, "head", n_head, 2)]
    return jnp.stack([block] + got)


def gather_by(block, dims, order, n, n_head):
    rank = block.ndim
    for dim in dims:
        block = exchange(block, dim, n, n_head)
    at = [dims[::-1].index(dim) for dim in order]
    block = block.transpose(at + list(range(len(dims), len(dims) + rank)))
    return block.reshape((-1,) + block.shape[len(dims) :])


def on_device(
    token_ids, state_perm, token_count, tenant_bounds, old_states, embedding, mixer_gain,
    query_weight, forget_weight, input_weight, forget_floor, group_gain, output_weight, feed_gain,
    gate_weight, up_weight, down_weight, final_gain, tenant_gain, vocab_weight,
):
    requests, steps = token_ids.shape
    n = lax.axis_size("req")
    n_head = lax.axis_size("head")
    r = lax.axis_index("req")
    h = lax.axis_index("head")
    tokens = requests * steps
    everyone = requests * n
    sends = requests // n
    group = requests // n_head
    rows = group * steps
    width = D // n_head

    gate_full = lax.all_gather(gate_weight, "head", axis=0, tiled=True)
    up_full = lax.all_gather(up_weight, "head", axis=0, tiled=True)
    down_full = lax.all_gather(down_weight, "head", axis=0)
    vocab_other = swap(vocab_weight, "head", n_head, 1)

    packed = jnp.concatenate([token_ids.T, state_perm[None], token_count[None]], axis=0)
    packed = lax.all_gather(packed, "req", axis=0).transpose(1, 0, 2).reshape(steps + 2, everyone)
    every = jnp.arange(everyone, dtype=jnp.int32)
    source = packed[steps] // requests
    rank = jnp.sum(
        ((source[None, :] == source[:, None]) & (every[None, :] < every[:, None])).astype(jnp.int32),
        axis=1,
    )
    place = ((every // requests) ^ source) * sends + rank % sends
    at = (source ^ r) * requests + (place % n_head) * group + place // n_head
    chosen = (at[:, None] == every[None, :]).astype(F32)
    ordered = jnp.dot(packed.astype(F32), chosen, precision=lax.Precision.HIGHEST)
    ordered = (ordered + 0.5).astype(jnp.int32)

    ids = ordered[:steps].T.reshape(n * tokens)
    table = embedding.shape[0]
    local_ids = ids - r * table
    inside = (local_ids >= 0) & (local_ids < table)
    picked = jnp.take(embedding, jnp.clip(local_ids, 0, table - 1), axis=0, mode="clip")
    picked = jnp.where(inside[:, None], picked, jnp.zeros((), BF16)).reshape(n, tokens, width)
    embed_part = scatter_sum(picked, n, width // 2).astype(BF16)

    gains = jnp.concatenate([final_gain[None], tenant_gain], axis=0)
    gains_high, gains_low = bf16_parts(gains)
    extra = jnp.zeros((16 - 2 * gains.shape[0], width), BF16)
    embedded = lax.all_gather(
        jnp.concatenate([embed_part, gains_high, gains_low, extra], axis=0), "head", axis=1, tiled=True
    )
    gains = embedded[tokens : tokens + 5].astype(F32) + embedded[tokens + 5 : tokens + 10].astype(F32)

    old_order = (ordered[steps, :requests] - r * requests).reshape(n_head, group).T.reshape(requests)
    pieces = sort_states(old_order, old_states, n)
    live = (jnp.arange(steps)[None, :] < ordered[steps + 1, :requests][:, None]).astype(F32)
    own, *parts, kv = mixer(
        h[None], embedded, live.reshape(tokens, 1), mixer_gain[None], query_weight, forget_weight,
        input_weight, forget_floor[None], group_gain[None], output_weight, pieces, steps, n_head,
    )
    arrived = [pieces[0]] + [swap(pieces[k], "req", n, k) for k in range(1, n)]
    kv = kv.reshape(n, sends, 2 * steps, width)
    arrived_kv = jnp.stack([kv[0]] + [swap(kv[k], "req", n, k) for k in range(1, n)])

    total = parts[0].astype(F32)
    for e in range(1, n_head):
        total = total + swap(parts[e], "head", n_head, e).astype(F32)
    square = total[:, D : D + 1] + total[:, D + 127 : D + 128]
    after_mixer = own.astype(F32) + total[:, :D] * lax.rsqrt(square / D + epsilon)

    cut = D * 11 // 16
    after_mixer = after_mixer.astype(BF16)
    everything = jnp.concatenate(
        [
            gather_by(after_mixer[:, :cut], ["outer", "inner"], ["outer", "inner"], n, n_head),
            gather_by(after_mixer[:, cut:], ["inner", "outer"], ["outer", "inner"], n, n_head),
        ],
        axis=-1,
    ).reshape(n * rows, D)
    stream = everything.astype(F32)
    scale = lax.rsqrt(jnp.mean(stream * stream, axis=1, keepdims=True) + epsilon)
    feed_in = (stream * scale * feed_gain).astype(BF16)
    gate = jnp.dot(feed_in, gate_full, preferred_element_type=F32)
    up = jnp.dot(feed_in, up_full, preferred_element_type=F32)
    activated = (jax.nn.silu(gate) * up).astype(BF16)

    row = jnp.arange(n * rows, dtype=jnp.int32)
    by_owner, by_group, by_step = row // rows, (row % rows) // steps, row % steps
    if sends % n_head == 0:
        offset = by_group * n_head // sends
    else:
        offset = (by_group * n_head + h) // sends
    wanted = (by_owner ^ offset) * rows + by_group * steps + by_step
    pick = (wanted[:, None] == row[None, :]).astype(BF16)
    activated = jnp.dot(pick, activated, preferred_element_type=F32).astype(BF16)
    kept = jnp.dot(pick[:rows], everything, preferred_element_type=F32)
    down = jnp.concatenate(
        [jnp.dot(activated, down_full[b], preferred_element_type=F32).astype(BF16) for b in range(n_head)],
        axis=1,
    )
    hidden = kept + scatter_sum(down.reshape(n, rows, D), n, cut)
    mean_square = jnp.mean(hidden * hidden, axis=1, keepdims=True)

    slots = jnp.arange(requests, dtype=jnp.int32)
    source = state_perm // requests
    rank = jnp.sum(
        ((source[None, :] == source[:, None]) & (slots[None, :] < slots[:, None])).astype(jnp.int32),
        axis=1,
    )
    place = (source ^ r) * sends + rank
    slot_of = jnp.sum(jnp.where(place[None, :] == slots[:, None], slots[None, :], 0), axis=1)
    mine = jnp.sum(
        jnp.where(
            place[None, :] == (jnp.arange(group, dtype=jnp.int32) * n_head + h)[:, None],
            slots[None, :],
            0,
        ),
        axis=1,
    )
    tenant = jnp.sum(
        ((mine + r * requests)[:, None] >= tenant_bounds[None, 1:-1]).astype(jnp.int32), axis=1
    )
    tenant_rows = sum(
        jnp.where((tenant == t)[:, None], gains[1 + t][None, :], 0.0)
        for t in range(tenant_gain.shape[0])
    )
    token_gain = jnp.repeat(tenant_rows * gains[0][None, :], steps, axis=0)
    final = (hidden * lax.rsqrt(mean_square + epsilon) * token_gain).astype(BF16)

    order = ["outer", "inner", "head"]
    c1, c2 = D * 6 // 16, D * 11 // 16
    full = jnp.concatenate(
        [
            gather_by(final[:, :c1], ["outer", "inner", "head"], order, n, n_head),
            gather_by(final[:, c1:c2], ["head", "outer", "inner"], order, n, n_head),
            gather_by(final[:, c2:], ["inner", "head", "outer"], order, n, n_head),
        ],
        axis=-1,
    ).reshape(n * 2 * rows, D)
    best = jnp.maximum(
        jnp.max(jnp.dot(full, vocab_weight, preferred_element_type=F32), axis=1),
        jnp.max(jnp.dot(full, vocab_other, preferred_element_type=F32), axis=1),
    ).reshape(n, 2 * rows)
    got = best[0]
    for k in range(1, n):
        got = jnp.maximum(got, swap(best[k], "req", n, k))
    got = lax.all_gather(got, "head", axis=0).reshape(n_head, 2, rows)
    crossed = jnp.stack([got[i ^ 2, 1] for i in range(n_head)])
    best = jnp.maximum(got[:, 0], crossed).reshape(requests, steps)
    index = (place % n_head) * group + place // n_head
    match = (index[:, None] == slots[None, :])[:, :, None]
    best = jnp.sum(jnp.where(match, best[None], 0.0), axis=1)
    live = jnp.arange(steps)[None, :] < token_count[:, None]
    greatest = jnp.max(jnp.where(live, best, -1e30), axis=1)

    blocks = hidden.reshape(rows, n_head, width).transpose(1, 0, 2)
    tail = jnp.broadcast_to(mean_square, (rows, 128))
    whole = []
    for e in range(n_head):
        block = jnp.concatenate(
            [lax.dynamic_index_in_dim(blocks, h ^ e, 0, keepdims=False), tail], axis=1
        )
        whole.append(block if e == 0 else swap(block, "head", n_head, e))
    whole = jnp.stack(whole).reshape(requests, steps, width + 128)
    index = ((place % n_head) ^ h) * group + place // n_head
    whole = jnp.take(whole, index, axis=0, mode="clip")
    last = jnp.arange(steps)[None, :] == (token_count - 1)[:, None]
    last_norm = jnp.sqrt(jnp.sum(jnp.where(last, whole[:, :, width], 0.0), axis=1) + epsilon)

    new_states = update_states(
        slot_of, arrived_kv.reshape(requests, 2 * steps, width).astype(F32), arrived, steps
    )
    return whole[:, :, :width], new_states, last_norm, greatest


def solution(mesh):
    placed = (
        P("req", None),
        P("req"),
        P("req"),
        P(),
        P("req", "head", None, None),
        P("req", "head"),
        P(),
        P(None, "head"),
        P(None, "head"),
        P(None, "head"),
        P("head"),
        P("head"),
        P("head", None),
        P(),
        P("head", "req"),
        P("head", "req"),
        P("req", "head"),
        P("head"),
        P(None, "head"),
        P(None, ("req", "head")),
    )
    return jax.shard_map(
        on_device,
        mesh=mesh,
        in_specs=placed,
        out_specs=(P("req", None, "head"), P("req", "head", None, None), P("req"), P("req")),
        check_vma=False,
    )
```

```python
import functools

import jax
import jax.numpy as jnp
import numpy as np
from jax import lax
from jax.experimental import pallas as pl
from jax.experimental.pallas import tpu as pltpu
from jax.sharding import PartitionSpec as P

D = 2048
HEAD_DIM = 128
epsilon = 1e-06
F32 = jnp.float32
BF16 = jnp.bfloat16
VMEM = pltpu.VMEM
SMEM = pltpu.SMEM


def swap(x, axis, size, offset):
    return lax.ppermute(x, axis, [(i, i ^ offset) for i in range(size)])


def bf16_parts(x):
    high = lax.reduce_precision(x, 8, 7)
    return high.astype(BF16), (x - high).astype(BF16)


def sort_kernel(sends, order_ref, old_ref, *rest):
    outs, held, in_sems, out_sems = rest[:sends], rest[sends], rest[sends + 1], rest[sends + 2]
    owners = held.shape[1]

    def load(rank, owner):
        at = owner * sends + rank
        return pltpu.make_async_copy(
            old_ref.at[order_ref[at]], held.at[rank, owner], in_sems.at[rank, owner]
        )

    def store(rank):
        return pltpu.make_async_copy(held.at[rank], outs[rank], out_sems.at[rank])

    for rank in range(sends):
        for owner in range(owners):
            load(rank, owner).start()
    for rank in range(sends):
        for owner in range(owners):
            load(rank, owner).wait()
        store(rank).start()
    for rank in range(sends):
        store(rank).wait()


def sort_states(order, old_states, owners):
    requests = old_states.shape[0]
    sends = requests // owners
    piece = (owners,) + old_states.shape[1:]
    return pl.pallas_call(
        functools.partial(sort_kernel, sends),
        out_shape=[jax.ShapeDtypeStruct(piece, old_states.dtype)] * sends,
        in_specs=[pl.BlockSpec(memory_space=SMEM), pl.BlockSpec(memory_space=pl.ANY)],
        out_specs=[pl.BlockSpec(memory_space=pl.ANY)] * sends,
        scratch_shapes=[
            VMEM((sends,) + piece, old_states.dtype),
            pltpu.SemaphoreType.DMA((sends, owners)),
            pltpu.SemaphoreType.DMA((sends,)),
        ],
        compiler_params=pltpu.CompilerParams(vmem_limit_bytes=56 << 20),
    )(order, old_states)


def roll(x, by):
    return pltpu.roll(x, by % x.shape[0], 0)


def mixer_kernel(
    sends, owners, heads, classes, steps,
    me_ref, emb_ref, live_ref, gain_ref, floor_ref, ggain_ref, qw_hbm, fw_hbm, iw_hbm, ow_hbm,
    *rest,
):
    states_hbm = rest[:sends]
    own_ref, part_ref, kv_ref = rest[sends : sends + 3]
    qw_ref, fw_ref, iw_ref, ow_ref, states, qhi_ref, qlo_ref, mixed_ref, sems = rest[sends + 3 :]
    weight_pairs = ((qw_hbm, qw_ref), (fw_hbm, fw_ref), (iw_hbm, iw_ref), (ow_hbm, ow_ref))
    loads = [
        pltpu.make_async_copy(there, here, sems.at[i]) for i, (there, here) in enumerate(weight_pairs)
    ]
    state_loads = [
        pltpu.make_async_copy(states_hbm[i], states.at[i], sems.at[4 + i]) for i in range(sends)
    ]
    for load in loads[:3] + state_loads + loads[3:]:
        load.start()
    tokens = live_ref.shape[0]
    requests = tokens // steps
    group = requests // classes
    rows = group * steps
    stream = emb_ref[0:tokens, :].astype(F32)
    scale = lax.rsqrt(jnp.mean(stream * stream, axis=1, keepdims=True) + epsilon)
    normed = (stream * scale * gain_ref[...]).astype(BF16)
    loads[0].wait()
    query = jnp.dot(normed, qw_ref[...], preferred_element_type=F32)
    query = query * jax.nn.sigmoid(query) * HEAD_DIM ** (-0.5)
    loads[1].wait()
    forget_raw = jnp.dot(normed, fw_ref[...], preferred_element_type=F32)
    loads[2].wait()
    value = jnp.dot(normed, iw_ref[...], preferred_element_type=F32)
    floor = floor_ref[...]
    forget = jnp.where(
        live_ref[...] > 0.0, floor + (1.0 - floor) * jax.nn.sigmoid(forget_raw), 1.0
    )
    key = 1.0 - forget
    step = lax.broadcasted_iota(jnp.int32, forget.shape, 0) % steps
    upto = forget * jnp.where(step >= 1, roll(forget, 1), 1.0)
    upto = upto * jnp.where(step >= 2, roll(upto, 2), 1.0)
    after = jnp.where(step <= steps - 2, roll(forget, -1), 1.0)
    after = after * jnp.where(step <= steps - 3, roll(forget, -2), 1.0)
    after = after * jnp.where(step <= steps - 4, roll(forget, -3), 1.0)
    carried = query * upto
    high = carried.astype(BF16).astype(F32)
    qhi_ref[...] = high
    qlo_ref[...] = carried - high
    lag_key, lag_value = key, value
    local = [jnp.zeros((tokens, HEAD_DIM), F32) for _ in range(heads)]
    for lag in range(steps):
        if lag:
            lag_key = roll(lag_key, 1) * forget
            lag_value = roll(lag_value, 1)
        product = jnp.where(step >= lag, query * lag_key, 0.0)
        for head in range(heads):
            cols = slice(head * HEAD_DIM, (head + 1) * HEAD_DIM)
            weight = jnp.sum(product[:, cols], axis=1, keepdims=True)
            local[head] = local[head] + weight * lag_value[:, cols]
    for head in range(heads):
        mixed_ref[:, head * HEAD_DIM : (head + 1) * HEAD_DIM] = local[head]
    for load in state_loads:
        load.wait()
    here = me_ref[0]
    upper = lax.broadcasted_iota(jnp.int32, (8, HEAD_DIM), 0) < steps
    for tile in range(tokens // 8):
        for head in range(heads):
            cols = slice(head * HEAD_DIM, (head + 1) * HEAD_DIM)
            at = slice(tile * 8, tile * 8 + 8)
            left = jnp.concatenate([qhi_ref[at, cols], qlo_ref[at, cols]], axis=0).astype(BF16)
            got = []
            for request in (2 * tile, 2 * tile + 1):
                place = (request % group) * classes + request // group
                old = states[place % sends, here ^ (place // sends), head]
                product = jnp.dot(left, old, preferred_element_type=F32)
                got.append(product[0:8] + product[8:16])
            mixed_ref[at, cols] += jnp.where(upper, got[0], got[1])
    mixed = mixed_ref[...]
    square = jnp.sum(mixed * mixed, axis=1, keepdims=True)
    loads[3].wait()
    part_ref[:, 0:D] = jnp.dot(
        (mixed * ggain_ref[...]).astype(BF16), ow_ref[...], preferred_element_type=F32
    ).astype(BF16)
    square_high = square.astype(BF16).astype(F32)
    lane = lax.broadcasted_iota(jnp.int32, (tokens, 128), 1)
    part_ref[:, D : D + 128] = jnp.where(lane < 64, square_high, square - square_high).astype(BF16)
    own_ref[...] = emb_ref[pl.ds(pl.multiple_of(me_ref[1] * rows, rows), rows), :]
    both = jnp.concatenate([(key * after).astype(BF16), value.astype(BF16)], axis=0)
    shape = (2 * tokens, 2 * tokens)
    target = lax.broadcasted_iota(jnp.int32, shape, 0)
    source = lax.broadcasted_iota(jnp.int32, shape, 1)
    slot, within = target // (2 * steps), target % (2 * steps)
    place = ((slot // sends) ^ here) * sends + slot % sends
    request = (place % classes) * group + place // classes
    wanted = request * steps + within % steps + jnp.where(within >= steps, tokens, 0)
    pick = jnp.where(source == wanted, 1.0, 0.0).astype(BF16)
    kv_ref[...] = jnp.dot(pick, both, preferred_element_type=F32).astype(BF16)


def mixer(me, emb, live, gain, floor, ggain, weights, states, steps, classes):
    tokens = live.shape[0]
    sends, (owners, heads) = len(states), states[0].shape[:2]
    width = floor.shape[1]
    rows = tokens // classes
    vmem, anywhere = pl.BlockSpec(memory_space=VMEM), pl.BlockSpec(memory_space=pl.ANY)
    return pl.pallas_call(
        functools.partial(mixer_kernel, sends, owners, heads, classes, steps),
        out_shape=[
            jax.ShapeDtypeStruct((rows, D), BF16),
            jax.ShapeDtypeStruct((tokens, D + 128), BF16),
            jax.ShapeDtypeStruct((2 * tokens, width), BF16),
        ],
        in_specs=[pl.BlockSpec(memory_space=SMEM)] + [vmem] * 5 + [anywhere] * (4 + sends),
        out_specs=[vmem] * 3,
        scratch_shapes=[VMEM(w.shape, BF16) for w in weights]
        + [
            VMEM((sends,) + states[0].shape, BF16),
            VMEM((tokens, width), F32),
            VMEM((tokens, width), F32),
            VMEM((tokens, width), F32),
            pltpu.SemaphoreType.DMA((4 + sends,)),
        ],
        compiler_params=pltpu.CompilerParams(vmem_limit_bytes=56 << 20),
    )(me, emb, live, gain, floor, ggain, *weights, *states)


def update_kernel(sends, owners, heads, steps, slot_ref, kv_ref, *rest):
    states, out_ref = rest[:sends], rest[sends]
    diagonal = lax.broadcasted_iota(jnp.int32, (HEAD_DIM, HEAD_DIM), 0) == lax.broadcasted_iota(
        jnp.int32, (HEAD_DIM, HEAD_DIM), 1
    )
    first = lax.broadcasted_iota(jnp.int32, (2 * steps, HEAD_DIM), 0) < steps
    for k in range(owners):
        for rank in range(sends):
            place = k * sends + rank
            slot = slot_ref[place]
            for head in range(heads):
                cols = slice(head * HEAD_DIM, (head + 1) * HEAD_DIM)
                both = kv_ref[place, :, cols]
                key = jnp.where(first, both, 0.0)
                value = jnp.where(first, roll(both, steps), 0.0)
                kept = 1.0 - jnp.sum(key, axis=0, keepdims=True)
                keep = jnp.where(diagonal, kept, 0.0).astype(BF16)
                fresh = lax.dot_general(
                    key, value, (((0,), (0,)), ((), ())), preferred_element_type=F32
                )
                old = jnp.dot(keep, states[rank][k, head], preferred_element_type=F32)
                out_ref[slot, head] = (old + fresh).astype(BF16)


def update_states(slots, kv, states, steps):
    sends, (owners, heads) = len(states), states[0].shape[:2]
    vmem = pl.BlockSpec(memory_space=VMEM)
    return pl.pallas_call(
        functools.partial(update_kernel, sends, owners, heads, steps),
        out_shape=jax.ShapeDtypeStruct((owners * sends,) + states[0].shape[1:], BF16),
        in_specs=[pl.BlockSpec(memory_space=SMEM)] + [vmem] * (1 + sends),
        out_specs=vmem,
        compiler_params=pltpu.CompilerParams(vmem_limit_bytes=56 << 20),
    )(slots, kv, *states)


def to_all(x, axis):
    return lax.all_to_all(x, axis, split_axis=0, concat_axis=0, tiled=True)


def tied(x, *others):
    return lax.optimization_barrier((x,) + others)[0]


def on_device(
    token_ids, state_perm, token_count, tenant_bounds, old_states, embedding, mixer_gain,
    query_weight, forget_weight, input_weight, forget_floor, group_gain, output_weight, feed_gain,
    gate_weight, up_weight, down_weight, final_gain, tenant_gain, vocab_weight,
):
    requests, steps = token_ids.shape
    n = lax.axis_size("req")
    n_head = lax.axis_size("head")
    r = lax.axis_index("req")
    h = lax.axis_index("head")
    tokens = requests * steps
    everyone = requests * n
    sends = requests // n
    group = requests // n_head
    rows = group * steps
    width = D // n_head

    packed = jnp.concatenate([token_ids.T, state_perm[None], token_count[None]], axis=0)
    packed = lax.all_gather(packed, "req", axis=0).transpose(1, 0, 2).reshape(steps + 2, everyone)
    every = jnp.arange(everyone, dtype=jnp.int32)
    gate_full = lax.all_gather(tied(gate_weight, packed), "head", axis=0, tiled=True)
    up_full = lax.all_gather(tied(up_weight, packed), "head", axis=0, tiled=True)
    down_full = lax.all_gather(tied(down_weight, packed), "head", axis=0)
    source = packed[steps] // requests
    rank = jnp.sum(
        ((source[None, :] == source[:, None]) & (every[None, :] < every[:, None])).astype(jnp.int32),
        axis=1,
    )
    place = ((every // requests) ^ source) * sends + rank % sends
    at = source * requests + (place % n_head) * group + place // n_head
    chosen = (at[:, None] == every[None, :]).astype(F32)
    ordered = jnp.dot(packed.astype(F32), chosen, precision=lax.Precision.HIGHEST)
    ordered = (ordered + 0.5).astype(jnp.int32)

    ids = ordered[:steps].T.reshape(n * tokens)
    table = embedding.shape[0]
    local_ids = ids - r * table
    inside = (local_ids >= 0) & (local_ids < table)
    picked = jnp.take(embedding, jnp.clip(local_ids, 0, table - 1), axis=0, mode="clip")
    picked = jnp.where(inside[:, None], picked, jnp.zeros((), BF16)).reshape(n, tokens, width)
    embed_part = jnp.sum(to_all(picked, "req").astype(F32), axis=0).astype(BF16)
    vocab_other = swap(tied(vocab_weight, embed_part), "head", n_head, 1)

    gains = jnp.concatenate([final_gain[None], tenant_gain], axis=0)
    gains_high, gains_low = bf16_parts(gains)
    extra = jnp.zeros((16 - 2 * gains.shape[0], width), BF16)
    embedded = lax.all_gather(
        jnp.concatenate([embed_part, gains_high, gains_low, extra], axis=0), "head", axis=1, tiled=True
    )
    gains = embedded[tokens : tokens + 5].astype(F32) + embedded[tokens + 5 : tokens + 10].astype(F32)

    ordered = lax.dynamic_slice_in_dim(ordered, r * requests, requests, 1)
    old_order = (ordered[steps] - r * requests).reshape(n_head, group).T.reshape(n, sends)
    old_order = jnp.take(old_order, jnp.arange(n) ^ r, axis=0).reshape(requests)
    pieces = sort_states(old_order, old_states, n)
    live = (jnp.arange(steps)[None, :] < ordered[steps + 1][:, None]).astype(F32)
    own, parts, kv = mixer(
        jnp.stack([r, h]), embedded, live.reshape(tokens, 1), mixer_gain[None], forget_floor[None],
        group_gain[None], (query_weight, forget_weight, input_weight, output_weight), pieces,
        steps, n_head,
    )
    arrived = [
        to_all(tied(piece, embed_part), "req") for piece in pieces[: (sends + 1) // 2]
    ]

    total = jnp.sum(to_all(parts.reshape(n_head, rows, D + 128), "head").astype(F32), axis=0)
    square = total[:, D : D + 1] + total[:, D + 127 : D + 128]
    after_mixer = own.astype(F32) + total[:, :D] * lax.rsqrt(square / D + epsilon)
    after_mixer = tied(after_mixer.astype(BF16), *arrived)
    half = D // 2
    everything = jnp.concatenate(
        [lax.all_gather(after_mixer[:, at : at + half], "req", axis=0) for at in (0, half)], axis=-1
    ).reshape(n * rows, D)
    arrived_kv = to_all(tied(kv, everything).reshape(n, -1, width), "req")
    if sends >= 4:
        arrived += [to_all(tied(pieces[2], everything), "req")]
    stream = everything.astype(F32)
    scale = lax.rsqrt(jnp.mean(stream * stream, axis=1, keepdims=True) + epsilon)
    feed_in = (stream * scale * feed_gain).astype(BF16)
    gate = jnp.dot(feed_in, gate_full, preferred_element_type=F32)
    up = jnp.dot(feed_in, up_full, preferred_element_type=F32)
    activated = (jax.nn.silu(gate) * up).astype(BF16)

    row = jnp.arange(n * rows, dtype=jnp.int32)
    by_owner, by_group, by_step = row // rows, (row % rows) // steps, row % steps
    if sends % n_head == 0:
        offset = by_group * n_head // sends
    else:
        offset = (by_group * n_head + h) // sends
    wanted = (by_owner ^ offset) * rows + by_group * steps + by_step
    pick = (wanted[None, :] == row[:, None]).astype(BF16)
    activated = jnp.dot(pick, activated, preferred_element_type=F32).astype(BF16)
    mine = (wanted[None, :] == (r * rows + row[:rows])[:, None]).astype(BF16)
    kept = jnp.dot(mine, everything, preferred_element_type=F32)
    down = jnp.concatenate(
        [jnp.dot(activated, down_full[b], preferred_element_type=F32).astype(BF16) for b in range(n_head)],
        axis=1,
    )
    down = tied(down, *arrived)
    hidden = kept + jnp.sum(to_all(down.reshape(n, rows, D), "req").astype(F32), axis=0)
    mean_square = jnp.mean(hidden * hidden, axis=1, keepdims=True)

    slots = jnp.arange(requests, dtype=jnp.int32)
    source = state_perm // requests
    rank = jnp.sum(
        ((source[None, :] == source[:, None]) & (slots[None, :] < slots[:, None])).astype(jnp.int32),
        axis=1,
    )
    place = (source ^ r) * sends + rank
    natural = source * sends + rank
    slot_of = jnp.sum(jnp.where(natural[None, :] == slots[:, None], slots[None, :], 0), axis=1)
    mine = jnp.sum(
        jnp.where(
            place[None, :] == (jnp.arange(group, dtype=jnp.int32) * n_head + h)[:, None],
            slots[None, :],
            0,
        ),
        axis=1,
    )
    tenant = jnp.sum(
        ((mine + r * requests)[:, None] >= tenant_bounds[None, 1:-1]).astype(jnp.int32), axis=1
    )
    tenant_rows = sum(
        jnp.where((tenant == t)[:, None], gains[1 + t][None, :], 0.0)
        for t in range(tenant_gain.shape[0])
    )
    token_gain = jnp.repeat(tenant_rows * gains[0][None, :], steps, axis=0)
    final = (hidden * lax.rsqrt(mean_square + epsilon) * token_gain).astype(BF16)

    final = jnp.stack([final, swap(final, "head", n_head, 2)])
    quarter = D // 4
    full = jnp.concatenate(
        [
            lax.all_gather(final[:, :, at : at + quarter], "req", axis=0)
            for at in range(0, D, quarter)
        ],
        axis=-1,
    ).reshape(n * 2 * rows, D)
    if sends >= 4:
        arrived += [to_all(tied(pieces[3], full), "req")]
    best = jnp.maximum(
        jnp.max(jnp.dot(full, vocab_weight, preferred_element_type=F32), axis=1),
        jnp.max(jnp.dot(full, vocab_other, preferred_element_type=F32), axis=1),
    ).reshape(n, 2 * rows)
    got = jnp.max(to_all(best, "req"), axis=0)
    got = lax.all_gather(got, "head", axis=0).reshape(n_head, 2, rows)
    crossed = jnp.stack([got[i ^ 2, 1] for i in range(n_head)])
    best = jnp.maximum(got[:, 0], crossed).reshape(requests, steps)
    index = (place % n_head) * group + place // n_head
    match = (index[:, None] == slots[None, :])[:, :, None]
    best = jnp.sum(jnp.where(match, best[None], 0.0), axis=1)
    live = jnp.arange(steps)[None, :] < token_count[:, None]
    greatest = jnp.max(jnp.where(live, best, -1e30), axis=1)

    blocks = hidden.reshape(rows, n_head, width).transpose(1, 0, 2)
    tail = jnp.broadcast_to(mean_square[None], (n_head, rows, 128))
    whole = to_all(jnp.concatenate([blocks, tail], axis=2), "head")
    whole = whole.reshape(requests, steps, width + 128)
    whole = jnp.take(whole, (place % n_head) * group + place // n_head, axis=0, mode="clip")
    last = jnp.arange(steps)[None, :] == (token_count - 1)[:, None]
    last_norm = jnp.sqrt(jnp.sum(jnp.where(last, whole[:, :, width], 0.0), axis=1) + epsilon)

    new_states = update_states(
        slot_of, arrived_kv.reshape(requests, 2 * steps, width).astype(F32), arrived, steps
    )
    return whole[:, :, :width], new_states, last_norm, greatest


def solution(mesh):
    placed = (
        P("req", None),
        P("req"),
        P("req"),
        P(),
        P("req", "head", None, None),
        P("req", "head"),
        P(),
        P(None, "head"),
        P(None, "head"),
        P(None, "head"),
        P("head"),
        P("head"),
        P("head", None),
        P(),
        P("head", "req"),
        P("head", "req"),
        P("req", "head"),
        P("head"),
        P(None, "head"),
        P(None, ("req", "head")),
    )
    return jax.shard_map(
        on_device,
        mesh=mesh,
        in_specs=placed,
        out_specs=(P("req", None, "head"), P("req", "head", None, None), P("req"), P("req")),
        check_vma=False,
    )
```

```python
import functools

import jax
import jax.numpy as jnp
import numpy as np
from jax import lax
from jax.experimental import pallas as pl
from jax.experimental.pallas import tpu as pltpu
from jax.sharding import PartitionSpec as P

D = 2048
HEAD_DIM = 128
epsilon = 1e-06
F32 = jnp.float32
BF16 = jnp.bfloat16
VMEM = pltpu.VMEM
SMEM = pltpu.SMEM


def swap(x, axis, size, offset):
    return lax.ppermute(x, axis, [(i, i ^ offset) for i in range(size)])


def bf16_parts(x):
    high = lax.reduce_precision(x, 8, 7)
    return high.astype(BF16), (x - high).astype(BF16)


def sort_kernel(sends, order_ref, old_ref, *rest):
    outs, held, in_sems, out_sems = rest[:sends], rest[sends], rest[sends + 1], rest[sends + 2]
    owners = held.shape[1]

    def load(rank, owner):
        at = owner * sends + rank
        return pltpu.make_async_copy(
            old_ref.at[order_ref[at]], held.at[rank, owner], in_sems.at[rank, owner]
        )

    def store(rank):
        return pltpu.make_async_copy(held.at[rank], outs[rank], out_sems.at[rank])

    for rank in range(sends):
        for owner in range(owners):
            load(rank, owner).start()
    for rank in range(sends):
        for owner in range(owners):
            load(rank, owner).wait()
        store(rank).start()
    for rank in range(sends):
        store(rank).wait()


def sort_states(order, old_states, owners):
    requests = old_states.shape[0]
    sends = requests // owners
    piece = (owners,) + old_states.shape[1:]
    return pl.pallas_call(
        functools.partial(sort_kernel, sends),
        out_shape=[jax.ShapeDtypeStruct(piece, old_states.dtype)] * sends,
        in_specs=[pl.BlockSpec(memory_space=SMEM), pl.BlockSpec(memory_space=pl.ANY)],
        out_specs=[pl.BlockSpec(memory_space=pl.ANY)] * sends,
        scratch_shapes=[
            VMEM((sends,) + piece, old_states.dtype),
            pltpu.SemaphoreType.DMA((sends, owners)),
            pltpu.SemaphoreType.DMA((sends,)),
        ],
        compiler_params=pltpu.CompilerParams(vmem_limit_bytes=56 << 20),
    )(order, old_states)


def roll(x, by):
    return pltpu.roll(x, by % x.shape[0], 0)


def mixer_kernel(
    sends, owners, heads, classes, steps,
    me_ref, emb_ref, live_ref, gain_ref, floor_ref, ggain_ref, qw_hbm, fw_hbm, iw_hbm, ow_hbm,
    *rest,
):
    states_hbm = rest[:sends]
    own_ref, kv_ref = rest[sends : sends + 2]
    parts = rest[sends + 2 : sends + 2 + classes]
    (qw_ref, fw_ref, iw_ref, ow_ref, states, qhi_ref, qlo_ref, mixed_ref, part_ref, sems) = rest[
        sends + 2 + classes :
    ]
    weight_pairs = ((qw_hbm, qw_ref), (fw_hbm, fw_ref), (iw_hbm, iw_ref), (ow_hbm, ow_ref))
    loads = [
        pltpu.make_async_copy(there, here, sems.at[i]) for i, (there, here) in enumerate(weight_pairs)
    ]
    state_loads = [
        pltpu.make_async_copy(states_hbm[i], states.at[i], sems.at[4 + i]) for i in range(sends)
    ]
    for load in loads[:3] + state_loads + loads[3:]:
        load.start()
    tokens = live_ref.shape[0]
    requests = tokens // steps
    group = requests // classes
    rows = group * steps
    stream = emb_ref[0:tokens, :].astype(F32)
    scale = lax.rsqrt(jnp.mean(stream * stream, axis=1, keepdims=True) + epsilon)
    normed = (stream * scale * gain_ref[...]).astype(BF16)
    loads[0].wait()
    query = jnp.dot(normed, qw_ref[...], preferred_element_type=F32)
    query = query * jax.nn.sigmoid(query) * HEAD_DIM ** (-0.5)
    loads[1].wait()
    forget_raw = jnp.dot(normed, fw_ref[...], preferred_element_type=F32)
    loads[2].wait()
    value = jnp.dot(normed, iw_ref[...], preferred_element_type=F32)
    floor = floor_ref[...]
    forget = jnp.where(
        live_ref[...] > 0.0, floor + (1.0 - floor) * jax.nn.sigmoid(forget_raw), 1.0
    )
    key = 1.0 - forget
    step = lax.broadcasted_iota(jnp.int32, forget.shape, 0) % steps
    upto = forget * jnp.where(step >= 1, roll(forget, 1), 1.0)
    upto = upto * jnp.where(step >= 2, roll(upto, 2), 1.0)
    after = jnp.where(step <= steps - 2, roll(forget, -1), 1.0)
    after = after * jnp.where(step <= steps - 3, roll(forget, -2), 1.0)
    after = after * jnp.where(step <= steps - 4, roll(forget, -3), 1.0)
    carried = query * upto
    high = carried.astype(BF16).astype(F32)
    qhi_ref[...] = high
    qlo_ref[...] = carried - high
    lag_key, lag_value = key, value
    local = [jnp.zeros((tokens, HEAD_DIM), F32) for _ in range(heads)]
    for lag in range(steps):
        if lag:
            lag_key = roll(lag_key, 1) * forget
            lag_value = roll(lag_value, 1)
        product = jnp.where(step >= lag, query * lag_key, 0.0)
        for head in range(heads):
            cols = slice(head * HEAD_DIM, (head + 1) * HEAD_DIM)
            weight = jnp.sum(product[:, cols], axis=1, keepdims=True)
            local[head] = local[head] + weight * lag_value[:, cols]
    for head in range(heads):
        mixed_ref[:, head * HEAD_DIM : (head + 1) * HEAD_DIM] = local[head]
    for load in state_loads:
        load.wait()
    here = me_ref[0]
    upper = lax.broadcasted_iota(jnp.int32, (8, HEAD_DIM), 0) < steps
    for tile in range(tokens // 8):
        for head in range(heads):
            cols = slice(head * HEAD_DIM, (head + 1) * HEAD_DIM)
            at = slice(tile * 8, tile * 8 + 8)
            left = jnp.concatenate([qhi_ref[at, cols], qlo_ref[at, cols]], axis=0).astype(BF16)
            got = []
            for request in (2 * tile, 2 * tile + 1):
                place = (request % group) * classes + request // group
                old = states[place % sends, here ^ (place // sends), head]
                product = jnp.dot(left, old, preferred_element_type=F32)
                got.append(product[0:8] + product[8:16])
            mixed_ref[at, cols] += jnp.where(upper, got[0], got[1])
    mixed = mixed_ref[...]
    square = jnp.sum(mixed * mixed, axis=1, keepdims=True)
    loads[3].wait()
    part_ref[:, 0:D] = jnp.dot(
        (mixed * ggain_ref[...]).astype(BF16), ow_ref[...], preferred_element_type=F32
    )
    square_high = square.astype(BF16).astype(F32)
    lane = lax.broadcasted_iota(jnp.int32, (tokens, 128), 1)
    part_ref[:, D : D + 128] = jnp.where(lane < 64, square_high, square - square_high)
    for e in range(classes):
        first = pl.multiple_of((me_ref[1] ^ e) * rows, rows)
        parts[e][...] = part_ref[pl.ds(first, rows), :].astype(BF16)
    own_ref[...] = emb_ref[pl.ds(pl.multiple_of(me_ref[1] * rows, rows), rows), :]
    both = jnp.concatenate([(key * after).astype(BF16), value.astype(BF16)], axis=0)
    shape = (2 * tokens, 2 * tokens)
    target = lax.broadcasted_iota(jnp.int32, shape, 0)
    source = lax.broadcasted_iota(jnp.int32, shape, 1)
    slot, within = target // (2 * steps), target % (2 * steps)
    place = ((slot // sends) ^ here) * sends + slot % sends
    request = (place % classes) * group + place // classes
    wanted = request * steps + within % steps + jnp.where(within >= steps, tokens, 0)
    pick = jnp.where(source == wanted, 1.0, 0.0).astype(BF16)
    kv_ref[...] = jnp.dot(pick, both, preferred_element_type=F32).astype(BF16)


def mixer(me, emb, live, gain, floor, ggain, weights, states, steps, classes):
    tokens = live.shape[0]
    sends, (owners, heads) = len(states), states[0].shape[:2]
    width = floor.shape[1]
    rows = tokens // classes
    vmem, anywhere = pl.BlockSpec(memory_space=VMEM), pl.BlockSpec(memory_space=pl.ANY)
    return pl.pallas_call(
        functools.partial(mixer_kernel, sends, owners, heads, classes, steps),
        out_shape=[
            jax.ShapeDtypeStruct((rows, D), BF16),
            jax.ShapeDtypeStruct((2 * tokens, width), BF16),
        ]
        + [jax.ShapeDtypeStruct((rows, D + 128), BF16)] * classes,
        in_specs=[pl.BlockSpec(memory_space=SMEM)] + [vmem] * 5 + [anywhere] * (4 + sends),
        out_specs=[vmem] * (2 + classes),
        scratch_shapes=[VMEM(w.shape, BF16) for w in weights]
        + [
            VMEM((sends,) + states[0].shape, BF16),
            VMEM((tokens, width), F32),
            VMEM((tokens, width), F32),
            VMEM((tokens, width), F32),
            VMEM((tokens, D + 128), F32),
            pltpu.SemaphoreType.DMA((4 + sends,)),
        ],
        compiler_params=pltpu.CompilerParams(vmem_limit_bytes=56 << 20),
    )(me, emb, live, gain, floor, ggain, *weights, *states)


def update_kernel(sends, owners, heads, steps, slot_ref, kv_ref, *rest):
    states, out_ref = rest[:sends], rest[sends]
    diagonal = lax.broadcasted_iota(jnp.int32, (HEAD_DIM, HEAD_DIM), 0) == lax.broadcasted_iota(
        jnp.int32, (HEAD_DIM, HEAD_DIM), 1
    )
    first = lax.broadcasted_iota(jnp.int32, (2 * steps, HEAD_DIM), 0) < steps
    for k in range(owners):
        for rank in range(sends):
            place = k * sends + rank
            slot = slot_ref[place]
            for head in range(heads):
                cols = slice(head * HEAD_DIM, (head + 1) * HEAD_DIM)
                both = kv_ref[place, :, cols]
                key = jnp.where(first, both, 0.0)
                value = jnp.where(first, roll(both, steps), 0.0)
                kept = 1.0 - jnp.sum(key, axis=0, keepdims=True)
                keep = jnp.where(diagonal, kept, 0.0).astype(BF16)
                fresh = lax.dot_general(
                    key, value, (((0,), (0,)), ((), ())), preferred_element_type=F32
                )
                old = jnp.dot(keep, states[rank][k, head], preferred_element_type=F32)
                out_ref[slot, head] = (old + fresh).astype(BF16)


def update_states(slots, kv, states, steps):
    sends, (owners, heads) = len(states), states[0].shape[:2]
    vmem = pl.BlockSpec(memory_space=VMEM)
    return pl.pallas_call(
        functools.partial(update_kernel, sends, owners, heads, steps),
        out_shape=jax.ShapeDtypeStruct((owners * sends,) + states[0].shape[1:], BF16),
        in_specs=[pl.BlockSpec(memory_space=SMEM)] + [vmem] * (1 + sends),
        out_specs=vmem,
        compiler_params=pltpu.CompilerParams(vmem_limit_bytes=56 << 20),
    )(slots, kv, *states)


def to_all(x, axis):
    return lax.all_to_all(x, axis, split_axis=0, concat_axis=0, tiled=True)


def tied(x, *others):
    return lax.optimization_barrier((x,) + others)[0]


def on_device(
    token_ids, state_perm, token_count, tenant_bounds, old_states, embedding, mixer_gain,
    query_weight, forget_weight, input_weight, forget_floor, group_gain, output_weight, feed_gain,
    gate_weight, up_weight, down_weight, final_gain, tenant_gain, vocab_weight,
):
    requests, steps = token_ids.shape
    n = lax.axis_size("req")
    n_head = lax.axis_size("head")
    r = lax.axis_index("req")
    h = lax.axis_index("head")
    tokens = requests * steps
    everyone = requests * n
    sends = requests // n
    group = requests // n_head
    rows = group * steps
    width = D // n_head

    gate_full = lax.all_gather(gate_weight, "head", axis=0, tiled=True)
    up_full = lax.all_gather(up_weight, "head", axis=0, tiled=True)
    down_full = lax.all_gather(down_weight, "head", axis=0)

    packed = jnp.concatenate([token_ids.T, state_perm[None], token_count[None]], axis=0)
    packed = to_all(jnp.broadcast_to(packed[None], (n,) + packed.shape), "req").transpose(1, 0, 2).reshape(steps + 2, everyone)
    every = jnp.arange(everyone, dtype=jnp.int32)
    source = packed[steps] // requests
    rank = jnp.sum(
        ((source[None, :] == source[:, None]) & (every[None, :] < every[:, None])).astype(jnp.int32),
        axis=1,
    )
    place = ((every // requests) ^ source) * sends + rank % sends
    at = source * requests + (place % n_head) * group + place // n_head
    chosen = (at[:, None] == every[None, :]).astype(F32)
    ordered = jnp.dot(packed.astype(F32), chosen, precision=lax.Precision.HIGHEST)
    ordered = (ordered + 0.5).astype(jnp.int32)

    ids = ordered[:steps].T.reshape(n * tokens)
    table = embedding.shape[0]
    local_ids = ids - r * table
    inside = (local_ids >= 0) & (local_ids < table)
    picked = jnp.take(embedding, jnp.clip(local_ids, 0, table - 1), axis=0, mode="clip")
    picked = jnp.where(inside[:, None], picked, jnp.zeros((), BF16)).reshape(n, tokens, width)
    embed_part = jnp.sum(to_all(picked, "req").astype(F32), axis=0).astype(BF16)
    vocab_other = swap(tied(vocab_weight, embed_part), "head", n_head, 1)

    gains = jnp.concatenate([final_gain[None], tenant_gain], axis=0)
    gains_high, gains_low = bf16_parts(gains)
    extra = jnp.zeros((16 - 2 * gains.shape[0], width), BF16)
    embedded = lax.all_gather(
        jnp.concatenate([embed_part, gains_high, gains_low, extra], axis=0), "head", axis=1, tiled=True
    )
    gains = embedded[tokens : tokens + 5].astype(F32) + embedded[tokens + 5 : tokens + 10].astype(F32)

    ordered = lax.dynamic_slice_in_dim(ordered, r * requests, requests, 1)
    old_order = (ordered[steps] - r * requests).reshape(n_head, group).T.reshape(n, sends)
    old_order = jnp.take(old_order, jnp.arange(n) ^ r, axis=0).reshape(requests)
    pieces = sort_states(old_order, old_states, n)
    live = (jnp.arange(steps)[None, :] < ordered[steps + 1][:, None]).astype(F32)
    own, kv, *parts = mixer(
        jnp.stack([r, h]), embedded, live.reshape(tokens, 1), mixer_gain[None], forget_floor[None],
        group_gain[None], (query_weight, forget_weight, input_weight, output_weight), pieces,
        steps, n_head,
    )
    arrived = [to_all(tied(pieces[0], embed_part), "req")]

    total = parts[0].astype(F32)
    for e in range(1, n_head):
        total = total + swap(parts[e], "head", n_head, e).astype(F32)
    square = total[:, D : D + 1] + total[:, D + 127 : D + 128]
    after_mixer = own.astype(F32) + total[:, :D] * lax.rsqrt(square / D + epsilon)
    after_mixer = tied(after_mixer.astype(BF16), gate_full, up_full, down_full, *arrived)
    everything = lax.all_gather(after_mixer, "req", axis=0, tiled=True)
    arrived += [to_all(tied(piece, after_mixer), "req") for piece in pieces[1:2]]
    arrived_kv = to_all(tied(kv, *arrived).reshape(n, -1, width), "req")
    stream = everything.astype(F32)
    scale = lax.rsqrt(jnp.mean(stream * stream, axis=1, keepdims=True) + epsilon)
    feed_in = (stream * scale * feed_gain).astype(BF16)
    gate = jnp.dot(feed_in, gate_full, preferred_element_type=F32)
    up = jnp.dot(feed_in, up_full, preferred_element_type=F32)
    activated = (jax.nn.silu(gate) * up).astype(BF16)

    row = jnp.arange(n * rows, dtype=jnp.int32)
    by_owner, by_group, by_step = row // rows, (row % rows) // steps, row % steps
    if sends % n_head == 0:
        offset = by_group * n_head // sends
    else:
        offset = (by_group * n_head + h) // sends
    wanted = (by_owner ^ offset) * rows + by_group * steps + by_step
    pick = (wanted[None, :] == row[:, None]).astype(BF16)
    activated = jnp.dot(pick, activated, preferred_element_type=F32).astype(BF16)
    mine = (wanted[None, :] == (r * rows + row[:rows])[:, None]).astype(BF16)
    kept = jnp.dot(mine, everything, preferred_element_type=F32)
    down = jnp.concatenate(
        [jnp.dot(activated, down_full[b], preferred_element_type=F32).astype(BF16) for b in range(n_head)],
        axis=1,
    )
    down = tied(down, arrived_kv, *arrived)
    hidden = kept + jnp.sum(to_all(down.reshape(n, rows, D), "req").astype(F32), axis=0)
    mean_square = jnp.mean(hidden * hidden, axis=1, keepdims=True)

    slots = jnp.arange(requests, dtype=jnp.int32)
    source = state_perm // requests
    rank = jnp.sum(
        ((source[None, :] == source[:, None]) & (slots[None, :] < slots[:, None])).astype(jnp.int32),
        axis=1,
    )
    place = (source ^ r) * sends + rank
    natural = source * sends + rank
    slot_of = jnp.sum(jnp.where(natural[None, :] == slots[:, None], slots[None, :], 0), axis=1)
    mine = jnp.sum(
        jnp.where(
            place[None, :] == (jnp.arange(group, dtype=jnp.int32) * n_head + h)[:, None],
            slots[None, :],
            0,
        ),
        axis=1,
    )
    tenant = jnp.sum(
        ((mine + r * requests)[:, None] >= tenant_bounds[None, 1:-1]).astype(jnp.int32), axis=1
    )
    tenant_rows = sum(
        jnp.where((tenant == t)[:, None], gains[1 + t][None, :], 0.0)
        for t in range(tenant_gain.shape[0])
    )
    token_gain = jnp.repeat(tenant_rows * gains[0][None, :], steps, axis=0)
    final = (hidden * lax.rsqrt(mean_square + epsilon) * token_gain).astype(BF16)

    final = jnp.stack([final, swap(final, "head", n_head, 2)])
    for piece in pieces[2:]:
        arrived += [to_all(tied(piece, final, *arrived[2:]), "req")]
    full = lax.all_gather(final, "req", axis=0, tiled=True).reshape(n * 2 * rows, D)
    best = jnp.maximum(
        jnp.max(jnp.dot(full, vocab_weight, preferred_element_type=F32), axis=1),
        jnp.max(jnp.dot(full, vocab_other, preferred_element_type=F32), axis=1),
    ).reshape(n, 2 * rows)
    got = jnp.max(to_all(tied(best, *arrived), "req"), axis=0)
    got = lax.all_gather(got, "head", axis=0).reshape(n_head, 2, rows)
    crossed = jnp.stack([got[i ^ 2, 1] for i in range(n_head)])
    best = jnp.maximum(got[:, 0], crossed).reshape(requests, steps)
    index = (place % n_head) * group + place // n_head
    match = (index[:, None] == slots[None, :])[:, :, None]
    best = jnp.sum(jnp.where(match, best[None], 0.0), axis=1)
    live = jnp.arange(steps)[None, :] < token_count[:, None]
    greatest = jnp.max(jnp.where(live, best, -1e30), axis=1)

    blocks = hidden.reshape(rows, n_head, width).transpose(1, 0, 2)
    tail = jnp.broadcast_to(mean_square, (rows, 128))
    whole = []
    for e in range(n_head):
        block = lax.dynamic_index_in_dim(blocks, h ^ e, 0, keepdims=False)
        block = jnp.concatenate([block, tail], axis=1)
        whole.append(block if e == 0 else swap(block, "head", n_head, e))
    whole = jnp.stack(whole).reshape(requests, steps, width + 128)
    index = ((place % n_head) ^ h) * group + place // n_head
    whole = jnp.take(whole, index, axis=0, mode="clip")
    last = jnp.arange(steps)[None, :] == (token_count - 1)[:, None]
    last_norm = jnp.sqrt(jnp.sum(jnp.where(last, whole[:, :, width], 0.0), axis=1) + epsilon)

    new_states = update_states(
        slot_of, arrived_kv.reshape(requests, 2 * steps, width).astype(F32), arrived, steps
    )
    return whole[:, :, :width], new_states, last_norm, greatest


def solution(mesh):
    placed = (
        P("req", None),
        P("req"),
        P("req"),
        P(),
        P("req", "head", None, None),
        P("req", "head"),
        P(),
        P(None, "head"),
        P(None, "head"),
        P(None, "head"),
        P("head"),
        P("head"),
        P("head", None),
        P(),
        P("head", "req"),
        P("head", "req"),
        P("req", "head"),
        P("head"),
        P(None, "head"),
        P(None, ("req", "head")),
    )
    return jax.shard_map(
        on_device,
        mesh=mesh,
        in_specs=placed,
        out_specs=(P("req", None, "head"), P("req", "head", None, None), P("req"), P("req")),
        check_vma=False,
    )
```

```python
import functools

import jax
import jax.numpy as jnp
import numpy as np
from jax import lax
from jax.experimental import pallas as pl
from jax.experimental.pallas import tpu as pltpu
from jax.sharding import PartitionSpec as P

D = 2048
HEAD_DIM = 128
epsilon = 1e-06
F32 = jnp.float32
BF16 = jnp.bfloat16
VMEM = pltpu.VMEM
SMEM = pltpu.SMEM


def swap(x, axis, size, offset):
    return lax.ppermute(x, axis, [(i, i ^ offset) for i in range(size)])


def bf16_parts(x):
    high = lax.reduce_precision(x, 8, 7)
    return high.astype(BF16), (x - high).astype(BF16)


def sort_kernel(sends, order_ref, old_ref, *rest):
    outs, (held, in_sems, out_sems) = rest[:-3], rest[-3:]
    owners = held.shape[0]
    spans, first = [], 0
    for out in outs:
        spans.append((first, out.shape[1]))
        first += out.shape[1]

    def load(owner, rank):
        at = owner * sends + rank
        return pltpu.make_async_copy(
            old_ref.at[order_ref[at]], held.at[owner, rank], in_sems.at[owner, rank]
        )

    def store(part):
        first, count = spans[part]
        return pltpu.make_async_copy(
            held.at[:, pl.ds(first, count)], outs[part], out_sems.at[part]
        )

    for first, count in spans:
        for owner in range(owners):
            for rank in range(first, first + count):
                load(owner, rank).start()
    for part, (first, count) in enumerate(spans):
        for owner in range(owners):
            for rank in range(first, first + count):
                load(owner, rank).wait()
        store(part).start()
    for part in range(len(outs)):
        store(part).wait()


def sort_states(order, old_states, owners, counts):
    sends = sum(counts)
    state = old_states.shape[1:]
    return pl.pallas_call(
        functools.partial(sort_kernel, sends),
        out_shape=[
            jax.ShapeDtypeStruct((owners, count) + state, old_states.dtype) for count in counts
        ],
        in_specs=[pl.BlockSpec(memory_space=SMEM), pl.BlockSpec(memory_space=pl.ANY)],
        out_specs=[pl.BlockSpec(memory_space=pl.ANY)] * len(counts),
        scratch_shapes=[
            VMEM((owners, sends) + state, old_states.dtype),
            pltpu.SemaphoreType.DMA((owners, sends)),
            pltpu.SemaphoreType.DMA((len(counts),)),
        ],
        compiler_params=pltpu.CompilerParams(vmem_limit_bytes=56 << 20),
    )(order, old_states)


def hand_on(x_ref, token_ref, out_ref):
    pass


def after(x, *others):
    corners = [other.reshape((-1,) + other.shape[-2:])[0, :8, :128] for other in others]
    anywhere = pl.BlockSpec(memory_space=pl.ANY)
    return pl.pallas_call(
        hand_on,
        out_shape=jax.ShapeDtypeStruct(x.shape, x.dtype),
        in_specs=[anywhere, anywhere],
        out_specs=anywhere,
        input_output_aliases={0: 0},
    )(x, sum(corners[1:], corners[0]))


def roll(x, by):
    return pltpu.roll(x, by % x.shape[0], 0)


def mixer_kernel(
    counts, owners, heads, classes, steps,
    me_ref, emb_ref, live_ref, gain_ref, floor_ref, ggain_ref, qw_hbm, fw_hbm, iw_hbm, ow_hbm,
    *rest,
):
    pieces, sends = len(counts), sum(counts)
    states_hbm = rest[:pieces]
    own_ref, kv_ref = rest[pieces : pieces + 2]
    parts = rest[pieces + 2 : pieces + 2 + classes]
    (qw_ref, fw_ref, iw_ref, ow_ref, states, qhi_ref, qlo_ref, mixed_ref, part_ref, sems) = rest[
        pieces + 2 + classes :
    ]
    weight_pairs = ((qw_hbm, qw_ref), (fw_hbm, fw_ref), (iw_hbm, iw_ref), (ow_hbm, ow_ref))
    loads = [
        pltpu.make_async_copy(there, here, sems.at[i]) for i, (there, here) in enumerate(weight_pairs)
    ]
    state_loads = [
        pltpu.make_async_copy(
            states_hbm[i], states.at[:, pl.ds(sum(counts[:i]), counts[i])], sems.at[4 + i]
        )
        for i in range(pieces)
    ]
    for load in loads[:3] + state_loads + loads[3:]:
        load.start()
    tokens = live_ref.shape[0]
    requests = tokens // steps
    group = requests // classes
    rows = group * steps
    stream = emb_ref[0:tokens, :].astype(F32)
    scale = lax.rsqrt(jnp.mean(stream * stream, axis=1, keepdims=True) + epsilon)
    normed = (stream * scale * gain_ref[...]).astype(BF16)
    loads[0].wait()
    query = jnp.dot(normed, qw_ref[...], preferred_element_type=F32)
    query = query * jax.nn.sigmoid(query) * HEAD_DIM ** (-0.5)
    loads[1].wait()
    forget_raw = jnp.dot(normed, fw_ref[...], preferred_element_type=F32)
    loads[2].wait()
    value = jnp.dot(normed, iw_ref[...], preferred_element_type=F32)
    floor = floor_ref[...]
    forget = jnp.where(
        live_ref[...] > 0.0, floor + (1.0 - floor) * jax.nn.sigmoid(forget_raw), 1.0
    )
    key = 1.0 - forget
    step = lax.broadcasted_iota(jnp.int32, forget.shape, 0) % steps
    upto = forget * jnp.where(step >= 1, roll(forget, 1), 1.0)
    upto = upto * jnp.where(step >= 2, roll(upto, 2), 1.0)
    after = jnp.where(step <= steps - 2, roll(forget, -1), 1.0)
    after = after * jnp.where(step <= steps - 3, roll(forget, -2), 1.0)
    after = after * jnp.where(step <= steps - 4, roll(forget, -3), 1.0)
    carried = query * upto
    high = carried.astype(BF16).astype(F32)
    qhi_ref[...] = high
    qlo_ref[...] = carried - high
    lag_key, lag_value = key, value
    local = [jnp.zeros((tokens, HEAD_DIM), F32) for _ in range(heads)]
    for lag in range(steps):
        if lag:
            lag_key = roll(lag_key, 1) * forget
            lag_value = roll(lag_value, 1)
        product = jnp.where(step >= lag, query * lag_key, 0.0)
        for head in range(heads):
            cols = slice(head * HEAD_DIM, (head + 1) * HEAD_DIM)
            weight = jnp.sum(product[:, cols], axis=1, keepdims=True)
            local[head] = local[head] + weight * lag_value[:, cols]
    for head in range(heads):
        mixed_ref[:, head * HEAD_DIM : (head + 1) * HEAD_DIM] = local[head]
    for load in state_loads:
        load.wait()
    here = me_ref[0]
    upper = lax.broadcasted_iota(jnp.int32, (8, HEAD_DIM), 0) < steps
    for tile in range(tokens // 8):
        for head in range(heads):
            cols = slice(head * HEAD_DIM, (head + 1) * HEAD_DIM)
            at = slice(tile * 8, tile * 8 + 8)
            left = jnp.concatenate([qhi_ref[at, cols], qlo_ref[at, cols]], axis=0).astype(BF16)
            got = []
            for request in (2 * tile, 2 * tile + 1):
                place = (request % group) * classes + request // group
                old = states[here ^ (place // sends), place % sends, head]
                product = jnp.dot(left, old, preferred_element_type=F32)
                got.append(product[0:8] + product[8:16])
            mixed_ref[at, cols] += jnp.where(upper, got[0], got[1])
    mixed = mixed_ref[...]
    square = jnp.sum(mixed * mixed, axis=1, keepdims=True)
    loads[3].wait()
    part_ref[:, 0:D] = jnp.dot(
        (mixed * ggain_ref[...]).astype(BF16), ow_ref[...], preferred_element_type=F32
    )
    square_high = square.astype(BF16).astype(F32)
    lane = lax.broadcasted_iota(jnp.int32, (tokens, 128), 1)
    part_ref[:, D : D + 128] = jnp.where(lane < 64, square_high, square - square_high)
    for e in range(classes):
        first = pl.multiple_of((me_ref[1] ^ e) * rows, rows)
        parts[e][...] = part_ref[pl.ds(first, rows), :].astype(BF16)
    own_ref[...] = emb_ref[pl.ds(pl.multiple_of(me_ref[1] * rows, rows), rows), :]
    both = jnp.concatenate([(key * after).astype(BF16), value.astype(BF16)], axis=0)
    shape = (2 * tokens, 2 * tokens)
    target = lax.broadcasted_iota(jnp.int32, shape, 0)
    source = lax.broadcasted_iota(jnp.int32, shape, 1)
    slot, within = target // (2 * steps), target % (2 * steps)
    place = ((slot // sends) ^ here) * sends + slot % sends
    request = (place % classes) * group + place // classes
    wanted = request * steps + within % steps + jnp.where(within >= steps, tokens, 0)
    pick = jnp.where(source == wanted, 1.0, 0.0).astype(BF16)
    kv_ref[...] = jnp.dot(pick, both, preferred_element_type=F32).astype(BF16)


def mixer(me, emb, live, gain, floor, ggain, weights, states, steps, classes):
    tokens = live.shape[0]
    counts = tuple(piece.shape[1] for piece in states)
    owners, _, heads = states[0].shape[:3]
    width = floor.shape[1]
    rows = tokens // classes
    vmem, anywhere = pl.BlockSpec(memory_space=VMEM), pl.BlockSpec(memory_space=pl.ANY)
    return pl.pallas_call(
        functools.partial(mixer_kernel, counts, owners, heads, classes, steps),
        out_shape=[
            jax.ShapeDtypeStruct((rows, D), BF16),
            jax.ShapeDtypeStruct((2 * tokens, width), BF16),
        ]
        + [jax.ShapeDtypeStruct((rows, D + 128), BF16)] * classes,
        in_specs=[pl.BlockSpec(memory_space=SMEM)] + [vmem] * 5 + [anywhere] * (4 + len(states)),
        out_specs=[vmem] * (2 + classes),
        scratch_shapes=[VMEM(w.shape, BF16) for w in weights]
        + [
            VMEM((owners, sum(counts)) + states[0].shape[2:], BF16),
            VMEM((tokens, width), F32),
            VMEM((tokens, width), F32),
            VMEM((tokens, width), F32),
            VMEM((tokens, D + 128), F32),
            pltpu.SemaphoreType.DMA((4 + len(states),)),
        ],
        compiler_params=pltpu.CompilerParams(vmem_limit_bytes=56 << 20),
    )(me, emb, live, gain, floor, ggain, *weights, *states)


def update_kernel(steps, slot_ref, kv_ref, *rest):
    states, out_ref = rest[:-1], rest[-1]
    owners, _, heads = states[0].shape[:3]
    ranks = [(piece, i) for piece in states for i in range(piece.shape[1])]
    sends = len(ranks)
    diagonal = lax.broadcasted_iota(jnp.int32, (HEAD_DIM, HEAD_DIM), 0) == lax.broadcasted_iota(
        jnp.int32, (HEAD_DIM, HEAD_DIM), 1
    )
    first = lax.broadcasted_iota(jnp.int32, (2 * steps, HEAD_DIM), 0) < steps
    for k in range(owners):
        for rank, (piece, i) in enumerate(ranks):
            place = k * sends + rank
            slot = slot_ref[place]
            for head in range(heads):
                cols = slice(head * HEAD_DIM, (head + 1) * HEAD_DIM)
                both = kv_ref[place, :, cols]
                key = jnp.where(first, both, 0.0)
                value = jnp.where(first, roll(both, steps), 0.0)
                kept = 1.0 - jnp.sum(key, axis=0, keepdims=True)
                keep = jnp.where(diagonal, kept, 0.0).astype(BF16)
                fresh = lax.dot_general(
                    key, value, (((0,), (0,)), ((), ())), preferred_element_type=F32
                )
                old = jnp.dot(keep, piece[k, i, head], preferred_element_type=F32)
                out_ref[slot, head] = (old + fresh).astype(BF16)


def update_states(slots, kv, states, steps):
    vmem = pl.BlockSpec(memory_space=VMEM)
    return pl.pallas_call(
        functools.partial(update_kernel, steps),
        out_shape=jax.ShapeDtypeStruct((slots.shape[0],) + states[0].shape[2:], BF16),
        in_specs=[pl.BlockSpec(memory_space=SMEM)] + [vmem] * (1 + len(states)),
        out_specs=vmem,
        compiler_params=pltpu.CompilerParams(vmem_limit_bytes=56 << 20),
    )(slots, kv, *states)


def dot_rows(a, b):
    return lax.dot_general(a, b, (((1,), (1,)), ((), ())), preferred_element_type=F32)


def to_all(x, axis):
    return lax.all_to_all(x, axis, split_axis=0, concat_axis=0, tiled=True)


def on_device(
    token_ids, state_perm, token_count, tenant_bounds, old_states, embedding, mixer_gain,
    query_weight, forget_weight, input_weight, forget_floor, group_gain, output_weight, feed_gain,
    gate_weight, up_weight, down_weight, final_gain, tenant_gain, vocab_weight,
):
    requests, steps = token_ids.shape
    n = lax.axis_size("req")
    n_head = lax.axis_size("head")
    r = lax.axis_index("req")
    h = lax.axis_index("head")
    tokens = requests * steps
    everyone = requests * n
    sends = requests // n
    group = requests // n_head
    rows = group * steps
    width = D // n_head

    gate_full = lax.all_gather(gate_weight.T, "head", axis=1, tiled=True)
    up_full = lax.all_gather(up_weight.T, "head", axis=1, tiled=True)
    down_full = lax.all_gather(down_weight, "head", axis=0)

    packed = jnp.concatenate([token_ids.T, state_perm[None], token_count[None]], axis=0)
    packed = to_all(jnp.broadcast_to(packed[None], (n,) + packed.shape), "req").transpose(1, 0, 2).reshape(steps + 2, everyone)
    every = jnp.arange(everyone, dtype=jnp.int32)
    source = packed[steps] // requests
    rank = jnp.sum(
        ((source[None, :] == source[:, None]) & (every[None, :] < every[:, None])).astype(jnp.int32),
        axis=1,
    )
    place = ((every // requests) ^ source) * sends + rank % sends
    at = source * requests + (place % n_head) * group + place // n_head
    chosen = (at[:, None] == every[None, :]).astype(F32)
    ordered = jnp.dot(packed.astype(F32), chosen, precision=lax.Precision.HIGHEST)
    ordered = (ordered + 0.5).astype(jnp.int32)

    ids = ordered[:steps].T.reshape(n, tokens)
    table = embedding.shape[0]
    room = tokens // 2
    holder = lax.div(ids, jnp.int32(table))
    held = holder == r
    earlier = jnp.triu(jnp.ones((tokens, tokens), BF16), 1)
    turn = jnp.dot(held.astype(BF16), earlier, preferred_element_type=F32).astype(jnp.int32)
    local_ids = jnp.where(held, ids - r * table, 0)
    seat = held[:, None] & (turn[:, None] == jnp.arange(room, dtype=jnp.int32)[None, :, None])
    wanted = jnp.sum(jnp.where(seat, local_ids[:, None], 0), axis=2).reshape(n * room)
    got = to_all(jnp.take(embedding, wanted, axis=0, mode="clip").reshape(n, room, width), "req")
    own_holder = lax.dynamic_index_in_dim(holder, r, 0, keepdims=False)
    order = jnp.arange(tokens, dtype=jnp.int32)
    own_turn = jnp.sum(
        ((own_holder[None, :] == own_holder[:, None]) & (order[None, :] < order[:, None])).astype(
            jnp.int32
        ),
        axis=1,
    )
    seat = jnp.where(own_turn < room, own_holder * room + own_turn, -1)
    pick = (seat[:, None] == jnp.arange(n * room, dtype=jnp.int32)[None, :]).astype(BF16)
    embed_part = jnp.dot(
        pick, got.reshape(n * room, width), preferred_element_type=F32
    ).astype(BF16)
    owners = jnp.arange(n, dtype=jnp.int32)
    load = jnp.sum((holder[:, None] == owners[None, :, None]).astype(jnp.int32), axis=2)

    def with_rest(part):
        rows = jnp.take(embedding, local_ids.reshape(n * tokens), axis=0, mode="clip")
        rest = (held & (turn >= room)).reshape(n * tokens, 1)
        rows = jnp.where(rest, rows, jnp.zeros((), BF16)).reshape(n, tokens, width)
        return (part.astype(F32) + jnp.sum(to_all(rows, "req").astype(F32), axis=0)).astype(BF16)

    embed_part = lax.cond(jnp.max(load) > room, with_rest, lambda part: part, embed_part)
    vocab_other = swap(vocab_weight.T, "head", n_head, 1)

    gains = jnp.concatenate([final_gain[None], tenant_gain], axis=0)
    gains_high, gains_low = bf16_parts(gains)
    extra = jnp.zeros((16 - 2 * gains.shape[0], width), BF16)
    embedded = lax.all_gather(
        jnp.concatenate([embed_part, gains_high, gains_low, extra], axis=0), "head", axis=1, tiled=True
    )
    gains = embedded[tokens : tokens + 5].astype(F32) + embedded[tokens + 5 : tokens + 10].astype(F32)

    ordered = lax.dynamic_slice_in_dim(ordered, r * requests, requests, 1)
    old_order = (ordered[steps] - r * requests).reshape(n_head, group).T.reshape(n, sends)
    old_order = jnp.take(old_order, jnp.arange(n) ^ r, axis=0).reshape(requests)
    counts = (1, 2, 1) if sends == 4 else (sends,)
    pieces = sort_states(old_order, old_states, n, counts)
    live = (jnp.arange(steps)[None, :] < ordered[steps + 1][:, None]).astype(F32)
    own, kv, *parts = mixer(
        jnp.stack([r, h]), embedded, live.reshape(tokens, 1), mixer_gain[None], forget_floor[None],
        group_gain[None], (query_weight, forget_weight, input_weight, output_weight), pieces,
        steps, n_head,
    )
    arrived = [to_all(pieces[0], "req")]

    total = parts[0].astype(F32)
    for e in range(1, n_head):
        total = total + swap(parts[e], "head", n_head, e).astype(F32)
    square = total[:, D : D + 1] + total[:, D + 127 : D + 128]
    after_mixer = own.astype(F32) + total[:, :D] * lax.rsqrt(square / D + epsilon)
    after_mixer = after(after_mixer.astype(BF16), gate_full, up_full, down_full)
    everything = lax.all_gather(after_mixer, "req", axis=0, tiled=True)
    arrived += [to_all(piece, "req") for piece in pieces[1:2]]
    stream = everything.astype(F32)
    scale = lax.rsqrt(jnp.mean(stream * stream, axis=1, keepdims=True) + epsilon)
    feed_in = (stream * scale * feed_gain).astype(BF16)
    gate = dot_rows(feed_in, gate_full)
    up = dot_rows(feed_in, up_full)
    activated = (jax.nn.silu(gate) * up).astype(BF16)

    row = jnp.arange(n * rows, dtype=jnp.int32)
    by_owner, by_group, by_step = row // rows, (row % rows) // steps, row % steps
    if sends % n_head == 0:
        offset = by_group * n_head // sends
    else:
        offset = (by_group * n_head + h) // sends
    wanted = (by_owner ^ offset) * rows + by_group * steps + by_step
    pick = (wanted[None, :] == row[:, None]).astype(BF16)
    activated = jnp.dot(pick, activated, preferred_element_type=F32).astype(BF16)
    mine = (wanted[None, :] == (r * rows + row[:rows])[:, None]).astype(BF16)
    kept = jnp.dot(mine, everything, preferred_element_type=F32)
    down = jnp.concatenate(
        [jnp.dot(activated, down_full[b], preferred_element_type=F32).astype(BF16) for b in range(n_head)],
        axis=1,
    )
    down = after(down, *arrived)
    hidden = kept + jnp.sum(to_all(down.reshape(n, rows, D), "req").astype(F32), axis=0)
    mean_square = jnp.mean(hidden * hidden, axis=1, keepdims=True)

    slots = jnp.arange(requests, dtype=jnp.int32)
    source = state_perm // requests
    rank = jnp.sum(
        ((source[None, :] == source[:, None]) & (slots[None, :] < slots[:, None])).astype(jnp.int32),
        axis=1,
    )
    place = (source ^ r) * sends + rank
    natural = source * sends + rank
    slot_of = jnp.sum(jnp.where(natural[None, :] == slots[:, None], slots[None, :], 0), axis=1)
    mine = jnp.sum(
        jnp.where(
            place[None, :] == (jnp.arange(group, dtype=jnp.int32) * n_head + h)[:, None],
            slots[None, :],
            0,
        ),
        axis=1,
    )
    tenant = jnp.sum(
        ((mine + r * requests)[:, None] >= tenant_bounds[None, 1:-1]).astype(jnp.int32), axis=1
    )
    tenant_rows = sum(
        jnp.where((tenant == t)[:, None], gains[1 + t][None, :], 0.0)
        for t in range(tenant_gain.shape[0])
    )
    token_gain = jnp.repeat(tenant_rows * gains[0][None, :], steps, axis=0)
    final = (hidden * lax.rsqrt(mean_square + epsilon) * token_gain).astype(BF16)

    final = jnp.stack([final, swap(final, "head", n_head, 2)])
    arrived += [to_all(after(piece, final), "req") for piece in pieces[2:]]
    arrived_kv = to_all(after(kv, final).reshape(n, -1, width), "req")
    full = lax.all_gather(final, "req", axis=0, tiled=True).reshape(n * 2 * rows, D)
    best = jnp.maximum(
        jnp.max(dot_rows(full, vocab_weight.T), axis=1),
        jnp.max(dot_rows(full, vocab_other), axis=1),
    ).reshape(n, 2 * rows)
    got = jnp.max(to_all(best, "req"), axis=0)
    got = lax.all_gather(got, "head", axis=0).reshape(n_head, 2, rows)
    crossed = jnp.stack([got[i ^ 2, 1] for i in range(n_head)])
    best = jnp.maximum(got[:, 0], crossed).reshape(requests, steps)
    index = (place % n_head) * group + place // n_head
    match = (index[:, None] == slots[None, :])[:, :, None]
    best = jnp.sum(jnp.where(match, best[None], 0.0), axis=1)
    live = jnp.arange(steps)[None, :] < token_count[:, None]
    greatest = jnp.max(jnp.where(live, best, -1e30), axis=1)

    blocks = hidden.reshape(rows, n_head, width).transpose(1, 0, 2)
    tail = jnp.broadcast_to(mean_square, (rows, 128))
    whole = []
    for e in range(n_head):
        block = lax.dynamic_index_in_dim(blocks, h ^ e, 0, keepdims=False)
        block = jnp.concatenate([block, tail], axis=1)
        whole.append(block if e == 0 else swap(block, "head", n_head, e))
    whole = jnp.stack(whole).reshape(requests, steps, width + 128)
    index = ((place % n_head) ^ h) * group + place // n_head
    whole = jnp.take(whole, index, axis=0, mode="clip")
    last = jnp.arange(steps)[None, :] == (token_count - 1)[:, None]
    last_norm = jnp.sqrt(jnp.sum(jnp.where(last, whole[:, :, width], 0.0), axis=1) + epsilon)

    new_states = update_states(
        slot_of, arrived_kv.reshape(requests, 2 * steps, width).astype(F32), arrived, steps
    )
    return whole[:, :, :width], new_states, last_norm, greatest


def solution(mesh):
    placed = (
        P("req", None),
        P("req"),
        P("req"),
        P(),
        P("req", "head", None, None),
        P("req", "head"),
        P(),
        P(None, "head"),
        P(None, "head"),
        P(None, "head"),
        P("head"),
        P("head"),
        P("head", None),
        P(),
        P("head", "req"),
        P("head", "req"),
        P("req", "head"),
        P("head"),
        P(None, "head"),
        P(None, ("req", "head")),
    )
    return jax.shard_map(
        on_device,
        mesh=mesh,
        in_specs=placed,
        out_specs=(P("req", None, "head"), P("req", "head", None, None), P("req"), P("req")),
        check_vma=False,
    )
```

```python
import functools

import jax
import jax.numpy as jnp
import numpy as np
from jax import lax
from jax.experimental import pallas as pl
from jax.experimental.pallas import tpu as pltpu
from jax.sharding import PartitionSpec as P

D = 2048
HEAD_DIM = 128
epsilon = 1e-06
F32 = jnp.float32
BF16 = jnp.bfloat16
VMEM = pltpu.VMEM
SMEM = pltpu.SMEM


def swap(x, axis, size, offset):
    return lax.ppermute(x, axis, [(i, i ^ offset) for i in range(size)])


def bf16_parts(x):
    high = lax.reduce_precision(x, 8, 7)
    return high.astype(BF16), (x - high).astype(BF16)


def sort_kernel(sends, order_ref, old_ref, *rest):
    outs, (held, in_sems, out_sems) = rest[:-3], rest[-3:]
    owners = held.shape[0]
    spans, first = [], 0
    for out in outs:
        spans.append((first, out.shape[1]))
        first += out.shape[1]

    def load(owner, rank):
        at = owner * sends + rank
        return pltpu.make_async_copy(
            old_ref.at[order_ref[at]], held.at[owner, rank], in_sems.at[owner, rank]
        )

    def store(part):
        first, count = spans[part]
        return pltpu.make_async_copy(
            held.at[:, pl.ds(first, count)], outs[part], out_sems.at[part]
        )

    for first, count in spans:
        for owner in range(owners):
            for rank in range(first, first + count):
                load(owner, rank).start()
    for part, (first, count) in enumerate(spans):
        for owner in range(owners):
            for rank in range(first, first + count):
                load(owner, rank).wait()
        store(part).start()
    for part in range(len(outs)):
        store(part).wait()


def sort_states(order, old_states, owners, counts):
    sends = sum(counts)
    state = old_states.shape[1:]
    return pl.pallas_call(
        functools.partial(sort_kernel, sends),
        out_shape=[
            jax.ShapeDtypeStruct((owners, count) + state, old_states.dtype) for count in counts
        ],
        in_specs=[pl.BlockSpec(memory_space=SMEM), pl.BlockSpec(memory_space=pl.ANY)],
        out_specs=[pl.BlockSpec(memory_space=pl.ANY)] * len(counts),
        scratch_shapes=[
            VMEM((owners, sends) + state, old_states.dtype),
            pltpu.SemaphoreType.DMA((owners, sends)),
            pltpu.SemaphoreType.DMA((len(counts),)),
        ],
        compiler_params=pltpu.CompilerParams(vmem_limit_bytes=56 << 20),
    )(order, old_states)


def hand_on(x_ref, token_ref, out_ref):
    pass


def after(x, *others):
    corners = [other.reshape((-1,) + other.shape[-2:])[0, :8, :128] for other in others]
    anywhere = pl.BlockSpec(memory_space=pl.ANY)
    return pl.pallas_call(
        hand_on,
        out_shape=jax.ShapeDtypeStruct(x.shape, x.dtype),
        in_specs=[anywhere, anywhere],
        out_specs=anywhere,
        input_output_aliases={0: 0},
    )(x, sum(corners[1:], corners[0]))


def roll(x, by):
    return pltpu.roll(x, by % x.shape[0], 0)


def mixer_kernel(
    counts, owners, heads, classes, steps,
    me_ref, emb_ref, live_ref, gain_ref, floor_ref, ggain_ref, qw_hbm, fw_hbm, iw_hbm, ow_hbm,
    *rest,
):
    pieces, sends = len(counts), sum(counts)
    states_hbm = rest[:pieces]
    own_ref, kv_ref = rest[pieces : pieces + 2]
    parts = rest[pieces + 2 : pieces + 2 + classes]
    (qw_ref, fw_ref, iw_ref, ow_ref, states, qhi_ref, qlo_ref, mixed_ref, part_ref, sems) = rest[
        pieces + 2 + classes :
    ]
    weight_pairs = ((qw_hbm, qw_ref), (fw_hbm, fw_ref), (iw_hbm, iw_ref), (ow_hbm, ow_ref))
    loads = [
        pltpu.make_async_copy(there, here, sems.at[i]) for i, (there, here) in enumerate(weight_pairs)
    ]
    state_loads = [
        pltpu.make_async_copy(
            states_hbm[i], states.at[:, pl.ds(sum(counts[:i]), counts[i])], sems.at[4 + i]
        )
        for i in range(pieces)
    ]
    for load in loads[:3] + state_loads + loads[3:]:
        load.start()
    tokens = live_ref.shape[0]
    requests = tokens // steps
    group = requests // classes
    rows = group * steps
    stream = emb_ref[0:tokens, :].astype(F32)
    scale = lax.rsqrt(jnp.mean(stream * stream, axis=1, keepdims=True) + epsilon)
    normed = (stream * scale * gain_ref[...]).astype(BF16)
    loads[0].wait()
    query = jnp.dot(normed, qw_ref[...], preferred_element_type=F32)
    query = query * jax.nn.sigmoid(query) * HEAD_DIM ** (-0.5)
    loads[1].wait()
    forget_raw = jnp.dot(normed, fw_ref[...], preferred_element_type=F32)
    loads[2].wait()
    value = jnp.dot(normed, iw_ref[...], preferred_element_type=F32)
    floor = floor_ref[...]
    forget = jnp.where(
        live_ref[...] > 0.0, floor + (1.0 - floor) * jax.nn.sigmoid(forget_raw), 1.0
    )
    key = 1.0 - forget
    step = lax.broadcasted_iota(jnp.int32, forget.shape, 0) % steps
    upto = forget * jnp.where(step >= 1, roll(forget, 1), 1.0)
    upto = upto * jnp.where(step >= 2, roll(upto, 2), 1.0)
    after = jnp.where(step <= steps - 2, roll(forget, -1), 1.0)
    after = after * jnp.where(step <= steps - 3, roll(forget, -2), 1.0)
    after = after * jnp.where(step <= steps - 4, roll(forget, -3), 1.0)
    carried = query * upto
    high = carried.astype(BF16).astype(F32)
    qhi_ref[...] = high
    qlo_ref[...] = carried - high
    lag_key, lag_value = key, value
    local = [jnp.zeros((tokens, HEAD_DIM), F32) for _ in range(heads)]
    for lag in range(steps):
        if lag:
            lag_key = roll(lag_key, 1) * forget
            lag_value = roll(lag_value, 1)
        product = jnp.where(step >= lag, query * lag_key, 0.0)
        for head in range(heads):
            cols = slice(head * HEAD_DIM, (head + 1) * HEAD_DIM)
            weight = jnp.sum(product[:, cols], axis=1, keepdims=True)
            local[head] = local[head] + weight * lag_value[:, cols]
    for head in range(heads):
        mixed_ref[:, head * HEAD_DIM : (head + 1) * HEAD_DIM] = local[head]
    for load in state_loads:
        load.wait()
    here = me_ref[0]
    upper = lax.broadcasted_iota(jnp.int32, (8, HEAD_DIM), 0) < steps
    for tile in range(tokens // 8):
        for head in range(heads):
            cols = slice(head * HEAD_DIM, (head + 1) * HEAD_DIM)
            at = slice(tile * 8, tile * 8 + 8)
            left = jnp.concatenate([qhi_ref[at, cols], qlo_ref[at, cols]], axis=0).astype(BF16)
            got = []
            for request in (2 * tile, 2 * tile + 1):
                place = (request % group) * classes + request // group
                old = states[here ^ (place // sends), place % sends, head]
                product = jnp.dot(left, old, preferred_element_type=F32)
                got.append(product[0:8] + product[8:16])
            mixed_ref[at, cols] += jnp.where(upper, got[0], got[1])
    mixed = mixed_ref[...]
    square = jnp.sum(mixed * mixed, axis=1, keepdims=True)
    loads[3].wait()
    part_ref[:, 0:D] = jnp.dot(
        (mixed * ggain_ref[...]).astype(BF16), ow_ref[...], preferred_element_type=F32
    )
    square_high = square.astype(BF16).astype(F32)
    lane = lax.broadcasted_iota(jnp.int32, (tokens, 128), 1)
    part_ref[:, D : D + 128] = jnp.where(lane < 64, square_high, square - square_high)
    for e in range(classes):
        first = pl.multiple_of((me_ref[1] ^ e) * rows, rows)
        parts[e][...] = part_ref[pl.ds(first, rows), :].astype(BF16)
    own_ref[...] = emb_ref[pl.ds(pl.multiple_of(me_ref[1] * rows, rows), rows), :]
    both = jnp.concatenate([(key * after).astype(BF16), value.astype(BF16)], axis=0)
    shape = (2 * tokens, 2 * tokens)
    target = lax.broadcasted_iota(jnp.int32, shape, 0)
    source = lax.broadcasted_iota(jnp.int32, shape, 1)
    slot, within = target // (2 * steps), target % (2 * steps)
    place = ((slot // sends) ^ here) * sends + slot % sends
    request = (place % classes) * group + place // classes
    wanted = request * steps + within % steps + jnp.where(within >= steps, tokens, 0)
    pick = jnp.where(source == wanted, 1.0, 0.0).astype(BF16)
    kv_ref[...] = jnp.dot(pick, both, preferred_element_type=F32).astype(BF16)


def mixer(me, emb, live, gain, floor, ggain, weights, states, steps, classes):
    tokens = live.shape[0]
    counts = tuple(piece.shape[1] for piece in states)
    owners, _, heads = states[0].shape[:3]
    width = floor.shape[1]
    rows = tokens // classes
    vmem, anywhere = pl.BlockSpec(memory_space=VMEM), pl.BlockSpec(memory_space=pl.ANY)
    return pl.pallas_call(
        functools.partial(mixer_kernel, counts, owners, heads, classes, steps),
        out_shape=[
            jax.ShapeDtypeStruct((rows, D), BF16),
            jax.ShapeDtypeStruct((2 * tokens, width), BF16),
        ]
        + [jax.ShapeDtypeStruct((rows, D + 128), BF16)] * classes,
        in_specs=[pl.BlockSpec(memory_space=SMEM)] + [vmem] * 5 + [anywhere] * (4 + len(states)),
        out_specs=[vmem] * (2 + classes),
        scratch_shapes=[VMEM(w.shape, BF16) for w in weights]
        + [
            VMEM((owners, sum(counts)) + states[0].shape[2:], BF16),
            VMEM((tokens, width), F32),
            VMEM((tokens, width), F32),
            VMEM((tokens, width), F32),
            VMEM((tokens, D + 128), F32),
            pltpu.SemaphoreType.DMA((4 + len(states),)),
        ],
        compiler_params=pltpu.CompilerParams(vmem_limit_bytes=56 << 20),
    )(me, emb, live, gain, floor, ggain, *weights, *states)


def update_kernel(steps, slot_ref, kv_ref, *rest):
    states, out_ref = rest[:-1], rest[-1]
    owners, _, heads = states[0].shape[:3]
    ranks = [(piece, i) for piece in states for i in range(piece.shape[1])]
    sends = len(ranks)
    diagonal = lax.broadcasted_iota(jnp.int32, (HEAD_DIM, HEAD_DIM), 0) == lax.broadcasted_iota(
        jnp.int32, (HEAD_DIM, HEAD_DIM), 1
    )
    first = lax.broadcasted_iota(jnp.int32, (2 * steps, HEAD_DIM), 0) < steps
    for k in range(owners):
        for rank, (piece, i) in enumerate(ranks):
            place = k * sends + rank
            slot = slot_ref[place]
            for head in range(heads):
                cols = slice(head * HEAD_DIM, (head + 1) * HEAD_DIM)
                both = kv_ref[place, :, cols]
                key = jnp.where(first, both, 0.0)
                value = jnp.where(first, roll(both, steps), 0.0)
                kept = 1.0 - jnp.sum(key, axis=0, keepdims=True)
                keep = jnp.where(diagonal, kept, 0.0).astype(BF16)
                fresh = lax.dot_general(
                    key, value, (((0,), (0,)), ((), ())), preferred_element_type=F32
                )
                old = jnp.dot(keep, piece[k, i, head], preferred_element_type=F32)
                out_ref[slot, head] = (old + fresh).astype(BF16)


def update_states(slots, kv, states, steps):
    vmem = pl.BlockSpec(memory_space=VMEM)
    return pl.pallas_call(
        functools.partial(update_kernel, steps),
        out_shape=jax.ShapeDtypeStruct((slots.shape[0],) + states[0].shape[2:], BF16),
        in_specs=[pl.BlockSpec(memory_space=SMEM)] + [vmem] * (1 + len(states)),
        out_specs=vmem,
        compiler_params=pltpu.CompilerParams(vmem_limit_bytes=56 << 20),
    )(slots, kv, *states)


def greatest_kernel(full_hbm, *rest):
    count = (len(rest) - 3) // 2
    there, best_ref, full_ref, here, sems = (
        rest[:count], rest[count], rest[count + 1], rest[count + 2 : -1], rest[-1]
    )
    loads = [pltpu.make_async_copy(full_hbm, full_ref, sems.at[count])]
    loads += [pltpu.make_async_copy(there[i], here[i], sems.at[i]) for i in range(count)]
    for load in loads:
        load.start()
    loads[0].wait()
    best = None
    for i in range(count):
        loads[1 + i].wait()
        height = here[i].shape[0]
        for first in range(0, height, 256):
            entries = dot_rows(here[i][first : min(first + 256, height), :], full_ref[...])
            top = jnp.max(entries, axis=0, keepdims=True)
            best = top if best is None else jnp.maximum(best, top)
    best_ref[...] = best


def greatest_entries(full, *tables):
    anywhere = pl.BlockSpec(memory_space=pl.ANY)
    return pl.pallas_call(
        greatest_kernel,
        out_shape=jax.ShapeDtypeStruct((1, full.shape[0]), F32),
        in_specs=[anywhere] * (1 + len(tables)),
        out_specs=pl.BlockSpec(memory_space=VMEM),
        scratch_shapes=[VMEM(x.shape, BF16) for x in (full,) + tables]
        + [pltpu.SemaphoreType.DMA((1 + len(tables),))],
        compiler_params=pltpu.CompilerParams(vmem_limit_bytes=48 << 20),
    )(full, *tables)


def dot_rows(a, b):
    return lax.dot_general(a, b, (((1,), (1,)), ((), ())), preferred_element_type=F32)


def to_all(x, axis):
    return lax.all_to_all(x, axis, split_axis=0, concat_axis=0, tiled=True)


def on_device(
    token_ids, state_perm, token_count, tenant_bounds, old_states, embedding, mixer_gain,
    query_weight, forget_weight, input_weight, forget_floor, group_gain, output_weight, feed_gain,
    gate_weight, up_weight, down_weight, final_gain, tenant_gain, vocab_weight,
):
    requests, steps = token_ids.shape
    n = lax.axis_size("req")
    n_head = lax.axis_size("head")
    r = lax.axis_index("req")
    h = lax.axis_index("head")
    tokens = requests * steps
    everyone = requests * n
    sends = requests // n
    group = requests // n_head
    rows = group * steps
    width = D // n_head

    gate_full = lax.all_gather(gate_weight.T, "head", axis=1, tiled=True)
    up_full = lax.all_gather(up_weight.T, "head", axis=1, tiled=True)
    down_full = lax.all_gather(down_weight, "head", axis=0)

    packed = jnp.concatenate([token_ids.T, state_perm[None], token_count[None]], axis=0)
    packed = to_all(jnp.broadcast_to(packed[None], (n,) + packed.shape), "req").transpose(1, 0, 2).reshape(steps + 2, everyone)
    every = jnp.arange(everyone, dtype=jnp.int32)
    source = packed[steps] // requests
    rank = jnp.sum(
        ((source[None, :] == source[:, None]) & (every[None, :] < every[:, None])).astype(jnp.int32),
        axis=1,
    )
    place = ((every // requests) ^ source) * sends + rank % sends
    at = source * requests + (place % n_head) * group + place // n_head
    chosen = (at[:, None] == every[None, :]).astype(F32)
    ordered = jnp.dot(packed.astype(F32), chosen, precision=lax.Precision.HIGHEST)
    ordered = (ordered + 0.5).astype(jnp.int32)

    ids = ordered[:steps].T.reshape(n, tokens)
    table = embedding.shape[0]
    room = tokens // 2
    holder = lax.div(ids, jnp.int32(table))
    held = holder == r
    earlier = jnp.triu(jnp.ones((tokens, tokens), BF16), 1)
    turn = jnp.dot(held.astype(BF16), earlier, preferred_element_type=F32).astype(jnp.int32)
    local_ids = jnp.where(held, ids - r * table, 0)
    seat = held[:, None] & (turn[:, None] == jnp.arange(room, dtype=jnp.int32)[None, :, None])
    wanted = jnp.sum(jnp.where(seat, local_ids[:, None], 0), axis=2).reshape(n * room)
    got = to_all(jnp.take(embedding, wanted, axis=0, mode="clip").reshape(n, room, width), "req")
    own_holder = lax.dynamic_index_in_dim(holder, r, 0, keepdims=False)
    order = jnp.arange(tokens, dtype=jnp.int32)
    own_turn = jnp.sum(
        ((own_holder[None, :] == own_holder[:, None]) & (order[None, :] < order[:, None])).astype(
            jnp.int32
        ),
        axis=1,
    )
    seat = jnp.where(own_turn < room, own_holder * room + own_turn, -1)
    pick = (seat[:, None] == jnp.arange(n * room, dtype=jnp.int32)[None, :]).astype(BF16)
    embed_part = jnp.dot(
        pick, got.reshape(n * room, width), preferred_element_type=F32
    ).astype(BF16)
    owners = jnp.arange(n, dtype=jnp.int32)
    load = jnp.sum((holder[:, None] == owners[None, :, None]).astype(jnp.int32), axis=2)

    def with_rest(part):
        rows = jnp.take(embedding, local_ids.reshape(n * tokens), axis=0, mode="clip")
        rest = (held & (turn >= room)).reshape(n * tokens, 1)
        rows = jnp.where(rest, rows, jnp.zeros((), BF16)).reshape(n, tokens, width)
        return (part.astype(F32) + jnp.sum(to_all(rows, "req").astype(F32), axis=0)).astype(BF16)

    embed_part = lax.cond(jnp.max(load) > room, with_rest, lambda part: part, embed_part)
    vocab_other = swap(vocab_weight.T, "head", n_head, 1)

    gains = jnp.concatenate([final_gain[None], tenant_gain], axis=0)
    gains_high, gains_low = bf16_parts(gains)
    extra = jnp.zeros((16 - 2 * gains.shape[0], width), BF16)
    embedded = lax.all_gather(
        jnp.concatenate([embed_part, gains_high, gains_low, extra], axis=0), "head", axis=1, tiled=True
    )
    gains = embedded[tokens : tokens + 5].astype(F32) + embedded[tokens + 5 : tokens + 10].astype(F32)

    ordered = lax.dynamic_slice_in_dim(ordered, r * requests, requests, 1)
    old_order = (ordered[steps] - r * requests).reshape(n_head, group).T.reshape(n, sends)
    old_order = jnp.take(old_order, jnp.arange(n) ^ r, axis=0).reshape(requests)
    counts = (2, 2) if sends == 4 else (sends,)
    pieces = sort_states(old_order, old_states, n, counts)
    live = (jnp.arange(steps)[None, :] < ordered[steps + 1][:, None]).astype(F32)
    own, kv, *parts = mixer(
        jnp.stack([r, h]), embedded, live.reshape(tokens, 1), mixer_gain[None], forget_floor[None],
        group_gain[None], (query_weight, forget_weight, input_weight, output_weight), pieces,
        steps, n_head,
    )
    arrived = [to_all(pieces[0], "req")]

    total = parts[0].astype(F32)
    for e in range(1, n_head):
        total = total + swap(parts[e], "head", n_head, e).astype(F32)
    square = total[:, D : D + 1] + total[:, D + 127 : D + 128]
    after_mixer = own.astype(F32) + total[:, :D] * lax.rsqrt(square / D + epsilon)
    after_mixer = after(after_mixer.astype(BF16), gate_full, up_full, down_full)
    everything = lax.all_gather(after_mixer, "req", axis=0, tiled=True)
    arrived += [to_all(after(piece, after_mixer), "req") for piece in pieces[1:]]
    stream = everything.astype(F32)
    scale = lax.rsqrt(jnp.mean(stream * stream, axis=1, keepdims=True) + epsilon)
    feed_in = (stream * scale * feed_gain).astype(BF16)
    gate = dot_rows(feed_in, gate_full)
    up = dot_rows(feed_in, up_full)
    activated = (jax.nn.silu(gate) * up).astype(BF16)

    row = jnp.arange(n * rows, dtype=jnp.int32)
    by_owner, by_group, by_step = row // rows, (row % rows) // steps, row % steps
    if sends % n_head == 0:
        offset = by_group * n_head // sends
    else:
        offset = (by_group * n_head + h) // sends
    wanted = (by_owner ^ offset) * rows + by_group * steps + by_step
    pick = (wanted[None, :] == row[:, None]).astype(BF16)
    activated = jnp.dot(pick, activated, preferred_element_type=F32).astype(BF16)
    mine = (wanted[None, :] == (r * rows + row[:rows])[:, None]).astype(BF16)
    kept = jnp.dot(mine, everything, preferred_element_type=F32)
    down = jnp.concatenate(
        [jnp.dot(activated, down_full[b], preferred_element_type=F32).astype(BF16) for b in range(n_head)],
        axis=1,
    )
    down = after(down, *arrived)
    hidden = kept + jnp.sum(to_all(down.reshape(n, rows, D), "req").astype(F32), axis=0)
    mean_square = jnp.mean(hidden * hidden, axis=1, keepdims=True)

    slots = jnp.arange(requests, dtype=jnp.int32)
    source = state_perm // requests
    rank = jnp.sum(
        ((source[None, :] == source[:, None]) & (slots[None, :] < slots[:, None])).astype(jnp.int32),
        axis=1,
    )
    place = (source ^ r) * sends + rank
    natural = source * sends + rank
    slot_of = jnp.sum(jnp.where(natural[None, :] == slots[:, None], slots[None, :], 0), axis=1)
    mine = jnp.sum(
        jnp.where(
            place[None, :] == (jnp.arange(group, dtype=jnp.int32) * n_head + h)[:, None],
            slots[None, :],
            0,
        ),
        axis=1,
    )
    tenant = jnp.sum(
        ((mine + r * requests)[:, None] >= tenant_bounds[None, 1:-1]).astype(jnp.int32), axis=1
    )
    tenant_rows = sum(
        jnp.where((tenant == t)[:, None], gains[1 + t][None, :], 0.0)
        for t in range(tenant_gain.shape[0])
    )
    token_gain = jnp.repeat(tenant_rows * gains[0][None, :], steps, axis=0)
    final = (hidden * lax.rsqrt(mean_square + epsilon) * token_gain).astype(BF16)

    final = jnp.stack([final, swap(final, "head", n_head, 2)])
    arrived_kv = to_all(after(kv, final).reshape(n, -1, width), "req")
    full = lax.all_gather(final, "req", axis=0, tiled=True).reshape(n * 2 * rows, D)
    best = greatest_entries(full, vocab_weight.T, vocab_other).reshape(n, 2 * rows)
    got = jnp.max(to_all(best, "req"), axis=0)
    got = lax.all_gather(got, "head", axis=0).reshape(n_head, 2, rows)
    crossed = jnp.stack([got[i ^ 2, 1] for i in range(n_head)])
    best = jnp.maximum(got[:, 0], crossed).reshape(requests, steps)
    index = (place % n_head) * group + place // n_head
    match = (index[:, None] == slots[None, :])[:, :, None]
    best = jnp.sum(jnp.where(match, best[None], 0.0), axis=1)
    live = jnp.arange(steps)[None, :] < token_count[:, None]
    greatest = jnp.max(jnp.where(live, best, -1e30), axis=1)

    blocks = hidden.reshape(rows, n_head, width).transpose(1, 0, 2)
    tail = jnp.broadcast_to(mean_square, (rows, 128))
    whole = []
    for e in range(n_head):
        block = lax.dynamic_index_in_dim(blocks, h ^ e, 0, keepdims=False)
        block = jnp.concatenate([block, tail], axis=1)
        whole.append(block if e == 0 else swap(block, "head", n_head, e))
    whole = jnp.stack(whole).reshape(requests, steps, width + 128)
    index = ((place % n_head) ^ h) * group + place // n_head
    whole = jnp.take(whole, index, axis=0, mode="clip")
    last = jnp.arange(steps)[None, :] == (token_count - 1)[:, None]
    last_norm = jnp.sqrt(jnp.sum(jnp.where(last, whole[:, :, width], 0.0), axis=1) + epsilon)

    new_states = update_states(
        slot_of, arrived_kv.reshape(requests, 2 * steps, width).astype(F32), arrived, steps
    )
    return whole[:, :, :width], new_states, last_norm, greatest


def solution(mesh):
    placed = (
        P("req", None),
        P("req"),
        P("req"),
        P(),
        P("req", "head", None, None),
        P("req", "head"),
        P(),
        P(None, "head"),
        P(None, "head"),
        P(None, "head"),
        P("head"),
        P("head"),
        P("head", None),
        P(),
        P("head", "req"),
        P("head", "req"),
        P("req", "head"),
        P("head"),
        P(None, "head"),
        P(None, ("req", "head")),
    )
    return jax.shard_map(
        on_device,
        mesh=mesh,
        in_specs=placed,
        out_specs=(P("req", None, "head"), P("req", "head", None, None), P("req"), P("req")),
        check_vma=False,
    )
```

```python
import functools

import jax
import jax.numpy as jnp
import numpy as np
from jax import lax
from jax.experimental import pallas as pl
from jax.experimental.pallas import tpu as pltpu
from jax.sharding import PartitionSpec as P

D = 2048
HEAD_DIM = 128
epsilon = 1e-06
F32 = jnp.float32
BF16 = jnp.bfloat16
VMEM = pltpu.VMEM
SMEM = pltpu.SMEM


def swap(x, axis, size, offset):
    return lax.ppermute(x, axis, [(i, i ^ offset) for i in range(size)])


def bf16_parts(x):
    high = lax.reduce_precision(x, 8, 7)
    return high.astype(BF16), (x - high).astype(BF16)


def sort_kernel(sends, order_ref, old_ref, *rest):
    outs, (held, in_sems, out_sems) = rest[:-3], rest[-3:]
    owners = held.shape[0]
    spans, first = [], 0
    for out in outs:
        spans.append((first, out.shape[1]))
        first += out.shape[1]

    def load(owner, rank):
        at = owner * sends + rank
        return pltpu.make_async_copy(
            old_ref.at[order_ref[at]], held.at[owner, rank], in_sems.at[owner, rank]
        )

    def store(part):
        first, count = spans[part]
        return pltpu.make_async_copy(
            held.at[:, pl.ds(first, count)], outs[part], out_sems.at[part]
        )

    for first, count in spans:
        for owner in range(owners):
            for rank in range(first, first + count):
                load(owner, rank).start()
    for part, (first, count) in enumerate(spans):
        for owner in range(owners):
            for rank in range(first, first + count):
                load(owner, rank).wait()
        store(part).start()
    for part in range(len(outs)):
        store(part).wait()


def sort_states(order, old_states, owners, counts):
    sends = sum(counts)
    state = old_states.shape[1:]
    return pl.pallas_call(
        functools.partial(sort_kernel, sends),
        out_shape=[
            jax.ShapeDtypeStruct((owners, count) + state, old_states.dtype) for count in counts
        ],
        in_specs=[pl.BlockSpec(memory_space=SMEM), pl.BlockSpec(memory_space=pl.ANY)],
        out_specs=[pl.BlockSpec(memory_space=pl.ANY)] * len(counts),
        scratch_shapes=[
            VMEM((owners, sends) + state, old_states.dtype),
            pltpu.SemaphoreType.DMA((owners, sends)),
            pltpu.SemaphoreType.DMA((len(counts),)),
        ],
        compiler_params=pltpu.CompilerParams(vmem_limit_bytes=56 << 20),
    )(order, old_states)


def hand_on(*refs):
    pass


def after(x, *others):
    anywhere = pl.BlockSpec(memory_space=pl.ANY)
    return pl.pallas_call(
        hand_on,
        out_shape=jax.ShapeDtypeStruct(x.shape, x.dtype),
        in_specs=[anywhere] * (1 + len(others)),
        out_specs=anywhere,
        input_output_aliases={0: 0},
    )(x, *others)


def roll(x, by):
    return pltpu.roll(x, by % x.shape[0], 0)


def mixer_kernel(
    counts, owners, heads, classes, steps,
    me_ref, emb_ref, live_ref, gain_ref, floor_ref, ggain_ref, qw_hbm, fw_hbm, iw_hbm, ow_hbm,
    *rest,
):
    pieces, sends = len(counts), sum(counts)
    states_hbm = rest[:pieces]
    own_ref, kv_ref = rest[pieces : pieces + 2]
    parts = rest[pieces + 2 : pieces + 2 + classes]
    (qw_ref, fw_ref, iw_ref, ow_ref, states, qhi_ref, qlo_ref, mixed_ref, part_ref, sems) = rest[
        pieces + 2 + classes :
    ]
    weight_pairs = ((qw_hbm, qw_ref), (fw_hbm, fw_ref), (iw_hbm, iw_ref), (ow_hbm, ow_ref))
    loads = [
        pltpu.make_async_copy(there, here, sems.at[i]) for i, (there, here) in enumerate(weight_pairs)
    ]
    state_loads = [
        pltpu.make_async_copy(
            states_hbm[i], states.at[:, pl.ds(sum(counts[:i]), counts[i])], sems.at[4 + i]
        )
        for i in range(pieces)
    ]
    for load in loads[:3] + state_loads + loads[3:]:
        load.start()
    tokens = live_ref.shape[0]
    requests = tokens // steps
    group = requests // classes
    rows = group * steps
    stream = emb_ref[0:tokens, :].astype(F32)
    scale = lax.rsqrt(jnp.mean(stream * stream, axis=1, keepdims=True) + epsilon)
    normed = (stream * scale * gain_ref[...]).astype(BF16)
    loads[0].wait()
    query = jnp.dot(normed, qw_ref[...], preferred_element_type=F32)
    query = query * jax.nn.sigmoid(query) * HEAD_DIM ** (-0.5)
    loads[1].wait()
    forget_raw = jnp.dot(normed, fw_ref[...], preferred_element_type=F32)
    loads[2].wait()
    value = jnp.dot(normed, iw_ref[...], preferred_element_type=F32)
    floor = floor_ref[...]
    forget = jnp.where(
        live_ref[...] > 0.0, floor + (1.0 - floor) * jax.nn.sigmoid(forget_raw), 1.0
    )
    key = 1.0 - forget
    step = lax.broadcasted_iota(jnp.int32, forget.shape, 0) % steps
    upto = forget * jnp.where(step >= 1, roll(forget, 1), 1.0)
    upto = upto * jnp.where(step >= 2, roll(upto, 2), 1.0)
    after = jnp.where(step <= steps - 2, roll(forget, -1), 1.0)
    after = after * jnp.where(step <= steps - 3, roll(forget, -2), 1.0)
    after = after * jnp.where(step <= steps - 4, roll(forget, -3), 1.0)
    carried = query * upto
    high = carried.astype(BF16).astype(F32)
    qhi_ref[...] = high
    qlo_ref[...] = carried - high
    lag_key, lag_value = key, value
    local = [jnp.zeros((tokens, HEAD_DIM), F32) for _ in range(heads)]
    for lag in range(steps):
        if lag:
            lag_key = roll(lag_key, 1) * forget
            lag_value = roll(lag_value, 1)
        product = jnp.where(step >= lag, query * lag_key, 0.0)
        for head in range(heads):
            cols = slice(head * HEAD_DIM, (head + 1) * HEAD_DIM)
            weight = jnp.sum(product[:, cols], axis=1, keepdims=True)
            local[head] = local[head] + weight * lag_value[:, cols]
    for head in range(heads):
        mixed_ref[:, head * HEAD_DIM : (head + 1) * HEAD_DIM] = local[head]
    for load in state_loads:
        load.wait()
    here = me_ref[0]
    upper = lax.broadcasted_iota(jnp.int32, (8, HEAD_DIM), 0) < steps
    for tile in range(tokens // 8):
        for head in range(heads):
            cols = slice(head * HEAD_DIM, (head + 1) * HEAD_DIM)
            at = slice(tile * 8, tile * 8 + 8)
            left = jnp.concatenate([qhi_ref[at, cols], qlo_ref[at, cols]], axis=0).astype(BF16)
            got = []
            for request in (2 * tile, 2 * tile + 1):
                place = (request % group) * classes + request // group
                old = states[here ^ (place // sends), place % sends, head]
                product = jnp.dot(left, old, preferred_element_type=F32)
                got.append(product[0:8] + product[8:16])
            mixed_ref[at, cols] += jnp.where(upper, got[0], got[1])
    mixed = mixed_ref[...]
    square = jnp.sum(mixed * mixed, axis=1, keepdims=True)
    loads[3].wait()
    part_ref[:, 0:D] = jnp.dot(
        (mixed * ggain_ref[...]).astype(BF16), ow_ref[...], preferred_element_type=F32
    )
    square_high = square.astype(BF16).astype(F32)
    lane = lax.broadcasted_iota(jnp.int32, (tokens, 128), 1)
    part_ref[:, D : D + 128] = jnp.where(lane < 64, square_high, square - square_high)
    for e in range(classes):
        first = pl.multiple_of((me_ref[1] ^ e) * rows, rows)
        parts[e][...] = part_ref[pl.ds(first, rows), :].astype(BF16)
    own_ref[...] = emb_ref[pl.ds(pl.multiple_of(me_ref[1] * rows, rows), rows), :]
    both = jnp.concatenate([(key * after).astype(BF16), value.astype(BF16)], axis=0)
    shape = (2 * tokens, 2 * tokens)
    target = lax.broadcasted_iota(jnp.int32, shape, 0)
    source = lax.broadcasted_iota(jnp.int32, shape, 1)
    slot, within = target // (2 * steps), target % (2 * steps)
    place = ((slot // sends) ^ here) * sends + slot % sends
    request = (place % classes) * group + place // classes
    wanted = request * steps + within % steps + jnp.where(within >= steps, tokens, 0)
    pick = jnp.where(source == wanted, 1.0, 0.0).astype(BF16)
    kv_ref[...] = jnp.dot(pick, both, preferred_element_type=F32).astype(BF16)


def mixer(me, emb, live, gain, floor, ggain, weights, states, steps, classes):
    tokens = live.shape[0]
    counts = tuple(piece.shape[1] for piece in states)
    owners, _, heads = states[0].shape[:3]
    width = floor.shape[1]
    rows = tokens // classes
    vmem, anywhere = pl.BlockSpec(memory_space=VMEM), pl.BlockSpec(memory_space=pl.ANY)
    return pl.pallas_call(
        functools.partial(mixer_kernel, counts, owners, heads, classes, steps),
        out_shape=[
            jax.ShapeDtypeStruct((rows, D), BF16),
            jax.ShapeDtypeStruct((2 * tokens, width), BF16),
        ]
        + [jax.ShapeDtypeStruct((rows, D + 128), BF16)] * classes,
        in_specs=[pl.BlockSpec(memory_space=SMEM)] + [vmem] * 5 + [anywhere] * (4 + len(states)),
        out_specs=[vmem] * (2 + classes),
        scratch_shapes=[VMEM(w.shape, BF16) for w in weights]
        + [
            VMEM((owners, sum(counts)) + states[0].shape[2:], BF16),
            VMEM((tokens, width), F32),
            VMEM((tokens, width), F32),
            VMEM((tokens, width), F32),
            VMEM((tokens, D + 128), F32),
            pltpu.SemaphoreType.DMA((4 + len(states),)),
        ],
        compiler_params=pltpu.CompilerParams(vmem_limit_bytes=56 << 20),
    )(me, emb, live, gain, floor, ggain, *weights, *states)


def update_kernel(steps, slot_ref, kv_ref, *rest):
    states, out_ref = rest[:-1], rest[-1]
    owners, _, heads = states[0].shape[:3]
    ranks = [(piece, i) for piece in states for i in range(piece.shape[1])]
    sends = len(ranks)
    diagonal = lax.broadcasted_iota(jnp.int32, (HEAD_DIM, HEAD_DIM), 0) == lax.broadcasted_iota(
        jnp.int32, (HEAD_DIM, HEAD_DIM), 1
    )
    first = lax.broadcasted_iota(jnp.int32, (2 * steps, HEAD_DIM), 0) < steps
    for k in range(owners):
        for rank, (piece, i) in enumerate(ranks):
            place = k * sends + rank
            slot = slot_ref[place]
            for head in range(heads):
                cols = slice(head * HEAD_DIM, (head + 1) * HEAD_DIM)
                both = kv_ref[place, :, cols]
                key = jnp.where(first, both, 0.0)
                value = jnp.where(first, roll(both, steps), 0.0)
                kept = 1.0 - jnp.sum(key, axis=0, keepdims=True)
                keep = jnp.where(diagonal, kept, 0.0).astype(BF16)
                fresh = lax.dot_general(
                    key, value, (((0,), (0,)), ((), ())), preferred_element_type=F32
                )
                old = jnp.dot(keep, piece[k, i, head], preferred_element_type=F32)
                out_ref[slot, head] = (old + fresh).astype(BF16)


def update_states(slots, kv, states, steps):
    vmem = pl.BlockSpec(memory_space=VMEM)
    return pl.pallas_call(
        functools.partial(update_kernel, steps),
        out_shape=jax.ShapeDtypeStruct((slots.shape[0],) + states[0].shape[2:], BF16),
        in_specs=[pl.BlockSpec(memory_space=SMEM)] + [vmem] * (1 + len(states)),
        out_specs=vmem,
        compiler_params=pltpu.CompilerParams(vmem_limit_bytes=56 << 20),
    )(slots, kv, *states)


def dot_rows(a, b):
    return lax.dot_general(a, b, (((1,), (1,)), ((), ())), preferred_element_type=F32)


def feed_kernel(
    x_hbm, weights_hbm, pick_ref, mine_ref, gain_ref, down_ref, kept_ref, x, weights, feed, act, sems
):
    blocks, height, depth = weights.shape
    units = height // 3
    loads = [pltpu.make_async_copy(x_hbm, x, sems.at[3])]
    for i in range(3):
        span = pl.ds(i * units, units)
        loads.append(
            pltpu.make_async_copy(weights_hbm.at[:, span], weights.at[:, span], sems.at[i])
        )
    for load in loads:
        load.start()
    loads[0].wait()
    stream = x[...].astype(F32)
    scale = lax.rsqrt(jnp.mean(stream * stream, axis=1, keepdims=True) + epsilon)
    feed[...] = (stream * scale * gain_ref[...]).astype(BF16)
    kept_ref[...] = jnp.dot(mine_ref[...], x[...], preferred_element_type=F32).astype(BF16)
    loads[1].wait()
    loads[2].wait()
    for first in range(0, units, 256):
        last = min(first + 256, units)
        gate = up = 0.0
        for b in range(blocks):
            part = feed[:, b * depth : (b + 1) * depth]
            gate += dot_rows(part, weights[b, first:last, :])
            up += dot_rows(part, weights[b, units + first : units + last, :])
        act[:, first:last] = (gate * jax.nn.sigmoid(gate) * up).astype(BF16)
    placed = jnp.dot(pick_ref[...], act[...], preferred_element_type=F32).astype(BF16)
    loads[3].wait()
    for b in range(blocks):
        down_ref[:, b * depth : (b + 1) * depth] = jnp.dot(
            placed, weights[b, 2 * units :, :], preferred_element_type=F32
        ).astype(BF16)


def feed_forward(x, weights, pick, mine, gain):
    vmem, anywhere = pl.BlockSpec(memory_space=VMEM), pl.BlockSpec(memory_space=pl.ANY)
    tokens, width = x.shape
    return pl.pallas_call(
        feed_kernel,
        out_shape=[
            jax.ShapeDtypeStruct((tokens, width), BF16),
            jax.ShapeDtypeStruct((mine.shape[0], width), BF16),
        ],
        in_specs=[anywhere] * 2 + [vmem] * 3,
        out_specs=[vmem] * 2,
        scratch_shapes=[
            VMEM(x.shape, BF16),
            VMEM(weights.shape, BF16),
            VMEM(x.shape, BF16),
            VMEM((tokens, weights.shape[1] // 3), BF16),
            pltpu.SemaphoreType.DMA((4,)),
        ],
        compiler_params=pltpu.CompilerParams(vmem_limit_bytes=58 << 20),
    )(x, weights, pick, mine, gain)


def greatest_kernel(states_hbm, full_hbm, own_hbm, other_hbm, best_ref, full, own, other, sems):
    loads = [
        pltpu.make_async_copy(there, here, sems.at[i])
        for i, (there, here) in enumerate(((full_hbm, full), (own_hbm, own), (other_hbm, other)))
    ]
    for load in loads:
        load.start()
    loads[0].wait()
    best = None
    for i, table in enumerate((own, other)):
        loads[1 + i].wait()
        height = table.shape[0]
        for first in range(0, height, 256):
            entries = dot_rows(table[first : min(first + 256, height), :], full[...])
            top = jnp.max(entries, axis=0, keepdims=True)
            best = top if best is None else jnp.maximum(best, top)
    width = best_ref.shape[1]
    for k in range(best_ref.shape[0]):
        best_ref[k : k + 1, :] = best[:, k * width : (k + 1) * width]


def greatest_entries(blocks, states, full, own, other):
    anywhere = pl.BlockSpec(memory_space=pl.ANY)
    return pl.pallas_call(
        greatest_kernel,
        out_shape=jax.ShapeDtypeStruct((blocks, full.shape[0] // blocks), F32),
        in_specs=[anywhere] * 4,
        out_specs=pl.BlockSpec(memory_space=VMEM),
        scratch_shapes=[VMEM(x.shape, BF16) for x in (full, own, other)]
        + [pltpu.SemaphoreType.DMA((3,))],
        compiler_params=pltpu.CompilerParams(vmem_limit_bytes=58 << 20),
    )(states, full, own, other)


def to_all(x, axis):
    return lax.all_to_all(x, axis, split_axis=0, concat_axis=0, tiled=True)


def on_device(
    token_ids, state_perm, token_count, tenant_bounds, old_states, embedding, mixer_gain,
    query_weight, forget_weight, input_weight, forget_floor, group_gain, output_weight, feed_gain,
    gate_weight, up_weight, down_weight, final_gain, tenant_gain, vocab_weight,
):
    requests, steps = token_ids.shape
    n = lax.axis_size("req")
    n_head = lax.axis_size("head")
    r = lax.axis_index("req")
    h = lax.axis_index("head")
    tokens = requests * steps
    everyone = requests * n
    sends = requests // n
    group = requests // n_head
    rows = group * steps
    width = D // n_head

    feed_weights = jnp.concatenate([gate_weight.T, up_weight.T, down_weight], axis=0)
    feed_weights = lax.all_gather(feed_weights, "head", axis=0)

    packed = jnp.concatenate([token_ids.T, state_perm[None], token_count[None]], axis=0)
    packed = to_all(jnp.broadcast_to(packed[None], (n,) + packed.shape), "req").transpose(1, 0, 2).reshape(steps + 2, everyone)
    every = jnp.arange(everyone, dtype=jnp.int32)
    source = packed[steps] // requests
    rank = jnp.sum(
        ((source[None, :] == source[:, None]) & (every[None, :] < every[:, None])).astype(jnp.int32),
        axis=1,
    )
    place = ((every // requests) ^ source) * sends + rank % sends
    at = source * requests + (place % n_head) * group + place // n_head
    chosen = (at[:, None] == every[None, :]).astype(F32)
    ordered = jnp.dot(packed.astype(F32), chosen, precision=lax.Precision.HIGHEST)
    ordered = (ordered + 0.5).astype(jnp.int32)

    ids = ordered[:steps].T.reshape(n, tokens)
    table = embedding.shape[0]
    room = tokens // 2
    holder = lax.div(ids, jnp.int32(table))
    held = holder == r
    earlier = jnp.triu(jnp.ones((tokens, tokens), BF16), 1)
    turn = jnp.dot(held.astype(BF16), earlier, preferred_element_type=F32).astype(jnp.int32)
    local_ids = jnp.where(held, ids - r * table, 0)
    seat = held[:, None] & (turn[:, None] == jnp.arange(room, dtype=jnp.int32)[None, :, None])
    wanted = jnp.sum(jnp.where(seat, local_ids[:, None], 0), axis=2).reshape(n * room)
    got = to_all(jnp.take(embedding, wanted, axis=0, mode="clip").reshape(n, room, width), "req")
    own_holder = lax.dynamic_index_in_dim(holder, r, 0, keepdims=False)
    order = jnp.arange(tokens, dtype=jnp.int32)
    own_turn = jnp.sum(
        ((own_holder[None, :] == own_holder[:, None]) & (order[None, :] < order[:, None])).astype(
            jnp.int32
        ),
        axis=1,
    )
    seat = jnp.where(own_turn < room, own_holder * room + own_turn, -1)
    pick = (seat[:, None] == jnp.arange(n * room, dtype=jnp.int32)[None, :]).astype(BF16)
    embed_part = jnp.dot(
        pick, got.reshape(n * room, width), preferred_element_type=F32
    ).astype(BF16)
    owners = jnp.arange(n, dtype=jnp.int32)
    load = jnp.sum((holder[:, None] == owners[None, :, None]).astype(jnp.int32), axis=2)

    def with_rest(part):
        rows = jnp.take(embedding, local_ids.reshape(n * tokens), axis=0, mode="clip")
        rest = (held & (turn >= room)).reshape(n * tokens, 1)
        rows = jnp.where(rest, rows, jnp.zeros((), BF16)).reshape(n, tokens, width)
        return (part.astype(F32) + jnp.sum(to_all(rows, "req").astype(F32), axis=0)).astype(BF16)

    embed_part = lax.cond(jnp.max(load) > room, with_rest, lambda part: part, embed_part)
    vocab_other = swap(vocab_weight.T, "head", n_head, 1)

    gains = jnp.concatenate([final_gain[None], tenant_gain], axis=0)
    gains_high, gains_low = bf16_parts(gains)
    extra = jnp.zeros((16 - 2 * gains.shape[0], width), BF16)
    embedded = lax.all_gather(
        jnp.concatenate([embed_part, gains_high, gains_low, extra], axis=0), "head", axis=1, tiled=True
    )
    gains = embedded[tokens : tokens + 5].astype(F32) + embedded[tokens + 5 : tokens + 10].astype(F32)

    ordered = lax.dynamic_slice_in_dim(ordered, r * requests, requests, 1)
    old_order = (ordered[steps] - r * requests).reshape(n_head, group).T.reshape(n, sends)
    old_order = jnp.take(old_order, jnp.arange(n) ^ r, axis=0).reshape(requests)
    counts = (1, 1, 1, 1) if sends == 4 else (sends,)
    pieces = sort_states(old_order, old_states, n, counts)
    live = (jnp.arange(steps)[None, :] < ordered[steps + 1][:, None]).astype(F32)
    own, kv, *parts = mixer(
        jnp.stack([r, h]), embedded, live.reshape(tokens, 1), mixer_gain[None], forget_floor[None],
        group_gain[None], (query_weight, forget_weight, input_weight, output_weight), pieces,
        steps, n_head,
    )
    arrived = [to_all(pieces[0], "req")]

    total = parts[0].astype(F32)
    for e in range(1, n_head):
        total = total + swap(parts[e], "head", n_head, e).astype(F32)
    square = total[:, D : D + 1] + total[:, D + 127 : D + 128]
    after_mixer = own.astype(F32) + total[:, :D] * lax.rsqrt(square / D + epsilon)
    after_mixer = after(after_mixer.astype(BF16), feed_weights)
    everything = lax.all_gather(after_mixer, "req", axis=0, tiled=True)
    for piece in pieces[1:3]:
        arrived += [to_all(after(piece, after_mixer, *arrived[1:]), "req")]

    row = jnp.arange(n * rows, dtype=jnp.int32)
    by_owner, by_group, by_step = row // rows, (row % rows) // steps, row % steps
    if sends % n_head == 0:
        offset = by_group * n_head // sends
    else:
        offset = (by_group * n_head + h) // sends
    wanted = (by_owner ^ offset) * rows + by_group * steps + by_step
    pick = (wanted[None, :] == row[:, None]).astype(BF16)
    mine = (wanted[None, :] == (r * rows + row[:rows])[:, None]).astype(BF16)
    down, kept = feed_forward(everything, feed_weights, pick, mine, feed_gain[None])
    down = after(down, *arrived)
    hidden = kept.astype(F32) + jnp.sum(to_all(down.reshape(n, rows, D), "req").astype(F32), axis=0)
    mean_square = jnp.mean(hidden * hidden, axis=1, keepdims=True)

    slots = jnp.arange(requests, dtype=jnp.int32)
    source = state_perm // requests
    rank = jnp.sum(
        ((source[None, :] == source[:, None]) & (slots[None, :] < slots[:, None])).astype(jnp.int32),
        axis=1,
    )
    place = (source ^ r) * sends + rank
    natural = source * sends + rank
    slot_of = jnp.sum(jnp.where(natural[None, :] == slots[:, None], slots[None, :], 0), axis=1)
    mine = jnp.sum(
        jnp.where(
            place[None, :] == (jnp.arange(group, dtype=jnp.int32) * n_head + h)[:, None],
            slots[None, :],
            0,
        ),
        axis=1,
    )
    tenant = jnp.sum(
        ((mine + r * requests)[:, None] >= tenant_bounds[None, 1:-1]).astype(jnp.int32), axis=1
    )
    tenant_rows = sum(
        jnp.where((tenant == t)[:, None], gains[1 + t][None, :], 0.0)
        for t in range(tenant_gain.shape[0])
    )
    token_gain = jnp.repeat(tenant_rows * gains[0][None, :], steps, axis=0)
    final = (hidden * lax.rsqrt(mean_square + epsilon) * token_gain).astype(BF16)

    final = jnp.stack([final, swap(final, "head", n_head, 2)])
    arrived += [to_all(after(piece, final), "req") for piece in pieces[3:]]
    arrived_kv = to_all(after(kv, final).reshape(n, -1, width), "req")
    full = lax.all_gather(final, "req", axis=0, tiled=True).reshape(n * 2 * rows, D)
    new_states = update_states(
        slot_of, arrived_kv.reshape(requests, 2 * steps, width).astype(F32), arrived, steps
    )
    best = greatest_entries(n, new_states, full, vocab_weight.T, vocab_other)
    got = jnp.max(to_all(best, "req"), axis=0)
    got = lax.all_gather(got, "head", axis=0).reshape(n_head, 2, rows)
    crossed = jnp.stack([got[i ^ 2, 1] for i in range(n_head)])
    best = jnp.maximum(got[:, 0], crossed).reshape(requests, steps)
    index = (place % n_head) * group + place // n_head
    match = (index[:, None] == slots[None, :])[:, :, None]
    best = jnp.sum(jnp.where(match, best[None], 0.0), axis=1)
    live = jnp.arange(steps)[None, :] < token_count[:, None]
    greatest = jnp.max(jnp.where(live, best, -1e30), axis=1)

    blocks = hidden.reshape(rows, n_head, width).transpose(1, 0, 2)
    tail = jnp.broadcast_to(mean_square, (rows, 128))
    whole = []
    for e in range(n_head):
        block = lax.dynamic_index_in_dim(blocks, h ^ e, 0, keepdims=False)
        block = jnp.concatenate([block, tail], axis=1)
        whole.append(block if e == 0 else swap(block, "head", n_head, e))
    whole = jnp.stack(whole).reshape(requests, steps, width + 128)
    index = ((place % n_head) ^ h) * group + place // n_head
    whole = jnp.take(whole, index, axis=0, mode="clip")
    last = jnp.arange(steps)[None, :] == (token_count - 1)[:, None]
    last_norm = jnp.sqrt(jnp.sum(jnp.where(last, whole[:, :, width], 0.0), axis=1) + epsilon)

    return whole[:, :, :width], new_states, last_norm, greatest


def solution(mesh):
    placed = (
        P("req", None),
        P("req"),
        P("req"),
        P(),
        P("req", "head", None, None),
        P("req", "head"),
        P(),
        P(None, "head"),
        P(None, "head"),
        P(None, "head"),
        P("head"),
        P("head"),
        P("head", None),
        P(),
        P("head", "req"),
        P("head", "req"),
        P("req", "head"),
        P("head"),
        P(None, "head"),
        P(None, ("req", "head")),
    )
    return jax.shard_map(
        on_device,
        mesh=mesh,
        in_specs=placed,
        out_specs=(P("req", None, "head"), P("req", "head", None, None), P("req"), P("req")),
        check_vma=False,
    )
```

```python
import functools

import jax
import jax.numpy as jnp
import numpy as np
from jax import lax
from jax.experimental import pallas as pl
from jax.experimental.pallas import tpu as pltpu
from jax.sharding import PartitionSpec as P

D = 2048
HEAD_DIM = 128
epsilon = 1e-06
F32 = jnp.float32
BF16 = jnp.bfloat16
VMEM = pltpu.VMEM
SMEM = pltpu.SMEM


def swap(x, axis, size, offset):
    return lax.ppermute(x, axis, [(i, i ^ offset) for i in range(size)])


def bf16_parts(x):
    high = lax.reduce_precision(x, 8, 7)
    return high.astype(BF16), (x - high).astype(BF16)


def sort_kernel(sends, order_ref, old_ref, *rest):
    outs, (held, in_sems, out_sems) = rest[:-3], rest[-3:]
    owners = held.shape[0]
    spans, first = [], 0
    for out in outs:
        spans.append((first, out.shape[1]))
        first += out.shape[1]

    def load(owner, rank):
        at = owner * sends + rank
        return pltpu.make_async_copy(
            old_ref.at[order_ref[at]], held.at[owner, rank], in_sems.at[owner, rank]
        )

    def store(part):
        first, count = spans[part]
        return pltpu.make_async_copy(
            held.at[:, pl.ds(first, count)], outs[part], out_sems.at[part]
        )

    for first, count in spans:
        for owner in range(owners):
            for rank in range(first, first + count):
                load(owner, rank).start()
    for part, (first, count) in enumerate(spans):
        for owner in range(owners):
            for rank in range(first, first + count):
                load(owner, rank).wait()
        store(part).start()
    for part in range(len(outs)):
        store(part).wait()


def sort_states(order, old_states, owners, counts):
    sends = sum(counts)
    state = old_states.shape[1:]
    return pl.pallas_call(
        functools.partial(sort_kernel, sends),
        out_shape=[
            jax.ShapeDtypeStruct((owners, count) + state, old_states.dtype) for count in counts
        ],
        in_specs=[pl.BlockSpec(memory_space=SMEM), pl.BlockSpec(memory_space=pl.ANY)],
        out_specs=[pl.BlockSpec(memory_space=pl.ANY)] * len(counts),
        scratch_shapes=[
            VMEM((owners, sends) + state, old_states.dtype),
            pltpu.SemaphoreType.DMA((owners, sends)),
            pltpu.SemaphoreType.DMA((len(counts),)),
        ],
        compiler_params=pltpu.CompilerParams(vmem_limit_bytes=56 << 20),
    )(order, old_states)


def hand_on(*refs):
    pass


def after(x, *others):
    anywhere = pl.BlockSpec(memory_space=pl.ANY)
    return pl.pallas_call(
        hand_on,
        out_shape=jax.ShapeDtypeStruct(x.shape, x.dtype),
        in_specs=[anywhere] * (1 + len(others)),
        out_specs=anywhere,
        input_output_aliases={0: 0},
    )(x, *others)


def roll(x, by):
    return pltpu.roll(x, by % x.shape[0], 0)


def mixer_kernel(
    counts, owners, heads, classes, steps,
    me_ref, emb_ref, live_ref, gain_ref, floor_ref, ggain_ref, qw_hbm, fw_hbm, iw_hbm, ow_hbm,
    *rest,
):
    pieces, sends = len(counts), sum(counts)
    states_hbm = rest[:pieces]
    own_ref, kv_ref = rest[pieces : pieces + 2]
    parts = rest[pieces + 2 : pieces + 2 + classes]
    (qw_ref, fw_ref, iw_ref, ow_ref, states, qhi_ref, qlo_ref, mixed_ref, part_ref, sems) = rest[
        pieces + 2 + classes :
    ]
    weight_pairs = ((qw_hbm, qw_ref), (fw_hbm, fw_ref), (iw_hbm, iw_ref), (ow_hbm, ow_ref))
    loads = [
        pltpu.make_async_copy(there, here, sems.at[i]) for i, (there, here) in enumerate(weight_pairs)
    ]
    state_loads = [
        pltpu.make_async_copy(
            states_hbm[i], states.at[:, pl.ds(sum(counts[:i]), counts[i])], sems.at[4 + i]
        )
        for i in range(pieces)
    ]
    for load in loads[:3] + state_loads + loads[3:]:
        load.start()
    tokens = live_ref.shape[0]
    requests = tokens // steps
    group = requests // classes
    rows = group * steps
    stream = emb_ref[0:tokens, :].astype(F32)
    scale = lax.rsqrt(jnp.mean(stream * stream, axis=1, keepdims=True) + epsilon)
    normed = (stream * scale * gain_ref[...]).astype(BF16)
    loads[0].wait()
    query = jnp.dot(normed, qw_ref[...], preferred_element_type=F32)
    query = query * jax.nn.sigmoid(query) * HEAD_DIM ** (-0.5)
    loads[1].wait()
    forget_raw = jnp.dot(normed, fw_ref[...], preferred_element_type=F32)
    loads[2].wait()
    value = jnp.dot(normed, iw_ref[...], preferred_element_type=F32)
    floor = floor_ref[...]
    forget = jnp.where(
        live_ref[...] > 0.0, floor + (1.0 - floor) * jax.nn.sigmoid(forget_raw), 1.0
    )
    key = 1.0 - forget
    step = lax.broadcasted_iota(jnp.int32, forget.shape, 0) % steps
    upto = forget * jnp.where(step >= 1, roll(forget, 1), 1.0)
    upto = upto * jnp.where(step >= 2, roll(upto, 2), 1.0)
    after = jnp.where(step <= steps - 2, roll(forget, -1), 1.0)
    after = after * jnp.where(step <= steps - 3, roll(forget, -2), 1.0)
    after = after * jnp.where(step <= steps - 4, roll(forget, -3), 1.0)
    carried = query * upto
    high = carried.astype(BF16).astype(F32)
    qhi_ref[...] = high
    qlo_ref[...] = carried - high
    lag_key, lag_value = key, value
    local = [jnp.zeros((tokens, HEAD_DIM), F32) for _ in range(heads)]
    for lag in range(steps):
        if lag:
            lag_key = roll(lag_key, 1) * forget
            lag_value = roll(lag_value, 1)
        product = jnp.where(step >= lag, query * lag_key, 0.0)
        for head in range(heads):
            cols = slice(head * HEAD_DIM, (head + 1) * HEAD_DIM)
            weight = jnp.sum(product[:, cols], axis=1, keepdims=True)
            local[head] = local[head] + weight * lag_value[:, cols]
    for head in range(heads):
        mixed_ref[:, head * HEAD_DIM : (head + 1) * HEAD_DIM] = local[head]
    for load in state_loads:
        load.wait()
    here = me_ref[0]
    upper = lax.broadcasted_iota(jnp.int32, (8, HEAD_DIM), 0) < steps
    for tile in range(tokens // 8):
        for head in range(heads):
            cols = slice(head * HEAD_DIM, (head + 1) * HEAD_DIM)
            at = slice(tile * 8, tile * 8 + 8)
            left = jnp.concatenate([qhi_ref[at, cols], qlo_ref[at, cols]], axis=0).astype(BF16)
            got = []
            for request in (2 * tile, 2 * tile + 1):
                place = (request % group) * classes + request // group
                old = states[here ^ (place // sends), place % sends, head]
                product = jnp.dot(left, old, preferred_element_type=F32)
                got.append(product[0:8] + product[8:16])
            mixed_ref[at, cols] += jnp.where(upper, got[0], got[1])
    mixed = mixed_ref[...]
    square = jnp.sum(mixed * mixed, axis=1, keepdims=True)
    loads[3].wait()
    part_ref[:, 0:D] = jnp.dot(
        (mixed * ggain_ref[...]).astype(BF16), ow_ref[...], preferred_element_type=F32
    )
    square_high = square.astype(BF16).astype(F32)
    lane = lax.broadcasted_iota(jnp.int32, (tokens, 128), 1)
    part_ref[:, D : D + 128] = jnp.where(lane < 64, square_high, square - square_high)
    for e in range(classes):
        first = pl.multiple_of((me_ref[1] ^ e) * rows, rows)
        parts[e][...] = part_ref[pl.ds(first, rows), :].astype(BF16)
    own_ref[...] = emb_ref[pl.ds(pl.multiple_of(me_ref[1] * rows, rows), rows), :]
    both = jnp.concatenate([(key * after).astype(BF16), value.astype(BF16)], axis=0)
    shape = (2 * tokens, 2 * tokens)
    target = lax.broadcasted_iota(jnp.int32, shape, 0)
    source = lax.broadcasted_iota(jnp.int32, shape, 1)
    slot, within = target // (2 * steps), target % (2 * steps)
    place = ((slot // sends) ^ here) * sends + slot % sends
    request = (place % classes) * group + place // classes
    wanted = request * steps + within % steps + jnp.where(within >= steps, tokens, 0)
    pick = jnp.where(source == wanted, 1.0, 0.0).astype(BF16)
    kv_ref[...] = jnp.dot(pick, both, preferred_element_type=F32).astype(BF16)


def mixer(me, emb, live, gain, floor, ggain, weights, states, steps, classes):
    tokens = live.shape[0]
    counts = tuple(piece.shape[1] for piece in states)
    owners, _, heads = states[0].shape[:3]
    width = floor.shape[1]
    rows = tokens // classes
    vmem, anywhere = pl.BlockSpec(memory_space=VMEM), pl.BlockSpec(memory_space=pl.ANY)
    return pl.pallas_call(
        functools.partial(mixer_kernel, counts, owners, heads, classes, steps),
        out_shape=[
            jax.ShapeDtypeStruct((rows, D), BF16),
            jax.ShapeDtypeStruct((2 * tokens, width), BF16),
        ]
        + [jax.ShapeDtypeStruct((rows, D + 128), BF16)] * classes,
        in_specs=[pl.BlockSpec(memory_space=SMEM)] + [vmem] * 5 + [anywhere] * (4 + len(states)),
        out_specs=[vmem] * (2 + classes),
        scratch_shapes=[VMEM(w.shape, BF16) for w in weights]
        + [
            VMEM((owners, sum(counts)) + states[0].shape[2:], BF16),
            VMEM((tokens, width), F32),
            VMEM((tokens, width), F32),
            VMEM((tokens, width), F32),
            VMEM((tokens, D + 128), F32),
            pltpu.SemaphoreType.DMA((4 + len(states),)),
        ],
        compiler_params=pltpu.CompilerParams(vmem_limit_bytes=56 << 20),
    )(me, emb, live, gain, floor, ggain, *weights, *states)


def update_kernel(steps, slot_ref, kv_ref, *rest):
    states, out_ref = rest[:-1], rest[-1]
    owners, _, heads = states[0].shape[:3]
    ranks = [(piece, i) for piece in states for i in range(piece.shape[1])]
    sends = len(ranks)
    diagonal = lax.broadcasted_iota(jnp.int32, (HEAD_DIM, HEAD_DIM), 0) == lax.broadcasted_iota(
        jnp.int32, (HEAD_DIM, HEAD_DIM), 1
    )
    first = lax.broadcasted_iota(jnp.int32, (2 * steps, HEAD_DIM), 0) < steps
    for k in range(owners):
        for rank, (piece, i) in enumerate(ranks):
            place = k * sends + rank
            slot = slot_ref[place]
            for head in range(heads):
                cols = slice(head * HEAD_DIM, (head + 1) * HEAD_DIM)
                both = kv_ref[place, :, cols]
                key = jnp.where(first, both, 0.0)
                value = jnp.where(first, roll(both, steps), 0.0)
                kept = 1.0 - jnp.sum(key, axis=0, keepdims=True)
                keep = jnp.where(diagonal, kept, 0.0).astype(BF16)
                fresh = lax.dot_general(
                    key, value, (((0,), (0,)), ((), ())), preferred_element_type=F32
                )
                old = jnp.dot(keep, piece[k, i, head], preferred_element_type=F32)
                out_ref[slot, head] = (old + fresh).astype(BF16)


def update_states(slots, kv, states, steps):
    vmem = pl.BlockSpec(memory_space=VMEM)
    return pl.pallas_call(
        functools.partial(update_kernel, steps),
        out_shape=jax.ShapeDtypeStruct((slots.shape[0],) + states[0].shape[2:], BF16),
        in_specs=[pl.BlockSpec(memory_space=SMEM)] + [vmem] * (1 + len(states)),
        out_specs=vmem,
        compiler_params=pltpu.CompilerParams(vmem_limit_bytes=56 << 20),
    )(slots, kv, *states)


def dot_rows(a, b):
    return lax.dot_general(a, b, (((1,), (1,)), ((), ())), preferred_element_type=F32)


def feed_kernel(
    x_hbm, weights_hbm, pick_ref, mine_ref, gain_ref, down_ref, kept_ref, x, weights, feed, act, sems
):
    blocks, height, depth = weights.shape
    units = height // 3
    loads = [pltpu.make_async_copy(x_hbm, x, sems.at[3])]
    for i in range(3):
        span = pl.ds(i * units, units)
        loads.append(
            pltpu.make_async_copy(weights_hbm.at[:, span], weights.at[:, span], sems.at[i])
        )
    for load in loads:
        load.start()
    loads[0].wait()
    stream = x[...].astype(F32)
    scale = lax.rsqrt(jnp.mean(stream * stream, axis=1, keepdims=True) + epsilon)
    feed[...] = (stream * scale * gain_ref[...]).astype(BF16)
    kept_ref[...] = jnp.dot(mine_ref[...], x[...], preferred_element_type=F32).astype(BF16)
    loads[1].wait()
    loads[2].wait()
    for first in range(0, units, 256):
        last = min(first + 256, units)
        gate = up = 0.0
        for b in range(blocks):
            part = feed[:, b * depth : (b + 1) * depth]
            gate += dot_rows(part, weights[b, first:last, :])
            up += dot_rows(part, weights[b, units + first : units + last, :])
        act[:, first:last] = (gate * jax.nn.sigmoid(gate) * up).astype(BF16)
    placed = jnp.dot(pick_ref[...], act[...], preferred_element_type=F32).astype(BF16)
    loads[3].wait()
    for b in range(blocks):
        down_ref[:, b * depth : (b + 1) * depth] = jnp.dot(
            placed, weights[b, 2 * units :, :], preferred_element_type=F32
        ).astype(BF16)


def feed_forward(x, weights, pick, mine, gain):
    vmem, anywhere = pl.BlockSpec(memory_space=VMEM), pl.BlockSpec(memory_space=pl.ANY)
    tokens, width = x.shape
    return pl.pallas_call(
        feed_kernel,
        out_shape=[
            jax.ShapeDtypeStruct((tokens, width), BF16),
            jax.ShapeDtypeStruct((mine.shape[0], width), BF16),
        ],
        in_specs=[anywhere] * 2 + [vmem] * 3,
        out_specs=[vmem] * 2,
        scratch_shapes=[
            VMEM(x.shape, BF16),
            VMEM(weights.shape, BF16),
            VMEM(x.shape, BF16),
            VMEM((tokens, weights.shape[1] // 3), BF16),
            pltpu.SemaphoreType.DMA((4,)),
        ],
        compiler_params=pltpu.CompilerParams(vmem_limit_bytes=58 << 20),
    )(x, weights, pick, mine, gain)


def greatest_kernel(full_hbm, own_hbm, other_hbm, best_ref, full, own, other, sems):
    loads = [
        pltpu.make_async_copy(there, here, sems.at[i])
        for i, (there, here) in enumerate(((full_hbm, full), (own_hbm, own), (other_hbm, other)))
    ]
    for load in loads:
        load.start()
    loads[0].wait()
    best = None
    for i, table in enumerate((own, other)):
        loads[1 + i].wait()
        height = table.shape[0]
        for first in range(0, height, 256):
            entries = dot_rows(table[first : min(first + 256, height), :], full[...])
            top = jnp.max(entries, axis=0, keepdims=True)
            best = top if best is None else jnp.maximum(best, top)
    width = best_ref.shape[1]
    for k in range(best_ref.shape[0]):
        best_ref[k : k + 1, :] = best[:, k * width : (k + 1) * width]


def greatest_entries(blocks, full, own, other):
    anywhere = pl.BlockSpec(memory_space=pl.ANY)
    return pl.pallas_call(
        greatest_kernel,
        out_shape=jax.ShapeDtypeStruct((blocks, full.shape[0] // blocks), F32),
        in_specs=[anywhere] * 3,
        out_specs=pl.BlockSpec(memory_space=VMEM),
        scratch_shapes=[VMEM(x.shape, BF16) for x in (full, own, other)]
        + [pltpu.SemaphoreType.DMA((3,))],
        compiler_params=pltpu.CompilerParams(vmem_limit_bytes=58 << 20),
    )(full, own, other)


def to_all(x, axis):
    return lax.all_to_all(x, axis, split_axis=0, concat_axis=0, tiled=True)


def on_device(
    token_ids, state_perm, token_count, tenant_bounds, old_states, embedding, mixer_gain,
    query_weight, forget_weight, input_weight, forget_floor, group_gain, output_weight, feed_gain,
    gate_weight, up_weight, down_weight, final_gain, tenant_gain, vocab_weight,
):
    requests, steps = token_ids.shape
    n = lax.axis_size("req")
    n_head = lax.axis_size("head")
    r = lax.axis_index("req")
    h = lax.axis_index("head")
    tokens = requests * steps
    everyone = requests * n
    sends = requests // n
    group = requests // n_head
    rows = group * steps
    width = D // n_head

    feed_weights = jnp.concatenate([gate_weight.T, up_weight.T, down_weight], axis=0)
    feed_weights = lax.all_gather(feed_weights, "head", axis=0)

    packed = jnp.concatenate([token_ids.T, state_perm[None], token_count[None]], axis=0)
    packed = to_all(jnp.broadcast_to(packed[None], (n,) + packed.shape), "req").transpose(1, 0, 2).reshape(steps + 2, everyone)
    every = jnp.arange(everyone, dtype=jnp.int32)
    source = packed[steps] // requests
    rank = jnp.sum(
        ((source[None, :] == source[:, None]) & (every[None, :] < every[:, None])).astype(jnp.int32),
        axis=1,
    )
    place = ((every // requests) ^ source) * sends + rank % sends
    at = source * requests + (place % n_head) * group + place // n_head
    chosen = (at[:, None] == every[None, :]).astype(F32)
    ordered = jnp.dot(packed.astype(F32), chosen, precision=lax.Precision.HIGHEST)
    ordered = (ordered + 0.5).astype(jnp.int32)

    ids = ordered[:steps].T.reshape(n, tokens)
    table = embedding.shape[0]
    room = tokens // 2
    holder = lax.div(ids, jnp.int32(table))
    held = holder == r
    earlier = jnp.triu(jnp.ones((tokens, tokens), BF16), 1)
    turn = jnp.dot(held.astype(BF16), earlier, preferred_element_type=F32).astype(jnp.int32)
    local_ids = jnp.where(held, ids - r * table, 0)
    seat = held[:, None] & (turn[:, None] == jnp.arange(room, dtype=jnp.int32)[None, :, None])
    wanted = jnp.sum(jnp.where(seat, local_ids[:, None], 0), axis=2).reshape(n * room)
    got = to_all(jnp.take(embedding, wanted, axis=0, mode="clip").reshape(n, room, width), "req")
    own_holder = lax.dynamic_index_in_dim(holder, r, 0, keepdims=False)
    order = jnp.arange(tokens, dtype=jnp.int32)
    own_turn = jnp.sum(
        ((own_holder[None, :] == own_holder[:, None]) & (order[None, :] < order[:, None])).astype(
            jnp.int32
        ),
        axis=1,
    )
    seat = jnp.where(own_turn < room, own_holder * room + own_turn, -1)
    pick = (seat[:, None] == jnp.arange(n * room, dtype=jnp.int32)[None, :]).astype(BF16)
    embed_part = jnp.dot(
        pick, got.reshape(n * room, width), preferred_element_type=F32
    ).astype(BF16)
    owners = jnp.arange(n, dtype=jnp.int32)
    load = jnp.sum((holder[:, None] == owners[None, :, None]).astype(jnp.int32), axis=2)

    def with_rest(part):
        rows = jnp.take(embedding, local_ids.reshape(n * tokens), axis=0, mode="clip")
        rest = (held & (turn >= room)).reshape(n * tokens, 1)
        rows = jnp.where(rest, rows, jnp.zeros((), BF16)).reshape(n, tokens, width)
        return (part.astype(F32) + jnp.sum(to_all(rows, "req").astype(F32), axis=0)).astype(BF16)

    embed_part = lax.cond(jnp.max(load) > room, with_rest, lambda part: part, embed_part)
    vocab_other = swap(vocab_weight.T, "head", n_head, 1)

    gains = jnp.concatenate([final_gain[None], tenant_gain], axis=0)
    gains_high, gains_low = bf16_parts(gains)
    extra = jnp.zeros((16 - 2 * gains.shape[0], width), BF16)
    embedded = lax.all_gather(
        jnp.concatenate([embed_part, gains_high, gains_low, extra], axis=0), "head", axis=1, tiled=True
    )
    gains = embedded[tokens : tokens + 5].astype(F32) + embedded[tokens + 5 : tokens + 10].astype(F32)

    ordered = lax.dynamic_slice_in_dim(ordered, r * requests, requests, 1)
    old_order = (ordered[steps] - r * requests).reshape(n_head, group).T.reshape(n, sends)
    old_order = jnp.take(old_order, jnp.arange(n) ^ r, axis=0).reshape(requests)
    counts = (2, 2) if sends == 4 else (sends,)
    pieces = sort_states(old_order, old_states, n, counts)
    live = (jnp.arange(steps)[None, :] < ordered[steps + 1][:, None]).astype(F32)
    own, kv, *parts = mixer(
        jnp.stack([r, h]), embedded, live.reshape(tokens, 1), mixer_gain[None], forget_floor[None],
        group_gain[None], (query_weight, forget_weight, input_weight, output_weight), pieces,
        steps, n_head,
    )
    arrived = [to_all(pieces[0], "req")]

    total = parts[0].astype(F32)
    for e in range(1, n_head):
        total = total + swap(parts[e], "head", n_head, e).astype(F32)
    square = total[:, D : D + 1] + total[:, D + 127 : D + 128]
    after_mixer = own.astype(F32) + total[:, :D] * lax.rsqrt(square / D + epsilon)
    after_mixer = after(after_mixer.astype(BF16), feed_weights)
    everything = lax.all_gather(after_mixer, "req", axis=0, tiled=True)
    for piece in pieces[1:]:
        arrived += [to_all(after(piece, after_mixer, *arrived), "req")]

    row = jnp.arange(n * rows, dtype=jnp.int32)
    by_owner, by_group, by_step = row // rows, (row % rows) // steps, row % steps
    if sends % n_head == 0:
        offset = by_group * n_head // sends
    else:
        offset = (by_group * n_head + h) // sends
    wanted = (by_owner ^ offset) * rows + by_group * steps + by_step
    pick = (wanted[None, :] == row[:, None]).astype(BF16)
    mine = (wanted[None, :] == (r * rows + row[:rows])[:, None]).astype(BF16)
    down, kept = feed_forward(everything, feed_weights, pick, mine, feed_gain[None])
    down = after(down, *arrived)
    hidden = kept.astype(F32) + jnp.sum(to_all(down.reshape(n, rows, D), "req").astype(F32), axis=0)
    mean_square = jnp.mean(hidden * hidden, axis=1, keepdims=True)

    slots = jnp.arange(requests, dtype=jnp.int32)
    source = state_perm // requests
    rank = jnp.sum(
        ((source[None, :] == source[:, None]) & (slots[None, :] < slots[:, None])).astype(jnp.int32),
        axis=1,
    )
    place = (source ^ r) * sends + rank
    natural = source * sends + rank
    slot_of = jnp.sum(jnp.where(natural[None, :] == slots[:, None], slots[None, :], 0), axis=1)
    mine = jnp.sum(
        jnp.where(
            place[None, :] == (jnp.arange(group, dtype=jnp.int32) * n_head + h)[:, None],
            slots[None, :],
            0,
        ),
        axis=1,
    )
    tenant = jnp.sum(
        ((mine + r * requests)[:, None] >= tenant_bounds[None, 1:-1]).astype(jnp.int32), axis=1
    )
    tenant_rows = sum(
        jnp.where((tenant == t)[:, None], gains[1 + t][None, :], 0.0)
        for t in range(tenant_gain.shape[0])
    )
    token_gain = jnp.repeat(tenant_rows * gains[0][None, :], steps, axis=0)
    final = (hidden * lax.rsqrt(mean_square + epsilon) * token_gain).astype(BF16)

    final = jnp.stack([final, swap(final, "head", n_head, 2)])
    arrived_kv = to_all(after(kv, final).reshape(n, -1, width), "req")
    full = lax.all_gather(final, "req", axis=0, tiled=True).reshape(n * 2 * rows, D)
    new_states = update_states(
        slot_of, arrived_kv.reshape(requests, 2 * steps, width).astype(F32), arrived, steps
    )
    best = greatest_entries(n, full, vocab_weight.T, vocab_other)
    got = jnp.max(to_all(best, "req"), axis=0)
    got = lax.all_gather(got, "head", axis=0).reshape(n_head, 2, rows)
    crossed = jnp.stack([got[i ^ 2, 1] for i in range(n_head)])
    best = jnp.maximum(got[:, 0], crossed).reshape(requests, steps)
    index = (place % n_head) * group + place // n_head
    match = (index[:, None] == slots[None, :])[:, :, None]
    best = jnp.sum(jnp.where(match, best[None], 0.0), axis=1)
    live = jnp.arange(steps)[None, :] < token_count[:, None]
    greatest = jnp.max(jnp.where(live, best, -1e30), axis=1)

    blocks = hidden.reshape(rows, n_head, width).transpose(1, 0, 2)
    tail = jnp.broadcast_to(mean_square, (rows, 128))
    whole = []
    for e in range(n_head):
        block = lax.dynamic_index_in_dim(blocks, h ^ e, 0, keepdims=False)
        block = jnp.concatenate([block, tail], axis=1)
        whole.append(block if e == 0 else swap(block, "head", n_head, e))
    whole = jnp.stack(whole).reshape(requests, steps, width + 128)
    index = ((place % n_head) ^ h) * group + place // n_head
    whole = jnp.take(whole, index, axis=0, mode="clip")
    last = jnp.arange(steps)[None, :] == (token_count - 1)[:, None]
    last_norm = jnp.sqrt(jnp.sum(jnp.where(last, whole[:, :, width], 0.0), axis=1) + epsilon)

    return whole[:, :, :width], new_states, last_norm, greatest


def solution(mesh):
    placed = (
        P("req", None),
        P("req"),
        P("req"),
        P(),
        P("req", "head", None, None),
        P("req", "head"),
        P(),
        P(None, "head"),
        P(None, "head"),
        P(None, "head"),
        P("head"),
        P("head"),
        P("head", None),
        P(),
        P("head", "req"),
        P("head", "req"),
        P("req", "head"),
        P("head"),
        P(None, "head"),
        P(None, ("req", "head")),
    )
    return jax.shard_map(
        on_device,
        mesh=mesh,
        in_specs=placed,
        out_specs=(P("req", None, "head"), P("req", "head", None, None), P("req"), P("req")),
        check_vma=False,
    )
```

```python
import functools

import jax
import jax.numpy as jnp
import numpy as np
from jax import lax
from jax.experimental import pallas as pl
from jax.experimental.pallas import tpu as pltpu
from jax.sharding import PartitionSpec as P

D = 2048
HEAD_DIM = 128
epsilon = 1e-06
F32 = jnp.float32
BF16 = jnp.bfloat16
VMEM = pltpu.VMEM
SMEM = pltpu.SMEM


def swap(x, axis, size, offset):
    return lax.ppermute(x, axis, [(i, i ^ offset) for i in range(size)])


def bf16_parts(x):
    high = lax.reduce_precision(x, 8, 7)
    return high.astype(BF16), (x - high).astype(BF16)


def sort_kernel(sends, order_ref, old_ref, *rest):
    outs, (held, in_sems, out_sems) = rest[:-3], rest[-3:]
    owners = held.shape[0]
    spans, first = [], 0
    for out in outs:
        spans.append((first, out.shape[1]))
        first += out.shape[1]

    def load(owner, rank):
        at = owner * sends + rank
        return pltpu.make_async_copy(
            old_ref.at[order_ref[at]], held.at[owner, rank], in_sems.at[owner, rank]
        )

    def store(part):
        first, count = spans[part]
        return pltpu.make_async_copy(
            held.at[:, pl.ds(first, count)], outs[part], out_sems.at[part]
        )

    for first, count in spans:
        for owner in range(owners):
            for rank in range(first, first + count):
                load(owner, rank).start()
    for part, (first, count) in enumerate(spans):
        for owner in range(owners):
            for rank in range(first, first + count):
                load(owner, rank).wait()
        store(part).start()
    for part in range(len(outs)):
        store(part).wait()


def sort_states(order, old_states, owners, counts):
    sends = sum(counts)
    state = old_states.shape[1:]
    return pl.pallas_call(
        functools.partial(sort_kernel, sends),
        out_shape=[
            jax.ShapeDtypeStruct((owners, count) + state, old_states.dtype) for count in counts
        ],
        in_specs=[pl.BlockSpec(memory_space=SMEM), pl.BlockSpec(memory_space=pl.ANY)],
        out_specs=[pl.BlockSpec(memory_space=pl.ANY)] * len(counts),
        scratch_shapes=[
            VMEM((owners, sends) + state, old_states.dtype),
            pltpu.SemaphoreType.DMA((owners, sends)),
            pltpu.SemaphoreType.DMA((len(counts),)),
        ],
        compiler_params=pltpu.CompilerParams(vmem_limit_bytes=56 << 20),
    )(order, old_states)


def hand_on(*refs):
    pass


def after(x, *others):
    anywhere = pl.BlockSpec(memory_space=pl.ANY)
    return pl.pallas_call(
        hand_on,
        out_shape=jax.ShapeDtypeStruct(x.shape, x.dtype),
        in_specs=[anywhere] * (1 + len(others)),
        out_specs=anywhere,
        input_output_aliases={0: 0},
    )(x, *others)


def roll(x, by):
    return pltpu.roll(x, by % x.shape[0], 0)


def mixer_kernel(
    counts, owners, heads, classes, steps,
    me_ref, emb_ref, live_ref, gain_ref, floor_ref, ggain_ref, qw_hbm, fw_hbm, iw_hbm, ow_hbm,
    *rest,
):
    pieces, sends = len(counts), sum(counts)
    states_hbm = rest[:pieces]
    own_ref, kv_ref = rest[pieces : pieces + 2]
    parts = rest[pieces + 2 : pieces + 2 + classes]
    (qw_ref, fw_ref, iw_ref, ow_ref, states, qhi_ref, qlo_ref, mixed_ref, part_ref, sems) = rest[
        pieces + 2 + classes :
    ]
    weight_pairs = ((qw_hbm, qw_ref), (fw_hbm, fw_ref), (iw_hbm, iw_ref), (ow_hbm, ow_ref))
    loads = [
        pltpu.make_async_copy(there, here, sems.at[i]) for i, (there, here) in enumerate(weight_pairs)
    ]
    state_loads = [
        pltpu.make_async_copy(
            states_hbm[i], states.at[:, pl.ds(sum(counts[:i]), counts[i])], sems.at[4 + i]
        )
        for i in range(pieces)
    ]
    for load in loads[:3] + state_loads + loads[3:]:
        load.start()
    tokens = live_ref.shape[0]
    requests = tokens // steps
    group = requests // classes
    rows = group * steps
    stream = emb_ref[0:tokens, :].astype(F32)
    scale = lax.rsqrt(jnp.mean(stream * stream, axis=1, keepdims=True) + epsilon)
    normed = (stream * scale * gain_ref[...]).astype(BF16)
    loads[0].wait()
    query = jnp.dot(normed, qw_ref[...], preferred_element_type=F32)
    query = query * jax.nn.sigmoid(query) * HEAD_DIM ** (-0.5)
    loads[1].wait()
    forget_raw = jnp.dot(normed, fw_ref[...], preferred_element_type=F32)
    loads[2].wait()
    value = jnp.dot(normed, iw_ref[...], preferred_element_type=F32)
    floor = floor_ref[...]
    forget = jnp.where(
        live_ref[...] > 0.0, floor + (1.0 - floor) * jax.nn.sigmoid(forget_raw), 1.0
    )
    key = 1.0 - forget
    step = lax.broadcasted_iota(jnp.int32, forget.shape, 0) % steps
    upto = forget * jnp.where(step >= 1, roll(forget, 1), 1.0)
    upto = upto * jnp.where(step >= 2, roll(upto, 2), 1.0)
    after = jnp.where(step <= steps - 2, roll(forget, -1), 1.0)
    after = after * jnp.where(step <= steps - 3, roll(forget, -2), 1.0)
    after = after * jnp.where(step <= steps - 4, roll(forget, -3), 1.0)
    carried = query * upto
    high = carried.astype(BF16).astype(F32)
    qhi_ref[...] = high
    qlo_ref[...] = carried - high
    lag_key, lag_value = key, value
    local = [jnp.zeros((tokens, HEAD_DIM), F32) for _ in range(heads)]
    for lag in range(steps):
        if lag:
            lag_key = roll(lag_key, 1) * forget
            lag_value = roll(lag_value, 1)
        product = jnp.where(step >= lag, query * lag_key, 0.0)
        for head in range(heads):
            cols = slice(head * HEAD_DIM, (head + 1) * HEAD_DIM)
            weight = jnp.sum(product[:, cols], axis=1, keepdims=True)
            local[head] = local[head] + weight * lag_value[:, cols]
    for head in range(heads):
        mixed_ref[:, head * HEAD_DIM : (head + 1) * HEAD_DIM] = local[head]
    for load in state_loads:
        load.wait()
    here = me_ref[0]
    upper = lax.broadcasted_iota(jnp.int32, (8, HEAD_DIM), 0) < steps
    for tile in range(tokens // 8):
        for head in range(heads):
            cols = slice(head * HEAD_DIM, (head + 1) * HEAD_DIM)
            at = slice(tile * 8, tile * 8 + 8)
            left = jnp.concatenate([qhi_ref[at, cols], qlo_ref[at, cols]], axis=0).astype(BF16)
            got = []
            for request in (2 * tile, 2 * tile + 1):
                place = (request % group) * classes + request // group
                old = states[here ^ (place // sends), place % sends, head]
                product = jnp.dot(left, old, preferred_element_type=F32)
                got.append(product[0:8] + product[8:16])
            mixed_ref[at, cols] += jnp.where(upper, got[0], got[1])
    mixed = mixed_ref[...]
    square = jnp.sum(mixed * mixed, axis=1, keepdims=True)
    loads[3].wait()
    part_ref[:, 0:D] = jnp.dot(
        (mixed * ggain_ref[...]).astype(BF16), ow_ref[...], preferred_element_type=F32
    )
    square_high = square.astype(BF16).astype(F32)
    lane = lax.broadcasted_iota(jnp.int32, (tokens, 128), 1)
    part_ref[:, D : D + 128] = jnp.where(lane < 64, square_high, square - square_high)
    for e in range(classes):
        first = pl.multiple_of((me_ref[1] ^ e) * rows, rows)
        parts[e][...] = part_ref[pl.ds(first, rows), :].astype(BF16)
    own_ref[...] = emb_ref[pl.ds(pl.multiple_of(me_ref[1] * rows, rows), rows), :]
    both = jnp.concatenate([(key * after).astype(BF16), value.astype(BF16)], axis=0)
    shape = (2 * tokens, 2 * tokens)
    target = lax.broadcasted_iota(jnp.int32, shape, 0)
    source = lax.broadcasted_iota(jnp.int32, shape, 1)
    slot, within = target // (2 * steps), target % (2 * steps)
    place = ((slot // sends) ^ here) * sends + slot % sends
    request = (place % classes) * group + place // classes
    wanted = request * steps + within % steps + jnp.where(within >= steps, tokens, 0)
    pick = jnp.where(source == wanted, 1.0, 0.0).astype(BF16)
    kv_ref[...] = jnp.dot(pick, both, preferred_element_type=F32).astype(BF16)


def mixer(me, emb, live, gain, floor, ggain, weights, states, steps, classes):
    tokens = live.shape[0]
    counts = tuple(piece.shape[1] for piece in states)
    owners, _, heads = states[0].shape[:3]
    width = floor.shape[1]
    rows = tokens // classes
    vmem, anywhere = pl.BlockSpec(memory_space=VMEM), pl.BlockSpec(memory_space=pl.ANY)
    return pl.pallas_call(
        functools.partial(mixer_kernel, counts, owners, heads, classes, steps),
        out_shape=[
            jax.ShapeDtypeStruct((rows, D), BF16),
            jax.ShapeDtypeStruct((2 * tokens, width), BF16),
        ]
        + [jax.ShapeDtypeStruct((rows, D + 128), BF16)] * classes,
        in_specs=[pl.BlockSpec(memory_space=SMEM)] + [vmem] * 5 + [anywhere] * (4 + len(states)),
        out_specs=[vmem] * (2 + classes),
        scratch_shapes=[VMEM(w.shape, BF16) for w in weights]
        + [
            VMEM((owners, sum(counts)) + states[0].shape[2:], BF16),
            VMEM((tokens, width), F32),
            VMEM((tokens, width), F32),
            VMEM((tokens, width), F32),
            VMEM((tokens, D + 128), F32),
            pltpu.SemaphoreType.DMA((4 + len(states),)),
        ],
        compiler_params=pltpu.CompilerParams(vmem_limit_bytes=56 << 20),
    )(me, emb, live, gain, floor, ggain, *weights, *states)


def update_kernel(steps, slot_ref, kv_ref, *rest):
    states, out_ref = rest[:-1], rest[-1]
    owners, _, heads = states[0].shape[:3]
    ranks = [(piece, i) for piece in states for i in range(piece.shape[1])]
    sends = len(ranks)
    diagonal = lax.broadcasted_iota(jnp.int32, (HEAD_DIM, HEAD_DIM), 0) == lax.broadcasted_iota(
        jnp.int32, (HEAD_DIM, HEAD_DIM), 1
    )
    first = lax.broadcasted_iota(jnp.int32, (2 * steps, HEAD_DIM), 0) < steps
    for k in range(owners):
        for rank, (piece, i) in enumerate(ranks):
            place = k * sends + rank
            slot = slot_ref[place]
            for head in range(heads):
                cols = slice(head * HEAD_DIM, (head + 1) * HEAD_DIM)
                both = kv_ref[place, :, cols]
                key = jnp.where(first, both, 0.0)
                value = jnp.where(first, roll(both, steps), 0.0)
                kept = 1.0 - jnp.sum(key, axis=0, keepdims=True)
                keep = jnp.where(diagonal, kept, 0.0).astype(BF16)
                fresh = lax.dot_general(
                    key, value, (((0,), (0,)), ((), ())), preferred_element_type=F32
                )
                old = jnp.dot(keep, piece[k, i, head], preferred_element_type=F32)
                out_ref[slot, head] = (old + fresh).astype(BF16)


def update_states(slots, kv, states, steps):
    vmem = pl.BlockSpec(memory_space=VMEM)
    return pl.pallas_call(
        functools.partial(update_kernel, steps),
        out_shape=jax.ShapeDtypeStruct((slots.shape[0],) + states[0].shape[2:], BF16),
        in_specs=[pl.BlockSpec(memory_space=SMEM)] + [vmem] * (1 + len(states)),
        out_specs=vmem,
        compiler_params=pltpu.CompilerParams(vmem_limit_bytes=56 << 20),
    )(slots, kv, *states)


def dot_rows(a, b):
    return lax.dot_general(a, b, (((1,), (1,)), ((), ())), preferred_element_type=F32)


def feed_kernel(
    x_hbm, weights_hbm, pick_ref, mine_ref, gain_ref, down_ref, kept_ref, x, weights, feed, act, sems
):
    blocks, height, depth = weights.shape
    units = height // 3
    loads = [pltpu.make_async_copy(x_hbm, x, sems.at[3])]
    for i in range(3):
        span = pl.ds(i * units, units)
        loads.append(
            pltpu.make_async_copy(weights_hbm.at[:, span], weights.at[:, span], sems.at[i])
        )
    for load in loads:
        load.start()
    loads[0].wait()
    stream = x[...].astype(F32)
    scale = lax.rsqrt(jnp.mean(stream * stream, axis=1, keepdims=True) + epsilon)
    feed[...] = (stream * scale * gain_ref[...]).astype(BF16)
    kept_ref[...] = jnp.dot(mine_ref[...], x[...], preferred_element_type=F32).astype(BF16)
    loads[1].wait()
    loads[2].wait()
    for first in range(0, units, 256):
        last = min(first + 256, units)
        gate = up = 0.0
        for b in range(blocks):
            part = feed[:, b * depth : (b + 1) * depth]
            gate += dot_rows(part, weights[b, first:last, :])
            up += dot_rows(part, weights[b, units + first : units + last, :])
        act[:, first:last] = (gate * jax.nn.sigmoid(gate) * up).astype(BF16)
    placed = jnp.dot(pick_ref[...], act[...], preferred_element_type=F32).astype(BF16)
    loads[3].wait()
    for b in range(blocks):
        down_ref[:, b * depth : (b + 1) * depth] = jnp.dot(
            placed, weights[b, 2 * units :, :], preferred_element_type=F32
        ).astype(BF16)


def feed_forward(x, weights, pick, mine, gain):
    vmem, anywhere = pl.BlockSpec(memory_space=VMEM), pl.BlockSpec(memory_space=pl.ANY)
    tokens, width = x.shape
    return pl.pallas_call(
        feed_kernel,
        out_shape=[
            jax.ShapeDtypeStruct((tokens, width), BF16),
            jax.ShapeDtypeStruct((mine.shape[0], width), BF16),
        ],
        in_specs=[anywhere] * 2 + [vmem] * 3,
        out_specs=[vmem] * 2,
        scratch_shapes=[
            VMEM(x.shape, BF16),
            VMEM(weights.shape, BF16),
            VMEM(x.shape, BF16),
            VMEM((tokens, weights.shape[1] // 3), BF16),
            pltpu.SemaphoreType.DMA((4,)),
        ],
        compiler_params=pltpu.CompilerParams(vmem_limit_bytes=58 << 20),
    )(x, weights, pick, mine, gain)


def greatest_kernel(full_hbm, own_hbm, other_hbm, best_ref, full, own, other, sems):
    loads = [
        pltpu.make_async_copy(there, here, sems.at[i])
        for i, (there, here) in enumerate(((full_hbm, full), (own_hbm, own), (other_hbm, other)))
    ]
    for load in loads:
        load.start()
    loads[0].wait()
    best = None
    for i, table in enumerate((own, other)):
        loads[1 + i].wait()
        height = table.shape[0]
        for first in range(0, height, 256):
            entries = dot_rows(table[first : min(first + 256, height), :], full[...])
            top = jnp.max(entries, axis=0, keepdims=True)
            best = top if best is None else jnp.maximum(best, top)
    width = best_ref.shape[1]
    for k in range(best_ref.shape[0]):
        best_ref[k : k + 1, :] = best[:, k * width : (k + 1) * width]


def greatest_entries(blocks, full, own, other):
    anywhere = pl.BlockSpec(memory_space=pl.ANY)
    return pl.pallas_call(
        greatest_kernel,
        out_shape=jax.ShapeDtypeStruct((blocks, full.shape[0] // blocks), F32),
        in_specs=[anywhere] * 3,
        out_specs=pl.BlockSpec(memory_space=VMEM),
        scratch_shapes=[VMEM(x.shape, BF16) for x in (full, own, other)]
        + [pltpu.SemaphoreType.DMA((3,))],
        compiler_params=pltpu.CompilerParams(vmem_limit_bytes=58 << 20),
    )(full, own, other)


def in_order(own, other, r):
    even = r % 2 == 0
    return jnp.stack([jnp.where(even, own, other), jnp.where(even, other, own)])


def gather_outer(x, n):
    groups = [list(range(first, n, 2)) for first in (0, 1)]
    return lax.all_gather(x, "req", axis=0, tiled=True, axis_index_groups=groups)


def to_all(x, axis):
    return lax.all_to_all(x, axis, split_axis=0, concat_axis=0, tiled=True)


def on_device(
    token_ids, state_perm, token_count, tenant_bounds, old_states, embedding, mixer_gain,
    query_weight, forget_weight, input_weight, forget_floor, group_gain, output_weight, feed_gain,
    gate_weight, up_weight, down_weight, final_gain, tenant_gain, vocab_weight,
):
    requests, steps = token_ids.shape
    n = lax.axis_size("req")
    n_head = lax.axis_size("head")
    r = lax.axis_index("req")
    h = lax.axis_index("head")
    tokens = requests * steps
    everyone = requests * n
    sends = requests // n
    group = requests // n_head
    rows = group * steps
    width = D // n_head

    feed_weights = jnp.concatenate([gate_weight.T, up_weight.T, down_weight], axis=0)
    feed_weights = lax.all_gather(feed_weights, "head", axis=0)

    packed = jnp.concatenate([token_ids.T, state_perm[None], token_count[None]], axis=0)
    packed = to_all(jnp.broadcast_to(packed[None], (n,) + packed.shape), "req").transpose(1, 0, 2).reshape(steps + 2, everyone)
    every = jnp.arange(everyone, dtype=jnp.int32)
    source = packed[steps] // requests
    rank = jnp.sum(
        ((source[None, :] == source[:, None]) & (every[None, :] < every[:, None])).astype(jnp.int32),
        axis=1,
    )
    place = ((every // requests) ^ source) * sends + rank % sends
    at = source * requests + (place % n_head) * group + place // n_head
    chosen = (at[:, None] == every[None, :]).astype(F32)
    ordered = jnp.dot(packed.astype(F32), chosen, precision=lax.Precision.HIGHEST)
    ordered = (ordered + 0.5).astype(jnp.int32)

    ids = ordered[:steps].T.reshape(n, tokens)
    table = embedding.shape[0]
    room = tokens // 2
    holder = lax.div(ids, jnp.int32(table))
    held = holder == r
    earlier = jnp.triu(jnp.ones((tokens, tokens), BF16), 1)
    turn = jnp.dot(held.astype(BF16), earlier, preferred_element_type=F32).astype(jnp.int32)
    local_ids = jnp.where(held, ids - r * table, 0)
    seat = held[:, None] & (turn[:, None] == jnp.arange(room, dtype=jnp.int32)[None, :, None])
    wanted = jnp.sum(jnp.where(seat, local_ids[:, None], 0), axis=2).reshape(n * room)
    got = to_all(jnp.take(embedding, wanted, axis=0, mode="clip").reshape(n, room, width), "req")
    own_holder = lax.dynamic_index_in_dim(holder, r, 0, keepdims=False)
    order = jnp.arange(tokens, dtype=jnp.int32)
    own_turn = jnp.sum(
        ((own_holder[None, :] == own_holder[:, None]) & (order[None, :] < order[:, None])).astype(
            jnp.int32
        ),
        axis=1,
    )
    seat = jnp.where(own_turn < room, own_holder * room + own_turn, -1)
    pick = (seat[:, None] == jnp.arange(n * room, dtype=jnp.int32)[None, :]).astype(BF16)
    embed_part = jnp.dot(
        pick, got.reshape(n * room, width), preferred_element_type=F32
    ).astype(BF16)
    owners = jnp.arange(n, dtype=jnp.int32)
    load = jnp.sum((holder[:, None] == owners[None, :, None]).astype(jnp.int32), axis=2)

    def with_rest(part):
        rows = jnp.take(embedding, local_ids.reshape(n * tokens), axis=0, mode="clip")
        rest = (held & (turn >= room)).reshape(n * tokens, 1)
        rows = jnp.where(rest, rows, jnp.zeros((), BF16)).reshape(n, tokens, width)
        return (part.astype(F32) + jnp.sum(to_all(rows, "req").astype(F32), axis=0)).astype(BF16)

    embed_part = lax.cond(jnp.max(load) > room, with_rest, lambda part: part, embed_part)
    vocab_other = swap(vocab_weight.T, "head", n_head, 1)

    gains = jnp.concatenate([final_gain[None], tenant_gain], axis=0)
    gains_high, gains_low = bf16_parts(gains)
    extra = jnp.zeros((16 - 2 * gains.shape[0], width), BF16)
    embedded = lax.all_gather(
        jnp.concatenate([embed_part, gains_high, gains_low, extra], axis=0), "head", axis=1, tiled=True
    )
    gains = embedded[tokens : tokens + 5].astype(F32) + embedded[tokens + 5 : tokens + 10].astype(F32)

    ordered = lax.dynamic_slice_in_dim(ordered, r * requests, requests, 1)
    old_order = (ordered[steps] - r * requests).reshape(n_head, group).T.reshape(n, sends)
    old_order = jnp.take(old_order, jnp.arange(n) ^ r, axis=0).reshape(requests)
    counts = (2, 2) if sends == 4 else (sends,)
    pieces = sort_states(old_order, old_states, n, counts)
    live = (jnp.arange(steps)[None, :] < ordered[steps + 1][:, None]).astype(F32)
    own, kv, *parts = mixer(
        jnp.stack([r, h]), embedded, live.reshape(tokens, 1), mixer_gain[None], forget_floor[None],
        group_gain[None], (query_weight, forget_weight, input_weight, output_weight), pieces,
        steps, n_head,
    )
    arrived = [to_all(pieces[0], "req")]

    total = parts[0].astype(F32)
    for e in range(1, n_head):
        total = total + swap(parts[e], "head", n_head, e).astype(F32)
    square = total[:, D : D + 1] + total[:, D + 127 : D + 128]
    after_mixer = own.astype(F32) + total[:, :D] * lax.rsqrt(square / D + epsilon)
    after_mixer = after(after_mixer.astype(BF16), feed_weights)
    pair = in_order(after_mixer, swap(after_mixer, "req", n, 1), r)
    everything = gather_outer(pair.reshape(2 * rows, D), n)
    for piece in pieces[1:]:
        arrived += [to_all(after(piece, after_mixer[:8, :128]), "req")]

    row = jnp.arange(n * rows, dtype=jnp.int32)
    by_owner, by_group, by_step = row // rows, (row % rows) // steps, row % steps
    if sends % n_head == 0:
        offset = by_group * n_head // sends
    else:
        offset = (by_group * n_head + h) // sends
    wanted = (by_owner ^ offset) * rows + by_group * steps + by_step
    pick = (wanted[None, :] == row[:, None]).astype(BF16)
    mine = (wanted[None, :] == (r * rows + row[:rows])[:, None]).astype(BF16)
    down, kept = feed_forward(everything, feed_weights, pick, mine, feed_gain[None])
    down = after(down, *arrived)
    hidden = kept.astype(F32) + jnp.sum(to_all(down.reshape(n, rows, D), "req").astype(F32), axis=0)
    mean_square = jnp.mean(hidden * hidden, axis=1, keepdims=True)

    slots = jnp.arange(requests, dtype=jnp.int32)
    source = state_perm // requests
    rank = jnp.sum(
        ((source[None, :] == source[:, None]) & (slots[None, :] < slots[:, None])).astype(jnp.int32),
        axis=1,
    )
    place = (source ^ r) * sends + rank
    natural = source * sends + rank
    slot_of = jnp.sum(jnp.where(natural[None, :] == slots[:, None], slots[None, :], 0), axis=1)
    mine = jnp.sum(
        jnp.where(
            place[None, :] == (jnp.arange(group, dtype=jnp.int32) * n_head + h)[:, None],
            slots[None, :],
            0,
        ),
        axis=1,
    )
    tenant = jnp.sum(
        ((mine + r * requests)[:, None] >= tenant_bounds[None, 1:-1]).astype(jnp.int32), axis=1
    )
    tenant_rows = sum(
        jnp.where((tenant == t)[:, None], gains[1 + t][None, :], 0.0)
        for t in range(tenant_gain.shape[0])
    )
    token_gain = jnp.repeat(tenant_rows * gains[0][None, :], steps, axis=0)
    final = (hidden * lax.rsqrt(mean_square + epsilon) * token_gain).astype(BF16)

    both = [(i * n_head + j, (i ^ 1) * n_head + (j ^ 2)) for i in range(n) for j in range(n_head)]
    here = jnp.stack([final, swap(final, "head", n_head, 2)])
    there = jnp.stack([swap(final, "req", n, 1), lax.ppermute(final, ("req", "head"), both)])
    pair = in_order(here, there, r)
    arrived_kv = to_all(after(kv, final).reshape(n, -1, width), "req")
    full = gather_outer(pair, n).reshape(n * 2 * rows, D)
    new_states = update_states(
        slot_of, arrived_kv.reshape(requests, 2 * steps, width).astype(F32), arrived, steps
    )
    best = greatest_entries(n, full, vocab_weight.T, vocab_other)
    got = jnp.max(to_all(best, "req"), axis=0)
    got = lax.all_gather(got, "head", axis=0).reshape(n_head, 2, rows)
    crossed = jnp.stack([got[i ^ 2, 1] for i in range(n_head)])
    best = jnp.maximum(got[:, 0], crossed).reshape(requests, steps)
    index = (place % n_head) * group + place // n_head
    match = (index[:, None] == slots[None, :])[:, :, None]
    best = jnp.sum(jnp.where(match, best[None], 0.0), axis=1)
    live = jnp.arange(steps)[None, :] < token_count[:, None]
    greatest = jnp.max(jnp.where(live, best, -1e30), axis=1)

    blocks = hidden.reshape(rows, n_head, width).transpose(1, 0, 2)
    tail = jnp.broadcast_to(mean_square, (rows, 128))
    whole = []
    for e in range(n_head):
        block = lax.dynamic_index_in_dim(blocks, h ^ e, 0, keepdims=False)
        block = jnp.concatenate([block, tail], axis=1)
        whole.append(block if e == 0 else swap(block, "head", n_head, e))
    whole = jnp.stack(whole).reshape(requests, steps, width + 128)
    index = ((place % n_head) ^ h) * group + place // n_head
    whole = jnp.take(whole, index, axis=0, mode="clip")
    last = jnp.arange(steps)[None, :] == (token_count - 1)[:, None]
    last_norm = jnp.sqrt(jnp.sum(jnp.where(last, whole[:, :, width], 0.0), axis=1) + epsilon)

    return whole[:, :, :width], new_states, last_norm, greatest


def solution(mesh):
    placed = (
        P("req", None),
        P("req"),
        P("req"),
        P(),
        P("req", "head", None, None),
        P("req", "head"),
        P(),
        P(None, "head"),
        P(None, "head"),
        P(None, "head"),
        P("head"),
        P("head"),
        P("head", None),
        P(),
        P("head", "req"),
        P("head", "req"),
        P("req", "head"),
        P("head"),
        P(None, "head"),
        P(None, ("req", "head")),
    )
    return jax.shard_map(
        on_device,
        mesh=mesh,
        in_specs=placed,
        out_specs=(P("req", None, "head"), P("req", "head", None, None), P("req"), P("req")),
        check_vma=False,
    )
```

```python
import functools

import jax
import jax.numpy as jnp
import numpy as np
from jax import lax
from jax.experimental import pallas as pl
from jax.experimental.pallas import tpu as pltpu
from jax.sharding import PartitionSpec as P

D = 2048
HEAD_DIM = 128
epsilon = 1e-06
F32 = jnp.float32
BF16 = jnp.bfloat16
VMEM = pltpu.VMEM
SMEM = pltpu.SMEM


def swap(x, axis, size, offset):
    return lax.ppermute(x, axis, [(i, i ^ offset) for i in range(size)])


def bf16_parts(x):
    high = lax.reduce_precision(x, 8, 7)
    return high.astype(BF16), (x - high).astype(BF16)


def sort_kernel(sends, order_ref, old_ref, *rest):
    outs, (held, in_sems, out_sems) = rest[:-3], rest[-3:]
    owners = held.shape[0]
    spans, first = [], 0
    for out in outs:
        spans.append((first, out.shape[1]))
        first += out.shape[1]

    def load(owner, rank):
        at = owner * sends + rank
        return pltpu.make_async_copy(
            old_ref.at[order_ref[at]], held.at[owner, rank], in_sems.at[owner, rank]
        )

    def store(part):
        first, count = spans[part]
        return pltpu.make_async_copy(
            held.at[:, pl.ds(first, count)], outs[part], out_sems.at[part]
        )

    for first, count in spans:
        for owner in range(owners):
            for rank in range(first, first + count):
                load(owner, rank).start()
    for part, (first, count) in enumerate(spans):
        for owner in range(owners):
            for rank in range(first, first + count):
                load(owner, rank).wait()
        store(part).start()
    for part in range(len(outs)):
        store(part).wait()


def sort_states(order, old_states, owners, counts):
    sends = sum(counts)
    state = old_states.shape[1:]
    return pl.pallas_call(
        functools.partial(sort_kernel, sends),
        out_shape=[
            jax.ShapeDtypeStruct((owners, count) + state, old_states.dtype) for count in counts
        ],
        in_specs=[pl.BlockSpec(memory_space=SMEM), pl.BlockSpec(memory_space=pl.ANY)],
        out_specs=[pl.BlockSpec(memory_space=pl.ANY)] * len(counts),
        scratch_shapes=[
            VMEM((owners, sends) + state, old_states.dtype),
            pltpu.SemaphoreType.DMA((owners, sends)),
            pltpu.SemaphoreType.DMA((len(counts),)),
        ],
        compiler_params=pltpu.CompilerParams(vmem_limit_bytes=56 << 20),
    )(order, old_states)


def hand_on(*refs):
    pass


def after(x, *others):
    anywhere = pl.BlockSpec(memory_space=pl.ANY)
    return pl.pallas_call(
        hand_on,
        out_shape=jax.ShapeDtypeStruct(x.shape, x.dtype),
        in_specs=[anywhere] * (1 + len(others)),
        out_specs=anywhere,
        input_output_aliases={0: 0},
    )(x, *others)


def roll(x, by):
    return pltpu.roll(x, by % x.shape[0], 0)


def mixer_kernel(
    counts, owners, heads, classes, steps,
    me_ref, emb_ref, live_ref, gain_ref, floor_ref, ggain_ref, qw_hbm, fw_hbm, iw_hbm, ow_hbm,
    *rest,
):
    pieces, sends = len(counts), sum(counts)
    states_hbm = rest[:pieces]
    own_ref, kv_ref = rest[pieces : pieces + 2]
    parts = rest[pieces + 2 : pieces + 2 + classes]
    (qw_ref, fw_ref, iw_ref, ow_ref, states, qhi_ref, qlo_ref, mixed_ref, part_ref, sems) = rest[
        pieces + 2 + classes :
    ]
    weight_pairs = ((qw_hbm, qw_ref), (fw_hbm, fw_ref), (iw_hbm, iw_ref), (ow_hbm, ow_ref))
    loads = [
        pltpu.make_async_copy(there, here, sems.at[i]) for i, (there, here) in enumerate(weight_pairs)
    ]
    state_loads = [
        pltpu.make_async_copy(
            states_hbm[i], states.at[:, pl.ds(sum(counts[:i]), counts[i])], sems.at[4 + i]
        )
        for i in range(pieces)
    ]
    for load in loads[:3] + state_loads + loads[3:]:
        load.start()
    tokens = live_ref.shape[0]
    requests = tokens // steps
    group = requests // classes
    rows = group * steps
    stream = emb_ref[0:tokens, :].astype(F32)
    scale = lax.rsqrt(jnp.mean(stream * stream, axis=1, keepdims=True) + epsilon)
    normed = (stream * scale * gain_ref[...]).astype(BF16)
    loads[0].wait()
    query = jnp.dot(normed, qw_ref[...], preferred_element_type=F32)
    query = query * jax.nn.sigmoid(query) * HEAD_DIM ** (-0.5)
    loads[1].wait()
    forget_raw = jnp.dot(normed, fw_ref[...], preferred_element_type=F32)
    loads[2].wait()
    value = jnp.dot(normed, iw_ref[...], preferred_element_type=F32)
    floor = floor_ref[...]
    forget = jnp.where(
        live_ref[...] > 0.0, floor + (1.0 - floor) * jax.nn.sigmoid(forget_raw), 1.0
    )
    key = 1.0 - forget
    step = lax.broadcasted_iota(jnp.int32, forget.shape, 0) % steps
    upto = forget * jnp.where(step >= 1, roll(forget, 1), 1.0)
    upto = upto * jnp.where(step >= 2, roll(upto, 2), 1.0)
    after = jnp.where(step <= steps - 2, roll(forget, -1), 1.0)
    after = after * jnp.where(step <= steps - 3, roll(forget, -2), 1.0)
    after = after * jnp.where(step <= steps - 4, roll(forget, -3), 1.0)
    carried = query * upto
    high = carried.astype(BF16).astype(F32)
    qhi_ref[...] = high
    qlo_ref[...] = carried - high
    lag_key, lag_value = key, value
    local = [jnp.zeros((tokens, HEAD_DIM), F32) for _ in range(heads)]
    for lag in range(steps):
        if lag:
            lag_key = roll(lag_key, 1) * forget
            lag_value = roll(lag_value, 1)
        product = jnp.where(step >= lag, query * lag_key, 0.0)
        for head in range(heads):
            cols = slice(head * HEAD_DIM, (head + 1) * HEAD_DIM)
            weight = jnp.sum(product[:, cols], axis=1, keepdims=True)
            local[head] = local[head] + weight * lag_value[:, cols]
    for head in range(heads):
        mixed_ref[:, head * HEAD_DIM : (head + 1) * HEAD_DIM] = local[head]
    for load in state_loads:
        load.wait()
    here = me_ref[0]
    upper = lax.broadcasted_iota(jnp.int32, (8, HEAD_DIM), 0) < steps
    for tile in range(tokens // 8):
        for head in range(heads):
            cols = slice(head * HEAD_DIM, (head + 1) * HEAD_DIM)
            at = slice(tile * 8, tile * 8 + 8)
            left = jnp.concatenate([qhi_ref[at, cols], qlo_ref[at, cols]], axis=0).astype(BF16)
            got = []
            for request in (2 * tile, 2 * tile + 1):
                place = (request % group) * classes + request // group
                old = states[here ^ (place // sends), place % sends, head]
                product = jnp.dot(left, old, preferred_element_type=F32)
                got.append(product[0:8] + product[8:16])
            mixed_ref[at, cols] += jnp.where(upper, got[0], got[1])
    mixed = mixed_ref[...]
    square = jnp.sum(mixed * mixed, axis=1, keepdims=True)
    loads[3].wait()
    part_ref[:, 0:D] = jnp.dot(
        (mixed * ggain_ref[...]).astype(BF16), ow_ref[...], preferred_element_type=F32
    )
    square_high = square.astype(BF16).astype(F32)
    lane = lax.broadcasted_iota(jnp.int32, (tokens, 128), 1)
    part_ref[:, D : D + 128] = jnp.where(lane < 64, square_high, square - square_high)
    for e in range(classes):
        first = pl.multiple_of((me_ref[1] ^ e) * rows, rows)
        parts[e][...] = part_ref[pl.ds(first, rows), :].astype(BF16)
    own_ref[...] = emb_ref[pl.ds(pl.multiple_of(me_ref[1] * rows, rows), rows), :]
    both = jnp.concatenate([(key * after).astype(BF16), value.astype(BF16)], axis=0)
    shape = (2 * tokens, 2 * tokens)
    target = lax.broadcasted_iota(jnp.int32, shape, 0)
    source = lax.broadcasted_iota(jnp.int32, shape, 1)
    slot, within = target // (2 * steps), target % (2 * steps)
    place = ((slot // sends) ^ here) * sends + slot % sends
    request = (place % classes) * group + place // classes
    wanted = request * steps + within % steps + jnp.where(within >= steps, tokens, 0)
    pick = jnp.where(source == wanted, 1.0, 0.0).astype(BF16)
    kv_ref[...] = jnp.dot(pick, both, preferred_element_type=F32).astype(BF16)


def mixer(me, emb, live, gain, floor, ggain, weights, states, steps, classes):
    tokens = live.shape[0]
    counts = tuple(piece.shape[1] for piece in states)
    owners, _, heads = states[0].shape[:3]
    width = floor.shape[1]
    rows = tokens // classes
    vmem, anywhere = pl.BlockSpec(memory_space=VMEM), pl.BlockSpec(memory_space=pl.ANY)
    return pl.pallas_call(
        functools.partial(mixer_kernel, counts, owners, heads, classes, steps),
        out_shape=[
            jax.ShapeDtypeStruct((rows, D), BF16),
            jax.ShapeDtypeStruct((2 * tokens, width), BF16),
        ]
        + [jax.ShapeDtypeStruct((rows, D + 128), BF16)] * classes,
        in_specs=[pl.BlockSpec(memory_space=SMEM)] + [vmem] * 5 + [anywhere] * (4 + len(states)),
        out_specs=[vmem] * (2 + classes),
        scratch_shapes=[VMEM(w.shape, BF16) for w in weights]
        + [
            VMEM((owners, sum(counts)) + states[0].shape[2:], BF16),
            VMEM((tokens, width), F32),
            VMEM((tokens, width), F32),
            VMEM((tokens, width), F32),
            VMEM((tokens, D + 128), F32),
            pltpu.SemaphoreType.DMA((4 + len(states),)),
        ],
        compiler_params=pltpu.CompilerParams(vmem_limit_bytes=56 << 20),
    )(me, emb, live, gain, floor, ggain, *weights, *states)


def update_kernel(steps, slot_ref, kv_ref, *rest):
    states, out_ref = rest[:-1], rest[-1]
    owners, _, heads = states[0].shape[:3]
    ranks = [(piece, i) for piece in states for i in range(piece.shape[1])]
    sends = len(ranks)
    diagonal = lax.broadcasted_iota(jnp.int32, (HEAD_DIM, HEAD_DIM), 0) == lax.broadcasted_iota(
        jnp.int32, (HEAD_DIM, HEAD_DIM), 1
    )
    first = lax.broadcasted_iota(jnp.int32, (2 * steps, HEAD_DIM), 0) < steps
    for k in range(owners):
        for rank, (piece, i) in enumerate(ranks):
            place = k * sends + rank
            slot = slot_ref[place]
            for head in range(heads):
                cols = slice(head * HEAD_DIM, (head + 1) * HEAD_DIM)
                both = kv_ref[place, :, cols]
                key = jnp.where(first, both, 0.0)
                value = jnp.where(first, roll(both, steps), 0.0)
                kept = 1.0 - jnp.sum(key, axis=0, keepdims=True)
                keep = jnp.where(diagonal, kept, 0.0).astype(BF16)
                fresh = lax.dot_general(
                    key, value, (((0,), (0,)), ((), ())), preferred_element_type=F32
                )
                old = jnp.dot(keep, piece[k, i, head], preferred_element_type=F32)
                out_ref[slot, head] = (old + fresh).astype(BF16)


def update_states(slots, kv, states, steps):
    vmem = pl.BlockSpec(memory_space=VMEM)
    return pl.pallas_call(
        functools.partial(update_kernel, steps),
        out_shape=jax.ShapeDtypeStruct((slots.shape[0],) + states[0].shape[2:], BF16),
        in_specs=[pl.BlockSpec(memory_space=SMEM)] + [vmem] * (1 + len(states)),
        out_specs=vmem,
        compiler_params=pltpu.CompilerParams(vmem_limit_bytes=56 << 20),
    )(slots, kv, *states)


def dot_rows(a, b):
    return lax.dot_general(a, b, (((1,), (1,)), ((), ())), preferred_element_type=F32)


def feed_kernel(
    x_hbm, weights_hbm, pick_ref, mine_ref, gain_ref, down_ref, kept_ref, x, weights, feed, act, sems
):
    blocks, height, depth = weights.shape
    units = height // 3
    loads = [pltpu.make_async_copy(x_hbm, x, sems.at[3])]
    for i in range(3):
        span = pl.ds(i * units, units)
        loads.append(
            pltpu.make_async_copy(weights_hbm.at[:, span], weights.at[:, span], sems.at[i])
        )
    for load in loads:
        load.start()
    loads[0].wait()
    stream = x[...].astype(F32)
    scale = lax.rsqrt(jnp.mean(stream * stream, axis=1, keepdims=True) + epsilon)
    feed[...] = (stream * scale * gain_ref[...]).astype(BF16)
    kept_ref[...] = jnp.dot(mine_ref[...], x[...], preferred_element_type=F32).astype(BF16)
    loads[1].wait()
    loads[2].wait()
    for first in range(0, units, 256):
        last = min(first + 256, units)
        gate = up = 0.0
        for b in range(blocks):
            part = feed[:, b * depth : (b + 1) * depth]
            gate += dot_rows(part, weights[b, first:last, :])
            up += dot_rows(part, weights[b, units + first : units + last, :])
        act[:, first:last] = (gate * jax.nn.sigmoid(gate) * up).astype(BF16)
    placed = jnp.dot(pick_ref[...], act[...], preferred_element_type=F32).astype(BF16)
    loads[3].wait()
    for b in range(blocks):
        down_ref[:, b * depth : (b + 1) * depth] = jnp.dot(
            placed, weights[b, 2 * units :, :], preferred_element_type=F32
        ).astype(BF16)


def feed_forward(x, weights, pick, mine, gain):
    vmem, anywhere = pl.BlockSpec(memory_space=VMEM), pl.BlockSpec(memory_space=pl.ANY)
    tokens, width = x.shape
    return pl.pallas_call(
        feed_kernel,
        out_shape=[
            jax.ShapeDtypeStruct((tokens, width), BF16),
            jax.ShapeDtypeStruct((mine.shape[0], width), BF16),
        ],
        in_specs=[anywhere] * 2 + [vmem] * 3,
        out_specs=[vmem] * 2,
        scratch_shapes=[
            VMEM(x.shape, BF16),
            VMEM(weights.shape, BF16),
            VMEM(x.shape, BF16),
            VMEM((tokens, weights.shape[1] // 3), BF16),
            pltpu.SemaphoreType.DMA((4,)),
        ],
        compiler_params=pltpu.CompilerParams(vmem_limit_bytes=58 << 20),
    )(x, weights, pick, mine, gain)


def greatest_kernel(full_hbm, own_hbm, other_hbm, best_ref, full, own, other, sems):
    loads = [
        pltpu.make_async_copy(there, here, sems.at[i])
        for i, (there, here) in enumerate(((full_hbm, full), (own_hbm, own), (other_hbm, other)))
    ]
    for load in loads:
        load.start()
    loads[0].wait()
    best = None
    for i, table in enumerate((own, other)):
        loads[1 + i].wait()
        height = table.shape[0]
        for first in range(0, height, 256):
            entries = dot_rows(table[first : min(first + 256, height), :], full[...])
            top = jnp.max(entries, axis=0, keepdims=True)
            best = top if best is None else jnp.maximum(best, top)
    width = best_ref.shape[1]
    for k in range(best_ref.shape[0]):
        best_ref[k : k + 1, :] = best[:, k * width : (k + 1) * width]


def greatest_entries(blocks, full, own, other):
    anywhere = pl.BlockSpec(memory_space=pl.ANY)
    return pl.pallas_call(
        greatest_kernel,
        out_shape=jax.ShapeDtypeStruct((blocks, full.shape[0] // blocks), F32),
        in_specs=[anywhere] * 3,
        out_specs=pl.BlockSpec(memory_space=VMEM),
        scratch_shapes=[VMEM(x.shape, BF16) for x in (full, own, other)]
        + [pltpu.SemaphoreType.DMA((3,))],
        compiler_params=pltpu.CompilerParams(vmem_limit_bytes=58 << 20),
    )(full, own, other)


def exchange(block, dim, n, n_head):
    if dim == "outer":
        got = [swap(block, "req", n, 2 * j) for j in range(1, n // 2)]
    elif dim == "inner":
        got = [swap(block, "req", n, 1)]
    else:
        got = [swap(block, "head", n_head, 2)]
    return jnp.stack([block] + got)


def gather_by(block, dims, n, n_head):
    rank = block.ndim
    for dim in dims:
        block = exchange(block, dim, n, n_head)
    at = [dims[::-1].index(dim) for dim in ("outer", "inner", "cross")]
    return block.transpose(at + list(range(len(dims), len(dims) + rank)))


def to_all(x, axis):
    return lax.all_to_all(x, axis, split_axis=0, concat_axis=0, tiled=True)


def on_device(
    token_ids, state_perm, token_count, tenant_bounds, old_states, embedding, mixer_gain,
    query_weight, forget_weight, input_weight, forget_floor, group_gain, output_weight, feed_gain,
    gate_weight, up_weight, down_weight, final_gain, tenant_gain, vocab_weight,
):
    requests, steps = token_ids.shape
    n = lax.axis_size("req")
    n_head = lax.axis_size("head")
    r = lax.axis_index("req")
    h = lax.axis_index("head")
    tokens = requests * steps
    everyone = requests * n
    sends = requests // n
    group = requests // n_head
    rows = group * steps
    width = D // n_head

    feed_weights = jnp.concatenate([gate_weight.T, up_weight.T, down_weight], axis=0)
    feed_weights = lax.all_gather(feed_weights, "head", axis=0)

    packed = jnp.concatenate([token_ids.T, state_perm[None], token_count[None]], axis=0)
    packed = to_all(jnp.broadcast_to(packed[None], (n,) + packed.shape), "req").transpose(1, 0, 2).reshape(steps + 2, everyone)
    every = jnp.arange(everyone, dtype=jnp.int32)
    source = packed[steps] // requests
    rank = jnp.sum(
        ((source[None, :] == source[:, None]) & (every[None, :] < every[:, None])).astype(jnp.int32),
        axis=1,
    )
    place = ((every // requests) ^ source) * sends + rank % sends
    at = source * requests + (place % n_head) * group + place // n_head
    chosen = (at[:, None] == every[None, :]).astype(F32)
    ordered = jnp.dot(packed.astype(F32), chosen, precision=lax.Precision.HIGHEST)
    ordered = (ordered + 0.5).astype(jnp.int32)

    ids = ordered[:steps].T.reshape(n, tokens)
    table = embedding.shape[0]
    room = tokens // 2
    holder = lax.div(ids, jnp.int32(table))
    held = holder == r
    earlier = jnp.triu(jnp.ones((tokens, tokens), BF16), 1)
    turn = jnp.dot(held.astype(BF16), earlier, preferred_element_type=F32).astype(jnp.int32)
    local_ids = jnp.where(held, ids - r * table, 0)
    seat = held[:, None] & (turn[:, None] == jnp.arange(room, dtype=jnp.int32)[None, :, None])
    wanted = jnp.sum(jnp.where(seat, local_ids[:, None], 0), axis=2).reshape(n * room)
    got = to_all(jnp.take(embedding, wanted, axis=0, mode="clip").reshape(n, room, width), "req")
    own_holder = lax.dynamic_index_in_dim(holder, r, 0, keepdims=False)
    order = jnp.arange(tokens, dtype=jnp.int32)
    own_turn = jnp.sum(
        ((own_holder[None, :] == own_holder[:, None]) & (order[None, :] < order[:, None])).astype(
            jnp.int32
        ),
        axis=1,
    )
    seat = jnp.where(own_turn < room, own_holder * room + own_turn, -1)
    pick = (seat[:, None] == jnp.arange(n * room, dtype=jnp.int32)[None, :]).astype(BF16)
    embed_part = jnp.dot(
        pick, got.reshape(n * room, width), preferred_element_type=F32
    ).astype(BF16)
    owners = jnp.arange(n, dtype=jnp.int32)
    load = jnp.sum((holder[:, None] == owners[None, :, None]).astype(jnp.int32), axis=2)

    def with_rest(part):
        rows = jnp.take(embedding, local_ids.reshape(n * tokens), axis=0, mode="clip")
        rest = (held & (turn >= room)).reshape(n * tokens, 1)
        rows = jnp.where(rest, rows, jnp.zeros((), BF16)).reshape(n, tokens, width)
        return (part.astype(F32) + jnp.sum(to_all(rows, "req").astype(F32), axis=0)).astype(BF16)

    embed_part = lax.cond(jnp.max(load) > room, with_rest, lambda part: part, embed_part)
    vocab_other = swap(vocab_weight.T, "head", n_head, 1)

    gains = jnp.concatenate([final_gain[None], tenant_gain], axis=0)
    gains_high, gains_low = bf16_parts(gains)
    extra = jnp.zeros((16 - 2 * gains.shape[0], width), BF16)
    embedded = lax.all_gather(
        jnp.concatenate([embed_part, gains_high, gains_low, extra], axis=0), "head", axis=1, tiled=True
    )
    gains = embedded[tokens : tokens + 5].astype(F32) + embedded[tokens + 5 : tokens + 10].astype(F32)

    ordered = lax.dynamic_slice_in_dim(ordered, r * requests, requests, 1)
    old_order = (ordered[steps] - r * requests).reshape(n_head, group).T.reshape(n, sends)
    old_order = jnp.take(old_order, jnp.arange(n) ^ r, axis=0).reshape(requests)
    counts = (2, 2) if sends == 4 else (sends,)
    pieces = sort_states(old_order, old_states, n, counts)
    live = (jnp.arange(steps)[None, :] < ordered[steps + 1][:, None]).astype(F32)
    own, kv, *parts = mixer(
        jnp.stack([r, h]), embedded, live.reshape(tokens, 1), mixer_gain[None], forget_floor[None],
        group_gain[None], (query_weight, forget_weight, input_weight, output_weight), pieces,
        steps, n_head,
    )
    arrived = [to_all(pieces[0], "req")]

    total = parts[0].astype(F32)
    for e in range(1, n_head):
        total = total + swap(parts[e], "head", n_head, e).astype(F32)
    square = total[:, D : D + 1] + total[:, D + 127 : D + 128]
    after_mixer = own.astype(F32) + total[:, :D] * lax.rsqrt(square / D + epsilon)
    after_mixer = after(after_mixer.astype(BF16), feed_weights)
    everything = lax.all_gather(after_mixer, "req", axis=0, tiled=True)
    arrived += [to_all(after(piece, after_mixer[:8, :128]), "req") for piece in pieces[1:]]
    arrived_kv = to_all(kv.reshape(n, -1, width), "req")

    row = jnp.arange(n * rows, dtype=jnp.int32)
    by_owner, by_group, by_step = row // rows, (row % rows) // steps, row % steps
    if sends % n_head == 0:
        offset = by_group * n_head // sends
    else:
        offset = (by_group * n_head + h) // sends
    wanted = (by_owner ^ offset) * rows + by_group * steps + by_step
    pick = (wanted[None, :] == row[:, None]).astype(BF16)
    mine = (wanted[None, :] == (r * rows + row[:rows])[:, None]).astype(BF16)
    down, kept = feed_forward(everything, feed_weights, pick, mine, feed_gain[None])
    down = after(down, arrived_kv, *arrived)
    hidden = kept.astype(F32) + jnp.sum(to_all(down.reshape(n, rows, D), "req").astype(F32), axis=0)
    mean_square = jnp.mean(hidden * hidden, axis=1, keepdims=True)

    slots = jnp.arange(requests, dtype=jnp.int32)
    source = state_perm // requests
    rank = jnp.sum(
        ((source[None, :] == source[:, None]) & (slots[None, :] < slots[:, None])).astype(jnp.int32),
        axis=1,
    )
    place = (source ^ r) * sends + rank
    natural = source * sends + rank
    slot_of = jnp.sum(jnp.where(natural[None, :] == slots[:, None], slots[None, :], 0), axis=1)
    mine = jnp.sum(
        jnp.where(
            place[None, :] == (jnp.arange(group, dtype=jnp.int32) * n_head + h)[:, None],
            slots[None, :],
            0,
        ),
        axis=1,
    )
    tenant = jnp.sum(
        ((mine + r * requests)[:, None] >= tenant_bounds[None, 1:-1]).astype(jnp.int32), axis=1
    )
    tenant_rows = sum(
        jnp.where((tenant == t)[:, None], gains[1 + t][None, :], 0.0)
        for t in range(tenant_gain.shape[0])
    )
    token_gain = jnp.repeat(tenant_rows * gains[0][None, :], steps, axis=0)
    final = (hidden * lax.rsqrt(mean_square + epsilon) * token_gain).astype(BF16)

    c1, c2 = D * 7 // 16, D * 13 // 16
    full = jnp.concatenate(
        [
            gather_by(final[:, :c1], ("outer", "inner", "cross"), n, n_head),
            gather_by(final[:, c1:c2], ("cross", "outer", "inner"), n, n_head),
            gather_by(final[:, c2:], ("inner", "cross", "outer"), n, n_head),
        ],
        axis=-1,
    ).reshape(n * 2 * rows, D)
    new_states = update_states(
        slot_of, arrived_kv.reshape(requests, 2 * steps, width).astype(F32), arrived, steps
    )
    best = greatest_entries(n, full, vocab_weight.T, vocab_other)
    best = jnp.take(best, jnp.arange(n) ^ r, axis=0)
    got = jnp.max(to_all(best, "req"), axis=0)
    got = lax.all_gather(got, "head", axis=0).reshape(n_head, 2, rows)
    crossed = jnp.stack([got[i ^ 2, 1] for i in range(n_head)])
    best = jnp.maximum(got[:, 0], crossed).reshape(requests, steps)
    index = (place % n_head) * group + place // n_head
    match = (index[:, None] == slots[None, :])[:, :, None]
    best = jnp.sum(jnp.where(match, best[None], 0.0), axis=1)
    live = jnp.arange(steps)[None, :] < token_count[:, None]
    greatest = jnp.max(jnp.where(live, best, -1e30), axis=1)

    blocks = hidden.reshape(rows, n_head, width).transpose(1, 0, 2)
    tail = jnp.broadcast_to(mean_square, (rows, 128))
    whole = []
    for e in range(n_head):
        block = lax.dynamic_index_in_dim(blocks, h ^ e, 0, keepdims=False)
        block = jnp.concatenate([block, tail], axis=1)
        whole.append(block if e == 0 else swap(block, "head", n_head, e))
    whole = jnp.stack(whole).reshape(requests, steps, width + 128)
    index = ((place % n_head) ^ h) * group + place // n_head
    whole = jnp.take(whole, index, axis=0, mode="clip")
    last = jnp.arange(steps)[None, :] == (token_count - 1)[:, None]
    last_norm = jnp.sqrt(jnp.sum(jnp.where(last, whole[:, :, width], 0.0), axis=1) + epsilon)

    return whole[:, :, :width], new_states, last_norm, greatest


def solution(mesh):
    placed = (
        P("req", None),
        P("req"),
        P("req"),
        P(),
        P("req", "head", None, None),
        P("req", "head"),
        P(),
        P(None, "head"),
        P(None, "head"),
        P(None, "head"),
        P("head"),
        P("head"),
        P("head", None),
        P(),
        P("head", "req"),
        P("head", "req"),
        P("req", "head"),
        P("head"),
        P(None, "head"),
        P(None, ("req", "head")),
    )
    return jax.shard_map(
        on_device,
        mesh=mesh,
        in_specs=placed,
        out_specs=(P("req", None, "head"), P("req", "head", None, None), P("req"), P("req")),
        check_vma=False,
    )
```

```python
import functools

import jax
import jax.numpy as jnp
import numpy as np
from jax import lax
from jax.experimental import pallas as pl
from jax.experimental.pallas import tpu as pltpu
from jax.sharding import PartitionSpec as P

D = 2048
HEAD_DIM = 128
epsilon = 1e-06
F32 = jnp.float32
BF16 = jnp.bfloat16
VMEM = pltpu.VMEM
SMEM = pltpu.SMEM


def swap(x, axis, size, offset):
    return lax.ppermute(x, axis, [(i, i ^ offset) for i in range(size)])


def bf16_parts(x):
    high = lax.reduce_precision(x, 8, 7)
    return high.astype(BF16), (x - high).astype(BF16)


def sort_kernel(sends, order_ref, old_ref, *rest):
    outs, (held, in_sems, out_sems) = rest[:-3], rest[-3:]
    owners = held.shape[0]
    spans, first = [], 0
    for out in outs:
        spans.append((first, out.shape[1]))
        first += out.shape[1]

    def load(owner, rank):
        at = owner * sends + rank
        return pltpu.make_async_copy(
            old_ref.at[order_ref[at]], held.at[owner, rank], in_sems.at[owner, rank]
        )

    def store(part):
        first, count = spans[part]
        return pltpu.make_async_copy(
            held.at[:, pl.ds(first, count)], outs[part], out_sems.at[part]
        )

    for first, count in spans:
        for owner in range(owners):
            for rank in range(first, first + count):
                load(owner, rank).start()
    for part, (first, count) in enumerate(spans):
        for owner in range(owners):
            for rank in range(first, first + count):
                load(owner, rank).wait()
        store(part).start()
    for part in range(len(outs)):
        store(part).wait()


def sort_states(order, old_states, owners, counts):
    sends = sum(counts)
    state = old_states.shape[1:]
    return pl.pallas_call(
        functools.partial(sort_kernel, sends),
        out_shape=[
            jax.ShapeDtypeStruct((owners, count) + state, old_states.dtype) for count in counts
        ],
        in_specs=[pl.BlockSpec(memory_space=SMEM), pl.BlockSpec(memory_space=pl.ANY)],
        out_specs=[pl.BlockSpec(memory_space=pl.ANY)] * len(counts),
        scratch_shapes=[
            VMEM((owners, sends) + state, old_states.dtype),
            pltpu.SemaphoreType.DMA((owners, sends)),
            pltpu.SemaphoreType.DMA((len(counts),)),
        ],
        compiler_params=pltpu.CompilerParams(vmem_limit_bytes=56 << 20),
    )(order, old_states)


def hand_on(*refs):
    pass


def after(x, *others):
    anywhere = pl.BlockSpec(memory_space=pl.ANY)
    return pl.pallas_call(
        hand_on,
        out_shape=jax.ShapeDtypeStruct(x.shape, x.dtype),
        in_specs=[anywhere] * (1 + len(others)),
        out_specs=anywhere,
        input_output_aliases={0: 0},
    )(x, *others)


def roll(x, by):
    return pltpu.roll(x, by % x.shape[0], 0)


def mixer_kernel(
    counts, owners, heads, classes, steps,
    me_ref, emb_ref, live_ref, gain_ref, floor_ref, ggain_ref, qw_hbm, fw_hbm, iw_hbm, ow_hbm,
    *rest,
):
    pieces, sends = len(counts), sum(counts)
    states_hbm = rest[:pieces]
    own_ref, kv_ref = rest[pieces : pieces + 2]
    parts = rest[pieces + 2 : pieces + 2 + classes]
    (qw_ref, fw_ref, iw_ref, ow_ref, states, qhi_ref, qlo_ref, mixed_ref, part_ref, sems) = rest[
        pieces + 2 + classes :
    ]
    weight_pairs = ((qw_hbm, qw_ref), (fw_hbm, fw_ref), (iw_hbm, iw_ref), (ow_hbm, ow_ref))
    loads = [
        pltpu.make_async_copy(there, here, sems.at[i]) for i, (there, here) in enumerate(weight_pairs)
    ]
    state_loads = [
        pltpu.make_async_copy(
            states_hbm[i], states.at[:, pl.ds(sum(counts[:i]), counts[i])], sems.at[4 + i]
        )
        for i in range(pieces)
    ]
    for load in loads[:3] + state_loads + loads[3:]:
        load.start()
    tokens = live_ref.shape[0]
    requests = tokens // steps
    group = requests // classes
    rows = group * steps
    stream = emb_ref[0:tokens, :].astype(F32)
    scale = lax.rsqrt(jnp.mean(stream * stream, axis=1, keepdims=True) + epsilon)
    normed = (stream * scale * gain_ref[...]).astype(BF16)
    loads[0].wait()
    query = jnp.dot(normed, qw_ref[...], preferred_element_type=F32)
    query = query * jax.nn.sigmoid(query) * HEAD_DIM ** (-0.5)
    loads[1].wait()
    forget_raw = jnp.dot(normed, fw_ref[...], preferred_element_type=F32)
    loads[2].wait()
    value = jnp.dot(normed, iw_ref[...], preferred_element_type=F32)
    floor = floor_ref[...]
    forget = jnp.where(
        live_ref[...] > 0.0, floor + (1.0 - floor) * jax.nn.sigmoid(forget_raw), 1.0
    )
    key = 1.0 - forget
    step = lax.broadcasted_iota(jnp.int32, forget.shape, 0) % steps
    upto = forget * jnp.where(step >= 1, roll(forget, 1), 1.0)
    upto = upto * jnp.where(step >= 2, roll(upto, 2), 1.0)
    after = jnp.where(step <= steps - 2, roll(forget, -1), 1.0)
    after = after * jnp.where(step <= steps - 3, roll(forget, -2), 1.0)
    after = after * jnp.where(step <= steps - 4, roll(forget, -3), 1.0)
    carried = query * upto
    high = carried.astype(BF16).astype(F32)
    qhi_ref[...] = high
    qlo_ref[...] = carried - high
    lag_key, lag_value = key, value
    local = [jnp.zeros((tokens, HEAD_DIM), F32) for _ in range(heads)]
    for lag in range(steps):
        if lag:
            lag_key = roll(lag_key, 1) * forget
            lag_value = roll(lag_value, 1)
        product = jnp.where(step >= lag, query * lag_key, 0.0)
        for head in range(heads):
            cols = slice(head * HEAD_DIM, (head + 1) * HEAD_DIM)
            weight = jnp.sum(product[:, cols], axis=1, keepdims=True)
            local[head] = local[head] + weight * lag_value[:, cols]
    for head in range(heads):
        mixed_ref[:, head * HEAD_DIM : (head + 1) * HEAD_DIM] = local[head]
    for load in state_loads:
        load.wait()
    here = me_ref[0]
    upper = lax.broadcasted_iota(jnp.int32, (8, HEAD_DIM), 0) < steps
    for tile in range(tokens // 8):
        for head in range(heads):
            cols = slice(head * HEAD_DIM, (head + 1) * HEAD_DIM)
            at = slice(tile * 8, tile * 8 + 8)
            left = jnp.concatenate([qhi_ref[at, cols], qlo_ref[at, cols]], axis=0).astype(BF16)
            got = []
            for request in (2 * tile, 2 * tile + 1):
                place = (request % group) * classes + request // group
                old = states[here ^ (place // sends), place % sends, head]
                product = jnp.dot(left, old, preferred_element_type=F32)
                got.append(product[0:8] + product[8:16])
            mixed_ref[at, cols] += jnp.where(upper, got[0], got[1])
    mixed = mixed_ref[...]
    square = jnp.sum(mixed * mixed, axis=1, keepdims=True)
    loads[3].wait()
    part_ref[:, 0:D] = jnp.dot(
        (mixed * ggain_ref[...]).astype(BF16), ow_ref[...], preferred_element_type=F32
    )
    square_high = square.astype(BF16).astype(F32)
    lane = lax.broadcasted_iota(jnp.int32, (tokens, 128), 1)
    part_ref[:, D : D + 128] = jnp.where(lane < 64, square_high, square - square_high)
    for e in range(classes):
        first = pl.multiple_of((me_ref[1] ^ e) * rows, rows)
        parts[e][...] = part_ref[pl.ds(first, rows), :].astype(BF16)
    own_ref[...] = emb_ref[pl.ds(pl.multiple_of(me_ref[1] * rows, rows), rows), :]
    both = jnp.concatenate([(key * after).astype(BF16), value.astype(BF16)], axis=0)
    shape = (2 * tokens, 2 * tokens)
    target = lax.broadcasted_iota(jnp.int32, shape, 0)
    source = lax.broadcasted_iota(jnp.int32, shape, 1)
    slot, within = target // (2 * steps), target % (2 * steps)
    place = ((slot // sends) ^ here) * sends + slot % sends
    request = (place % classes) * group + place // classes
    wanted = request * steps + within % steps + jnp.where(within >= steps, tokens, 0)
    pick = jnp.where(source == wanted, 1.0, 0.0).astype(BF16)
    kv_ref[...] = jnp.dot(pick, both, preferred_element_type=F32).astype(BF16)


def mixer(me, emb, live, gain, floor, ggain, weights, states, steps, classes):
    tokens = live.shape[0]
    counts = tuple(piece.shape[1] for piece in states)
    owners, _, heads = states[0].shape[:3]
    width = floor.shape[1]
    rows = tokens // classes
    vmem, anywhere = pl.BlockSpec(memory_space=VMEM), pl.BlockSpec(memory_space=pl.ANY)
    return pl.pallas_call(
        functools.partial(mixer_kernel, counts, owners, heads, classes, steps),
        out_shape=[
            jax.ShapeDtypeStruct((rows, D), BF16),
            jax.ShapeDtypeStruct((2 * tokens, width), BF16),
        ]
        + [jax.ShapeDtypeStruct((rows, D + 128), BF16)] * classes,
        in_specs=[pl.BlockSpec(memory_space=SMEM)] + [vmem] * 5 + [anywhere] * (4 + len(states)),
        out_specs=[vmem] * (2 + classes),
        scratch_shapes=[VMEM(w.shape, BF16) for w in weights]
        + [
            VMEM((owners, sum(counts)) + states[0].shape[2:], BF16),
            VMEM((tokens, width), F32),
            VMEM((tokens, width), F32),
            VMEM((tokens, width), F32),
            VMEM((tokens, D + 128), F32),
            pltpu.SemaphoreType.DMA((4 + len(states),)),
        ],
        compiler_params=pltpu.CompilerParams(vmem_limit_bytes=56 << 20),
    )(me, emb, live, gain, floor, ggain, *weights, *states)


def update_kernel(steps, slot_ref, kv_ref, *rest):
    states, out_ref = rest[:-1], rest[-1]
    owners, _, heads = states[0].shape[:3]
    ranks = [(piece, i) for piece in states for i in range(piece.shape[1])]
    sends = len(ranks)
    diagonal = lax.broadcasted_iota(jnp.int32, (HEAD_DIM, HEAD_DIM), 0) == lax.broadcasted_iota(
        jnp.int32, (HEAD_DIM, HEAD_DIM), 1
    )
    first = lax.broadcasted_iota(jnp.int32, (2 * steps, HEAD_DIM), 0) < steps
    for k in range(owners):
        for rank, (piece, i) in enumerate(ranks):
            place = k * sends + rank
            slot = slot_ref[place]
            for head in range(heads):
                cols = slice(head * HEAD_DIM, (head + 1) * HEAD_DIM)
                both = kv_ref[place, :, cols]
                key = jnp.where(first, both, 0.0)
                value = jnp.where(first, roll(both, steps), 0.0)
                kept = 1.0 - jnp.sum(key, axis=0, keepdims=True)
                keep = jnp.where(diagonal, kept, 0.0).astype(BF16)
                fresh = lax.dot_general(
                    key, value, (((0,), (0,)), ((), ())), preferred_element_type=F32
                )
                old = jnp.dot(keep, piece[k, i, head], preferred_element_type=F32)
                out_ref[slot, head] = (old + fresh).astype(BF16)


def update_states(slots, kv, states, steps):
    vmem = pl.BlockSpec(memory_space=VMEM)
    return pl.pallas_call(
        functools.partial(update_kernel, steps),
        out_shape=jax.ShapeDtypeStruct((slots.shape[0],) + states[0].shape[2:], BF16),
        in_specs=[pl.BlockSpec(memory_space=SMEM)] + [vmem] * (1 + len(states)),
        out_specs=vmem,
        compiler_params=pltpu.CompilerParams(vmem_limit_bytes=56 << 20),
    )(slots, kv, *states)


def dot_rows(a, b):
    return lax.dot_general(a, b, (((1,), (1,)), ((), ())), preferred_element_type=F32)


def feed_kernel(
    x_hbm, weights_hbm, pick_ref, mine_ref, gain_ref, down_ref, kept_ref, x, weights, feed, act, sems
):
    blocks, height, depth = weights.shape
    units = height // 3
    loads = [pltpu.make_async_copy(x_hbm, x, sems.at[3])]
    for i in range(3):
        span = pl.ds(i * units, units)
        loads.append(
            pltpu.make_async_copy(weights_hbm.at[:, span], weights.at[:, span], sems.at[i])
        )
    for load in loads:
        load.start()
    loads[0].wait()
    stream = x[...].astype(F32)
    scale = lax.rsqrt(jnp.mean(stream * stream, axis=1, keepdims=True) + epsilon)
    feed[...] = (stream * scale * gain_ref[...]).astype(BF16)
    kept_ref[...] = jnp.dot(mine_ref[...], x[...], preferred_element_type=F32).astype(BF16)
    loads[1].wait()
    loads[2].wait()
    for first in range(0, units, 256):
        last = min(first + 256, units)
        gate = up = 0.0
        for b in range(blocks):
            part = feed[:, b * depth : (b + 1) * depth]
            gate += dot_rows(part, weights[b, first:last, :])
            up += dot_rows(part, weights[b, units + first : units + last, :])
        act[:, first:last] = (gate * jax.nn.sigmoid(gate) * up).astype(BF16)
    placed = jnp.dot(pick_ref[...], act[...], preferred_element_type=F32).astype(BF16)
    loads[3].wait()
    for b in range(blocks):
        down_ref[:, b * depth : (b + 1) * depth] = jnp.dot(
            placed, weights[b, 2 * units :, :], preferred_element_type=F32
        ).astype(BF16)


def feed_forward(x, weights, pick, mine, gain):
    vmem, anywhere = pl.BlockSpec(memory_space=VMEM), pl.BlockSpec(memory_space=pl.ANY)
    tokens, width = x.shape
    return pl.pallas_call(
        feed_kernel,
        out_shape=[
            jax.ShapeDtypeStruct((tokens, width), BF16),
            jax.ShapeDtypeStruct((mine.shape[0], width), BF16),
        ],
        in_specs=[anywhere] * 2 + [vmem] * 3,
        out_specs=[vmem] * 2,
        scratch_shapes=[
            VMEM(x.shape, BF16),
            VMEM(weights.shape, BF16),
            VMEM(x.shape, BF16),
            VMEM((tokens, weights.shape[1] // 3), BF16),
            pltpu.SemaphoreType.DMA((4,)),
        ],
        cost_estimate=pl.CostEstimate(
            flops=32 * tokens * weights.size, bytes_accessed=2 * weights.size, transcendentals=0
        ),
        compiler_params=pltpu.CompilerParams(vmem_limit_bytes=58 << 20),
    )(x, weights, pick, mine, gain)


def greatest_kernel(full_hbm, own_hbm, other_hbm, best_ref, full, own, other, sems):
    loads = [
        pltpu.make_async_copy(there, here, sems.at[i])
        for i, (there, here) in enumerate(((full_hbm, full), (own_hbm, own), (other_hbm, other)))
    ]
    for load in loads:
        load.start()
    loads[0].wait()
    best = None
    for i, table in enumerate((own, other)):
        loads[1 + i].wait()
        height = table.shape[0]
        for first in range(0, height, 256):
            entries = dot_rows(table[first : min(first + 256, height), :], full[...])
            top = jnp.max(entries, axis=0, keepdims=True)
            best = top if best is None else jnp.maximum(best, top)
    width = best_ref.shape[1]
    for k in range(best_ref.shape[0]):
        best_ref[k : k + 1, :] = best[:, k * width : (k + 1) * width]


def greatest_entries(blocks, full, own, other):
    anywhere = pl.BlockSpec(memory_space=pl.ANY)
    return pl.pallas_call(
        greatest_kernel,
        out_shape=jax.ShapeDtypeStruct((blocks, full.shape[0] // blocks), F32),
        in_specs=[anywhere] * 3,
        out_specs=pl.BlockSpec(memory_space=VMEM),
        scratch_shapes=[VMEM(x.shape, BF16) for x in (full, own, other)]
        + [pltpu.SemaphoreType.DMA((3,))],
        compiler_params=pltpu.CompilerParams(vmem_limit_bytes=58 << 20),
    )(full, own, other)


def exchange(block, dim, n, n_head):
    if dim == "outer":
        got = [swap(block, "req", n, 2 * j) for j in range(1, n // 2)]
    elif dim == "inner":
        got = [swap(block, "req", n, 1)]
    else:
        got = [swap(block, "head", n_head, 2)]
    return jnp.stack([block] + got)


def gather_by(block, dims, n, n_head):
    rank = block.ndim
    for dim in dims:
        block = exchange(block, dim, n, n_head)
    at = [dims[::-1].index(dim) for dim in ("outer", "inner", "cross")]
    return block.transpose(at + list(range(len(dims), len(dims) + rank)))


def to_all(x, axis):
    return lax.all_to_all(x, axis, split_axis=0, concat_axis=0, tiled=True)


def on_device(
    token_ids, state_perm, token_count, tenant_bounds, old_states, embedding, mixer_gain,
    query_weight, forget_weight, input_weight, forget_floor, group_gain, output_weight, feed_gain,
    gate_weight, up_weight, down_weight, final_gain, tenant_gain, vocab_weight,
):
    requests, steps = token_ids.shape
    n = lax.axis_size("req")
    n_head = lax.axis_size("head")
    r = lax.axis_index("req")
    h = lax.axis_index("head")
    tokens = requests * steps
    everyone = requests * n
    sends = requests // n
    group = requests // n_head
    rows = group * steps
    width = D // n_head

    feed_weights = jnp.concatenate([gate_weight.T, up_weight.T, down_weight], axis=0)
    feed_weights = lax.all_gather(feed_weights, "head", axis=0)

    packed = jnp.concatenate([token_ids.T, state_perm[None], token_count[None]], axis=0)
    packed = to_all(jnp.broadcast_to(packed[None], (n,) + packed.shape), "req").transpose(1, 0, 2).reshape(steps + 2, everyone)
    every = jnp.arange(everyone, dtype=jnp.int32)
    source = packed[steps] // requests
    rank = jnp.sum(
        ((source[None, :] == source[:, None]) & (every[None, :] < every[:, None])).astype(jnp.int32),
        axis=1,
    )
    place = ((every // requests) ^ source) * sends + rank % sends
    at = source * requests + (place % n_head) * group + place // n_head
    chosen = (at[:, None] == every[None, :]).astype(F32)
    ordered = jnp.dot(packed.astype(F32), chosen, precision=lax.Precision.HIGHEST)
    ordered = (ordered + 0.5).astype(jnp.int32)

    ids = ordered[:steps].T.reshape(n, tokens)
    table = embedding.shape[0]
    room = tokens // 2
    holder = lax.div(ids, jnp.int32(table))
    held = holder == r
    earlier = jnp.triu(jnp.ones((tokens, tokens), BF16), 1)
    turn = jnp.dot(held.astype(BF16), earlier, preferred_element_type=F32).astype(jnp.int32)
    local_ids = jnp.where(held, ids - r * table, 0)
    seat = held[:, None] & (turn[:, None] == jnp.arange(room, dtype=jnp.int32)[None, :, None])
    wanted = jnp.sum(jnp.where(seat, local_ids[:, None], 0), axis=2).reshape(n * room)
    got = to_all(jnp.take(embedding, wanted, axis=0, mode="clip").reshape(n, room, width), "req")
    own_holder = lax.dynamic_index_in_dim(holder, r, 0, keepdims=False)
    order = jnp.arange(tokens, dtype=jnp.int32)
    own_turn = jnp.sum(
        ((own_holder[None, :] == own_holder[:, None]) & (order[None, :] < order[:, None])).astype(
            jnp.int32
        ),
        axis=1,
    )
    seat = jnp.where(own_turn < room, own_holder * room + own_turn, -1)
    pick = (seat[:, None] == jnp.arange(n * room, dtype=jnp.int32)[None, :]).astype(BF16)
    embed_part = jnp.dot(
        pick, got.reshape(n * room, width), preferred_element_type=F32
    ).astype(BF16)
    owners = jnp.arange(n, dtype=jnp.int32)
    load = jnp.sum((holder[:, None] == owners[None, :, None]).astype(jnp.int32), axis=2)

    def with_rest(part):
        rows = jnp.take(embedding, local_ids.reshape(n * tokens), axis=0, mode="clip")
        rest = (held & (turn >= room)).reshape(n * tokens, 1)
        rows = jnp.where(rest, rows, jnp.zeros((), BF16)).reshape(n, tokens, width)
        return (part.astype(F32) + jnp.sum(to_all(rows, "req").astype(F32), axis=0)).astype(BF16)

    embed_part = lax.cond(jnp.max(load) > room, with_rest, lambda part: part, embed_part)
    vocab_other = swap(vocab_weight.T, "head", n_head, 1)

    gains = jnp.concatenate([final_gain[None], tenant_gain], axis=0)
    gains_high, gains_low = bf16_parts(gains)
    extra = jnp.zeros((16 - 2 * gains.shape[0], width), BF16)
    embedded = lax.all_gather(
        jnp.concatenate([embed_part, gains_high, gains_low, extra], axis=0), "head", axis=1, tiled=True
    )
    gains = embedded[tokens : tokens + 5].astype(F32) + embedded[tokens + 5 : tokens + 10].astype(F32)

    ordered = lax.dynamic_slice_in_dim(ordered, r * requests, requests, 1)
    old_order = (ordered[steps] - r * requests).reshape(n_head, group).T.reshape(n, sends)
    old_order = jnp.take(old_order, jnp.arange(n) ^ r, axis=0).reshape(requests)
    counts = (2, 2) if sends == 4 else (sends,)
    pieces = sort_states(old_order, old_states, n, counts)
    live = (jnp.arange(steps)[None, :] < ordered[steps + 1][:, None]).astype(F32)
    own, kv, *parts = mixer(
        jnp.stack([r, h]), embedded, live.reshape(tokens, 1), mixer_gain[None], forget_floor[None],
        group_gain[None], (query_weight, forget_weight, input_weight, output_weight), pieces,
        steps, n_head,
    )
    arrived = [to_all(pieces[0], "req")]

    total = parts[0].astype(F32)
    for e in range(1, n_head):
        total = total + swap(parts[e], "head", n_head, e).astype(F32)
    square = total[:, D : D + 1] + total[:, D + 127 : D + 128]
    after_mixer = own.astype(F32) + total[:, :D] * lax.rsqrt(square / D + epsilon)
    after_mixer = after(after_mixer.astype(BF16), feed_weights)
    everything = lax.all_gather(after_mixer, "req", axis=0, tiled=True)
    arrived += [to_all(after(piece, after_mixer[:8, :128]), "req") for piece in pieces[1:]]
    arrived_kv = to_all(after(kv, arrived[-1]).reshape(n, -1, width), "req")

    row = jnp.arange(n * rows, dtype=jnp.int32)
    by_owner, by_group, by_step = row // rows, (row % rows) // steps, row % steps
    if sends % n_head == 0:
        offset = by_group * n_head // sends
    else:
        offset = (by_group * n_head + h) // sends
    wanted = (by_owner ^ offset) * rows + by_group * steps + by_step
    pick = (wanted[None, :] == row[:, None]).astype(BF16)
    mine = (wanted[None, :] == (r * rows + row[:rows])[:, None]).astype(BF16)
    down, kept = feed_forward(everything, feed_weights, pick, mine, feed_gain[None])
    down = after(down, arrived_kv, *arrived)
    hidden = kept.astype(F32) + jnp.sum(to_all(down.reshape(n, rows, D), "req").astype(F32), axis=0)
    mean_square = jnp.mean(hidden * hidden, axis=1, keepdims=True)

    slots = jnp.arange(requests, dtype=jnp.int32)
    source = state_perm // requests
    rank = jnp.sum(
        ((source[None, :] == source[:, None]) & (slots[None, :] < slots[:, None])).astype(jnp.int32),
        axis=1,
    )
    place = (source ^ r) * sends + rank
    natural = source * sends + rank
    slot_of = jnp.sum(jnp.where(natural[None, :] == slots[:, None], slots[None, :], 0), axis=1)
    mine = jnp.sum(
        jnp.where(
            place[None, :] == (jnp.arange(group, dtype=jnp.int32) * n_head + h)[:, None],
            slots[None, :],
            0,
        ),
        axis=1,
    )
    tenant = jnp.sum(
        ((mine + r * requests)[:, None] >= tenant_bounds[None, 1:-1]).astype(jnp.int32), axis=1
    )
    tenant_rows = sum(
        jnp.where((tenant == t)[:, None], gains[1 + t][None, :], 0.0)
        for t in range(tenant_gain.shape[0])
    )
    token_gain = jnp.repeat(tenant_rows * gains[0][None, :], steps, axis=0)
    final = (hidden * lax.rsqrt(mean_square + epsilon) * token_gain).astype(BF16)

    c1, c2 = D * 7 // 16, D * 13 // 16
    full = jnp.concatenate(
        [
            gather_by(final[:, :c1], ("outer", "inner", "cross"), n, n_head),
            gather_by(final[:, c1:c2], ("cross", "outer", "inner"), n, n_head),
            gather_by(final[:, c2:], ("inner", "cross", "outer"), n, n_head),
        ],
        axis=-1,
    ).reshape(n * 2 * rows, D)
    new_states = update_states(
        slot_of, arrived_kv.reshape(requests, 2 * steps, width).astype(F32), arrived, steps
    )
    best = greatest_entries(n, full, vocab_weight.T, vocab_other)
    best = jnp.take(best, jnp.arange(n) ^ r, axis=0)
    got = jnp.max(to_all(best, "req"), axis=0)
    got = lax.all_gather(got, "head", axis=0).reshape(n_head, 2, rows)
    crossed = jnp.stack([got[i ^ 2, 1] for i in range(n_head)])
    best = jnp.maximum(got[:, 0], crossed).reshape(requests, steps)
    index = (place % n_head) * group + place // n_head
    match = (index[:, None] == slots[None, :])[:, :, None]
    best = jnp.sum(jnp.where(match, best[None], 0.0), axis=1)
    live = jnp.arange(steps)[None, :] < token_count[:, None]
    greatest = jnp.max(jnp.where(live, best, -1e30), axis=1)

    blocks = hidden.reshape(rows, n_head, width).transpose(1, 0, 2)
    tail = jnp.broadcast_to(mean_square, (rows, 128))
    whole = []
    for e in range(n_head):
        block = lax.dynamic_index_in_dim(blocks, h ^ e, 0, keepdims=False)
        block = jnp.concatenate([block, tail], axis=1)
        whole.append(block if e == 0 else swap(block, "head", n_head, e))
    whole = jnp.stack(whole).reshape(requests, steps, width + 128)
    index = ((place % n_head) ^ h) * group + place // n_head
    whole = jnp.take(whole, index, axis=0, mode="clip")
    last = jnp.arange(steps)[None, :] == (token_count - 1)[:, None]
    last_norm = jnp.sqrt(jnp.sum(jnp.where(last, whole[:, :, width], 0.0), axis=1) + epsilon)

    return whole[:, :, :width], new_states, last_norm, greatest


def solution(mesh):
    placed = (
        P("req", None),
        P("req"),
        P("req"),
        P(),
        P("req", "head", None, None),
        P("req", "head"),
        P(),
        P(None, "head"),
        P(None, "head"),
        P(None, "head"),
        P("head"),
        P("head"),
        P("head", None),
        P(),
        P("head", "req"),
        P("head", "req"),
        P("req", "head"),
        P("head"),
        P(None, "head"),
        P(None, ("req", "head")),
    )
    return jax.shard_map(
        on_device,
        mesh=mesh,
        in_specs=placed,
        out_specs=(P("req", None, "head"), P("req", "head", None, None), P("req"), P("req")),
        check_vma=False,
    )
```

```python
import functools

import jax
import jax.numpy as jnp
import numpy as np
from jax import lax
from jax.experimental import pallas as pl
from jax.experimental.pallas import tpu as pltpu
from jax.sharding import PartitionSpec as P

D = 2048
HEAD_DIM = 128
epsilon = 1e-06
F32 = jnp.float32
BF16 = jnp.bfloat16
VMEM = pltpu.VMEM
SMEM = pltpu.SMEM


def swap(x, axis, size, offset):
    return lax.ppermute(x, axis, [(i, i ^ offset) for i in range(size)])


def bf16_parts(x):
    high = lax.reduce_precision(x, 8, 7)
    return high.astype(BF16), (x - high).astype(BF16)


def sort_kernel(sends, order_ref, old_ref, *rest):
    outs, (held, in_sems, out_sems) = rest[:-3], rest[-3:]
    owners = held.shape[0]
    spans, first = [], 0
    for out in outs:
        spans.append((first, out.shape[1]))
        first += out.shape[1]

    def load(owner, rank):
        at = owner * sends + rank
        return pltpu.make_async_copy(
            old_ref.at[order_ref[at]], held.at[owner, rank], in_sems.at[owner, rank]
        )

    def store(part):
        first, count = spans[part]
        return pltpu.make_async_copy(
            held.at[:, pl.ds(first, count)], outs[part], out_sems.at[part]
        )

    for first, count in spans:
        for owner in range(owners):
            for rank in range(first, first + count):
                load(owner, rank).start()
    for part, (first, count) in enumerate(spans):
        for owner in range(owners):
            for rank in range(first, first + count):
                load(owner, rank).wait()
        store(part).start()
    for part in range(len(outs)):
        store(part).wait()


def sort_states(order, old_states, owners, counts):
    sends = sum(counts)
    state = old_states.shape[1:]
    return pl.pallas_call(
        functools.partial(sort_kernel, sends),
        out_shape=[
            jax.ShapeDtypeStruct((owners, count) + state, old_states.dtype) for count in counts
        ],
        in_specs=[pl.BlockSpec(memory_space=SMEM), pl.BlockSpec(memory_space=pl.ANY)],
        out_specs=[pl.BlockSpec(memory_space=pl.ANY)] * len(counts),
        scratch_shapes=[
            VMEM((owners, sends) + state, old_states.dtype),
            pltpu.SemaphoreType.DMA((owners, sends)),
            pltpu.SemaphoreType.DMA((len(counts),)),
        ],
        compiler_params=pltpu.CompilerParams(vmem_limit_bytes=56 << 20),
    )(order, old_states)


def hand_on(*refs):
    pass


def after(x, *others, flops=0):
    anywhere = pl.BlockSpec(memory_space=pl.ANY)
    return pl.pallas_call(
        hand_on,
        out_shape=jax.ShapeDtypeStruct(x.shape, x.dtype),
        in_specs=[anywhere] * (1 + len(others)),
        out_specs=anywhere,
        input_output_aliases={0: 0},
        cost_estimate=pl.CostEstimate(flops=flops, bytes_accessed=0, transcendentals=0),
    )(x, *others)


def roll(x, by):
    return pltpu.roll(x, by % x.shape[0], 0)


def mixer_kernel(
    counts, owners, heads, classes, steps,
    me_ref, emb_ref, live_ref, gain_ref, floor_ref, ggain_ref, qw_hbm, fw_hbm, iw_hbm, ow_hbm,
    *rest,
):
    pieces, sends = len(counts), sum(counts)
    states_hbm = rest[:pieces]
    own_ref, kv_ref = rest[pieces : pieces + 2]
    parts = rest[pieces + 2 : pieces + 2 + classes]
    (qw_ref, fw_ref, iw_ref, ow_ref, states, qhi_ref, qlo_ref, mixed_ref, part_ref, sems) = rest[
        pieces + 2 + classes :
    ]
    weight_pairs = ((qw_hbm, qw_ref), (fw_hbm, fw_ref), (iw_hbm, iw_ref), (ow_hbm, ow_ref))
    loads = [
        pltpu.make_async_copy(there, here, sems.at[i]) for i, (there, here) in enumerate(weight_pairs)
    ]
    state_loads = [
        pltpu.make_async_copy(
            states_hbm[i], states.at[:, pl.ds(sum(counts[:i]), counts[i])], sems.at[4 + i]
        )
        for i in range(pieces)
    ]
    for load in loads[:3] + state_loads + loads[3:]:
        load.start()
    tokens = live_ref.shape[0]
    requests = tokens // steps
    group = requests // classes
    rows = group * steps
    stream = emb_ref[0:tokens, :].astype(F32)
    scale = lax.rsqrt(jnp.mean(stream * stream, axis=1, keepdims=True) + epsilon)
    normed = (stream * scale * gain_ref[...]).astype(BF16)
    loads[0].wait()
    query = jnp.dot(normed, qw_ref[...], preferred_element_type=F32)
    query = query * jax.nn.sigmoid(query) * HEAD_DIM ** (-0.5)
    loads[1].wait()
    forget_raw = jnp.dot(normed, fw_ref[...], preferred_element_type=F32)
    loads[2].wait()
    value = jnp.dot(normed, iw_ref[...], preferred_element_type=F32)
    floor = floor_ref[...]
    forget = jnp.where(
        live_ref[...] > 0.0, floor + (1.0 - floor) * jax.nn.sigmoid(forget_raw), 1.0
    )
    key = 1.0 - forget
    step = lax.broadcasted_iota(jnp.int32, forget.shape, 0) % steps
    upto = forget * jnp.where(step >= 1, roll(forget, 1), 1.0)
    upto = upto * jnp.where(step >= 2, roll(upto, 2), 1.0)
    after = jnp.where(step <= steps - 2, roll(forget, -1), 1.0)
    after = after * jnp.where(step <= steps - 3, roll(forget, -2), 1.0)
    after = after * jnp.where(step <= steps - 4, roll(forget, -3), 1.0)
    carried = query * upto
    high = carried.astype(BF16).astype(F32)
    qhi_ref[...] = high
    qlo_ref[...] = carried - high
    lag_key, lag_value = key, value
    local = [jnp.zeros((tokens, HEAD_DIM), F32) for _ in range(heads)]
    for lag in range(steps):
        if lag:
            lag_key = roll(lag_key, 1) * forget
            lag_value = roll(lag_value, 1)
        product = jnp.where(step >= lag, query * lag_key, 0.0)
        for head in range(heads):
            cols = slice(head * HEAD_DIM, (head + 1) * HEAD_DIM)
            weight = jnp.sum(product[:, cols], axis=1, keepdims=True)
            local[head] = local[head] + weight * lag_value[:, cols]
    for head in range(heads):
        mixed_ref[:, head * HEAD_DIM : (head + 1) * HEAD_DIM] = local[head]
    for load in state_loads:
        load.wait()
    here = me_ref[0]
    upper = lax.broadcasted_iota(jnp.int32, (8, HEAD_DIM), 0) < steps
    for tile in range(tokens // 8):
        for head in range(heads):
            cols = slice(head * HEAD_DIM, (head + 1) * HEAD_DIM)
            at = slice(tile * 8, tile * 8 + 8)
            left = jnp.concatenate([qhi_ref[at, cols], qlo_ref[at, cols]], axis=0).astype(BF16)
            got = []
            for request in (2 * tile, 2 * tile + 1):
                place = (request % group) * classes + request // group
                old = states[here ^ (place // sends), place % sends, head]
                product = jnp.dot(left, old, preferred_element_type=F32)
                got.append(product[0:8] + product[8:16])
            mixed_ref[at, cols] += jnp.where(upper, got[0], got[1])
    mixed = mixed_ref[...]
    square = jnp.sum(mixed * mixed, axis=1, keepdims=True)
    loads[3].wait()
    part_ref[:, 0:D] = jnp.dot(
        (mixed * ggain_ref[...]).astype(BF16), ow_ref[...], preferred_element_type=F32
    )
    square_high = square.astype(BF16).astype(F32)
    lane = lax.broadcasted_iota(jnp.int32, (tokens, 128), 1)
    part_ref[:, D : D + 128] = jnp.where(lane < 64, square_high, square - square_high)
    for e in range(classes):
        first = pl.multiple_of((me_ref[1] ^ e) * rows, rows)
        parts[e][...] = part_ref[pl.ds(first, rows), :].astype(BF16)
    own_ref[...] = emb_ref[pl.ds(pl.multiple_of(me_ref[1] * rows, rows), rows), :]
    both = jnp.concatenate([(key * after).astype(BF16), value.astype(BF16)], axis=0)
    shape = (2 * tokens, 2 * tokens)
    target = lax.broadcasted_iota(jnp.int32, shape, 0)
    source = lax.broadcasted_iota(jnp.int32, shape, 1)
    slot, within = target // (2 * steps), target % (2 * steps)
    place = ((slot // sends) ^ here) * sends + slot % sends
    request = (place % classes) * group + place // classes
    wanted = request * steps + within % steps + jnp.where(within >= steps, tokens, 0)
    pick = jnp.where(source == wanted, 1.0, 0.0).astype(BF16)
    kv_ref[...] = jnp.dot(pick, both, preferred_element_type=F32).astype(BF16)


def mixer(me, emb, live, gain, floor, ggain, weights, states, steps, classes):
    tokens = live.shape[0]
    counts = tuple(piece.shape[1] for piece in states)
    owners, _, heads = states[0].shape[:3]
    width = floor.shape[1]
    rows = tokens // classes
    vmem, anywhere = pl.BlockSpec(memory_space=VMEM), pl.BlockSpec(memory_space=pl.ANY)
    return pl.pallas_call(
        functools.partial(mixer_kernel, counts, owners, heads, classes, steps),
        out_shape=[
            jax.ShapeDtypeStruct((rows, D), BF16),
            jax.ShapeDtypeStruct((2 * tokens, width), BF16),
        ]
        + [jax.ShapeDtypeStruct((rows, D + 128), BF16)] * classes,
        in_specs=[pl.BlockSpec(memory_space=SMEM)] + [vmem] * 5 + [anywhere] * (4 + len(states)),
        out_specs=[vmem] * (2 + classes),
        scratch_shapes=[VMEM(w.shape, BF16) for w in weights]
        + [
            VMEM((owners, sum(counts)) + states[0].shape[2:], BF16),
            VMEM((tokens, width), F32),
            VMEM((tokens, width), F32),
            VMEM((tokens, width), F32),
            VMEM((tokens, D + 128), F32),
            pltpu.SemaphoreType.DMA((4 + len(states),)),
        ],
        compiler_params=pltpu.CompilerParams(vmem_limit_bytes=56 << 20),
    )(me, emb, live, gain, floor, ggain, *weights, *states)


def update_kernel(steps, slot_ref, kv_ref, *rest):
    states, out_ref = rest[:-1], rest[-1]
    owners, _, heads = states[0].shape[:3]
    ranks = [(piece, i) for piece in states for i in range(piece.shape[1])]
    sends = len(ranks)
    diagonal = lax.broadcasted_iota(jnp.int32, (HEAD_DIM, HEAD_DIM), 0) == lax.broadcasted_iota(
        jnp.int32, (HEAD_DIM, HEAD_DIM), 1
    )
    first = lax.broadcasted_iota(jnp.int32, (2 * steps, HEAD_DIM), 0) < steps
    for k in range(owners):
        for rank, (piece, i) in enumerate(ranks):
            place = k * sends + rank
            slot = slot_ref[place]
            for head in range(heads):
                cols = slice(head * HEAD_DIM, (head + 1) * HEAD_DIM)
                both = kv_ref[place, :, cols]
                key = jnp.where(first, both, 0.0)
                value = jnp.where(first, roll(both, steps), 0.0)
                kept = 1.0 - jnp.sum(key, axis=0, keepdims=True)
                keep = jnp.where(diagonal, kept, 0.0).astype(BF16)
                fresh = lax.dot_general(
                    key, value, (((0,), (0,)), ((), ())), preferred_element_type=F32
                )
                old = jnp.dot(keep, piece[k, i, head], preferred_element_type=F32)
                out_ref[slot, head] = (old + fresh).astype(BF16)


def update_states(slots, kv, states, steps):
    vmem = pl.BlockSpec(memory_space=VMEM)
    return pl.pallas_call(
        functools.partial(update_kernel, steps),
        out_shape=jax.ShapeDtypeStruct((slots.shape[0],) + states[0].shape[2:], BF16),
        in_specs=[pl.BlockSpec(memory_space=SMEM)] + [vmem] * (1 + len(states)),
        out_specs=vmem,
        compiler_params=pltpu.CompilerParams(vmem_limit_bytes=56 << 20),
    )(slots, kv, *states)


def dot_rows(a, b):
    return lax.dot_general(a, b, (((1,), (1,)), ((), ())), preferred_element_type=F32)


def feed_kernel(
    x_hbm, weights_hbm, pick_ref, mine_ref, gain_ref, down_ref, kept_ref, x, weights, feed, act, sems
):
    blocks, height, depth = weights.shape
    units = height // 3
    loads = [pltpu.make_async_copy(x_hbm, x, sems.at[3])]
    for i in range(3):
        span = pl.ds(i * units, units)
        loads.append(
            pltpu.make_async_copy(weights_hbm.at[:, span], weights.at[:, span], sems.at[i])
        )
    for load in loads:
        load.start()
    loads[0].wait()
    stream = x[...].astype(F32)
    scale = lax.rsqrt(jnp.mean(stream * stream, axis=1, keepdims=True) + epsilon)
    feed[...] = (stream * scale * gain_ref[...]).astype(BF16)
    kept_ref[...] = jnp.dot(mine_ref[...], x[...], preferred_element_type=F32).astype(BF16)
    loads[1].wait()
    loads[2].wait()
    for first in range(0, units, 256):
        last = min(first + 256, units)
        gate = up = 0.0
        for b in range(blocks):
            part = feed[:, b * depth : (b + 1) * depth]
            gate += dot_rows(part, weights[b, first:last, :])
            up += dot_rows(part, weights[b, units + first : units + last, :])
        act[:, first:last] = (gate * jax.nn.sigmoid(gate) * up).astype(BF16)
    placed = jnp.dot(pick_ref[...], act[...], preferred_element_type=F32).astype(BF16)
    loads[3].wait()
    for b in range(blocks):
        down_ref[:, b * depth : (b + 1) * depth] = jnp.dot(
            placed, weights[b, 2 * units :, :], preferred_element_type=F32
        ).astype(BF16)


def feed_forward(x, weights, pick, mine, gain):
    vmem, anywhere = pl.BlockSpec(memory_space=VMEM), pl.BlockSpec(memory_space=pl.ANY)
    tokens, width = x.shape
    return pl.pallas_call(
        feed_kernel,
        out_shape=[
            jax.ShapeDtypeStruct((tokens, width), BF16),
            jax.ShapeDtypeStruct((mine.shape[0], width), BF16),
        ],
        in_specs=[anywhere] * 2 + [vmem] * 3,
        out_specs=[vmem] * 2,
        scratch_shapes=[
            VMEM(x.shape, BF16),
            VMEM(weights.shape, BF16),
            VMEM(x.shape, BF16),
            VMEM((tokens, weights.shape[1] // 3), BF16),
            pltpu.SemaphoreType.DMA((4,)),
        ],
        compiler_params=pltpu.CompilerParams(vmem_limit_bytes=58 << 20),
    )(x, weights, pick, mine, gain)


def greatest_kernel(full_hbm, own_hbm, other_hbm, best_ref, full, own, other, sems):
    loads = [
        pltpu.make_async_copy(there, here, sems.at[i])
        for i, (there, here) in enumerate(((full_hbm, full), (own_hbm, own), (other_hbm, other)))
    ]
    for load in loads:
        load.start()
    loads[0].wait()
    best = None
    for i, table in enumerate((own, other)):
        loads[1 + i].wait()
        height = table.shape[0]
        for first in range(0, height, 256):
            entries = dot_rows(table[first : min(first + 256, height), :], full[...])
            top = jnp.max(entries, axis=0, keepdims=True)
            best = top if best is None else jnp.maximum(best, top)
    width = best_ref.shape[1]
    for k in range(best_ref.shape[0]):
        best_ref[k : k + 1, :] = best[:, k * width : (k + 1) * width]


def greatest_entries(blocks, full, own, other):
    anywhere = pl.BlockSpec(memory_space=pl.ANY)
    return pl.pallas_call(
        greatest_kernel,
        out_shape=jax.ShapeDtypeStruct((blocks, full.shape[0] // blocks), F32),
        in_specs=[anywhere] * 3,
        out_specs=pl.BlockSpec(memory_space=VMEM),
        scratch_shapes=[VMEM(x.shape, BF16) for x in (full, own, other)]
        + [pltpu.SemaphoreType.DMA((3,))],
        compiler_params=pltpu.CompilerParams(vmem_limit_bytes=58 << 20),
    )(full, own, other)


def exchange(block, dim, n, n_head):
    if dim == "outer":
        got = [swap(block, "req", n, 2 * j) for j in range(1, n // 2)]
    elif dim == "inner":
        got = [swap(block, "req", n, 1)]
    else:
        got = [swap(block, "head", n_head, 2)]
    return jnp.stack([block] + got)


def gather_by(block, dims, n, n_head):
    rank = block.ndim
    for dim in dims:
        block = exchange(block, dim, n, n_head)
    at = [dims[::-1].index(dim) for dim in ("outer", "inner", "cross")]
    return block.transpose(at + list(range(len(dims), len(dims) + rank)))


def to_all(x, axis):
    return lax.all_to_all(x, axis, split_axis=0, concat_axis=0, tiled=True)


def on_device(
    token_ids, state_perm, token_count, tenant_bounds, old_states, embedding, mixer_gain,
    query_weight, forget_weight, input_weight, forget_floor, group_gain, output_weight, feed_gain,
    gate_weight, up_weight, down_weight, final_gain, tenant_gain, vocab_weight,
):
    requests, steps = token_ids.shape
    n = lax.axis_size("req")
    n_head = lax.axis_size("head")
    r = lax.axis_index("req")
    h = lax.axis_index("head")
    tokens = requests * steps
    everyone = requests * n
    sends = requests // n
    group = requests // n_head
    rows = group * steps
    width = D // n_head

    feed_weights = jnp.concatenate([gate_weight.T, up_weight.T, down_weight], axis=0)
    feed_weights = lax.all_gather(feed_weights, "head", axis=0)

    packed = jnp.concatenate([token_ids.T, state_perm[None], token_count[None]], axis=0)
    packed = to_all(jnp.broadcast_to(packed[None], (n,) + packed.shape), "req").transpose(1, 0, 2).reshape(steps + 2, everyone)
    every = jnp.arange(everyone, dtype=jnp.int32)
    source = packed[steps] // requests
    rank = jnp.sum(
        ((source[None, :] == source[:, None]) & (every[None, :] < every[:, None])).astype(jnp.int32),
        axis=1,
    )
    place = ((every // requests) ^ source) * sends + rank % sends
    at = source * requests + (place % n_head) * group + place // n_head
    chosen = (at[:, None] == every[None, :]).astype(F32)
    ordered = jnp.dot(packed.astype(F32), chosen, precision=lax.Precision.HIGHEST)
    ordered = (ordered + 0.5).astype(jnp.int32)

    ids = ordered[:steps].T.reshape(n, tokens)
    table = embedding.shape[0]
    room = tokens // 2
    holder = lax.div(ids, jnp.int32(table))
    held = holder == r
    earlier = jnp.triu(jnp.ones((tokens, tokens), BF16), 1)
    turn = jnp.dot(held.astype(BF16), earlier, preferred_element_type=F32).astype(jnp.int32)
    local_ids = jnp.where(held, ids - r * table, 0)
    seat = held[:, None] & (turn[:, None] == jnp.arange(room, dtype=jnp.int32)[None, :, None])
    wanted = jnp.sum(jnp.where(seat, local_ids[:, None], 0), axis=2).reshape(n * room)
    got = to_all(jnp.take(embedding, wanted, axis=0, mode="clip").reshape(n, room, width), "req")
    own_holder = lax.dynamic_index_in_dim(holder, r, 0, keepdims=False)
    order = jnp.arange(tokens, dtype=jnp.int32)
    own_turn = jnp.sum(
        ((own_holder[None, :] == own_holder[:, None]) & (order[None, :] < order[:, None])).astype(
            jnp.int32
        ),
        axis=1,
    )
    seat = jnp.where(own_turn < room, own_holder * room + own_turn, -1)
    pick = (seat[:, None] == jnp.arange(n * room, dtype=jnp.int32)[None, :]).astype(BF16)
    embed_part = jnp.dot(
        pick, got.reshape(n * room, width), preferred_element_type=F32
    ).astype(BF16)
    owners = jnp.arange(n, dtype=jnp.int32)
    load = jnp.sum((holder[:, None] == owners[None, :, None]).astype(jnp.int32), axis=2)

    def with_rest(part):
        rows = jnp.take(embedding, local_ids.reshape(n * tokens), axis=0, mode="clip")
        rest = (held & (turn >= room)).reshape(n * tokens, 1)
        rows = jnp.where(rest, rows, jnp.zeros((), BF16)).reshape(n, tokens, width)
        return (part.astype(F32) + jnp.sum(to_all(rows, "req").astype(F32), axis=0)).astype(BF16)

    embed_part = lax.cond(jnp.max(load) > room, with_rest, lambda part: part, embed_part)
    vocab_other = swap(vocab_weight.T, "head", n_head, 1)

    gains = jnp.concatenate([final_gain[None], tenant_gain], axis=0)
    gains_high, gains_low = bf16_parts(gains)
    extra = jnp.zeros((16 - 2 * gains.shape[0], width), BF16)
    embedded = lax.all_gather(
        jnp.concatenate([embed_part, gains_high, gains_low, extra], axis=0), "head", axis=1, tiled=True
    )
    gains = embedded[tokens : tokens + 5].astype(F32) + embedded[tokens + 5 : tokens + 10].astype(F32)

    ordered = lax.dynamic_slice_in_dim(ordered, r * requests, requests, 1)
    old_order = (ordered[steps] - r * requests).reshape(n_head, group).T.reshape(n, sends)
    old_order = jnp.take(old_order, jnp.arange(n) ^ r, axis=0).reshape(requests)
    counts = (2, 2) if sends == 4 else (sends,)
    pieces = sort_states(old_order, old_states, n, counts)
    live = (jnp.arange(steps)[None, :] < ordered[steps + 1][:, None]).astype(F32)
    own, kv, *parts = mixer(
        jnp.stack([r, h]), embedded, live.reshape(tokens, 1), mixer_gain[None], forget_floor[None],
        group_gain[None], (query_weight, forget_weight, input_weight, output_weight), pieces,
        steps, n_head,
    )
    arrived = [to_all(pieces[0], "req")]

    total = parts[0].astype(F32)
    for e in range(1, n_head):
        total = total + swap(parts[e], "head", n_head, e).astype(F32)
    square = total[:, D : D + 1] + total[:, D + 127 : D + 128]
    after_mixer = own.astype(F32) + total[:, :D] * lax.rsqrt(square / D + epsilon)
    after_mixer = after(after_mixer.astype(BF16), feed_weights)
    everything = lax.all_gather(after_mixer, "req", axis=0, tiled=True)
    for piece in pieces[1:]:
        piece = after(piece, after_mixer, *arrived, flops=50_000_000_000)
        arrived += [to_all(piece, "req")]
    arrived_kv = to_all(after(kv, arrived[-1]).reshape(n, -1, width), "req")

    row = jnp.arange(n * rows, dtype=jnp.int32)
    by_owner, by_group, by_step = row // rows, (row % rows) // steps, row % steps
    if sends % n_head == 0:
        offset = by_group * n_head // sends
    else:
        offset = (by_group * n_head + h) // sends
    wanted = (by_owner ^ offset) * rows + by_group * steps + by_step
    pick = (wanted[None, :] == row[:, None]).astype(BF16)
    mine = (wanted[None, :] == (r * rows + row[:rows])[:, None]).astype(BF16)
    down, kept = feed_forward(everything, feed_weights, pick, mine, feed_gain[None])
    down = after(down, arrived_kv, *arrived)
    hidden = kept.astype(F32) + jnp.sum(to_all(down.reshape(n, rows, D), "req").astype(F32), axis=0)
    mean_square = jnp.mean(hidden * hidden, axis=1, keepdims=True)

    slots = jnp.arange(requests, dtype=jnp.int32)
    source = state_perm // requests
    rank = jnp.sum(
        ((source[None, :] == source[:, None]) & (slots[None, :] < slots[:, None])).astype(jnp.int32),
        axis=1,
    )
    place = (source ^ r) * sends + rank
    natural = source * sends + rank
    slot_of = jnp.sum(jnp.where(natural[None, :] == slots[:, None], slots[None, :], 0), axis=1)
    mine = jnp.sum(
        jnp.where(
            place[None, :] == (jnp.arange(group, dtype=jnp.int32) * n_head + h)[:, None],
            slots[None, :],
            0,
        ),
        axis=1,
    )
    tenant = jnp.sum(
        ((mine + r * requests)[:, None] >= tenant_bounds[None, 1:-1]).astype(jnp.int32), axis=1
    )
    tenant_rows = sum(
        jnp.where((tenant == t)[:, None], gains[1 + t][None, :], 0.0)
        for t in range(tenant_gain.shape[0])
    )
    token_gain = jnp.repeat(tenant_rows * gains[0][None, :], steps, axis=0)
    final = (hidden * lax.rsqrt(mean_square + epsilon) * token_gain).astype(BF16)

    c1, c2 = D * 7 // 16, D * 13 // 16
    full = jnp.concatenate(
        [
            gather_by(final[:, :c1], ("outer", "inner", "cross"), n, n_head),
            gather_by(final[:, c1:c2], ("cross", "outer", "inner"), n, n_head),
            gather_by(final[:, c2:], ("inner", "cross", "outer"), n, n_head),
        ],
        axis=-1,
    ).reshape(n * 2 * rows, D)
    new_states = update_states(
        slot_of, arrived_kv.reshape(requests, 2 * steps, width).astype(F32), arrived, steps
    )
    best = greatest_entries(n, full, vocab_weight.T, vocab_other)
    best = jnp.take(best, jnp.arange(n) ^ r, axis=0)
    got = jnp.max(to_all(best, "req"), axis=0)
    got = lax.all_gather(got, "head", axis=0).reshape(n_head, 2, rows)
    crossed = jnp.stack([got[i ^ 2, 1] for i in range(n_head)])
    best = jnp.maximum(got[:, 0], crossed).reshape(requests, steps)
    index = (place % n_head) * group + place // n_head
    match = (index[:, None] == slots[None, :])[:, :, None]
    best = jnp.sum(jnp.where(match, best[None], 0.0), axis=1)
    live = jnp.arange(steps)[None, :] < token_count[:, None]
    greatest = jnp.max(jnp.where(live, best, -1e30), axis=1)

    blocks = hidden.reshape(rows, n_head, width).transpose(1, 0, 2)
    tail = jnp.broadcast_to(mean_square, (rows, 128))
    whole = []
    for e in range(n_head):
        block = lax.dynamic_index_in_dim(blocks, h ^ e, 0, keepdims=False)
        block = jnp.concatenate([block, tail], axis=1)
        whole.append(block if e == 0 else swap(block, "head", n_head, e))
    whole = jnp.stack(whole).reshape(requests, steps, width + 128)
    index = ((place % n_head) ^ h) * group + place // n_head
    whole = jnp.take(whole, index, axis=0, mode="clip")
    last = jnp.arange(steps)[None, :] == (token_count - 1)[:, None]
    last_norm = jnp.sqrt(jnp.sum(jnp.where(last, whole[:, :, width], 0.0), axis=1) + epsilon)

    return whole[:, :, :width], new_states, last_norm, greatest


def solution(mesh):
    placed = (
        P("req", None),
        P("req"),
        P("req"),
        P(),
        P("req", "head", None, None),
        P("req", "head"),
        P(),
        P(None, "head"),
        P(None, "head"),
        P(None, "head"),
        P("head"),
        P("head"),
        P("head", None),
        P(),
        P("head", "req"),
        P("head", "req"),
        P("req", "head"),
        P("head"),
        P(None, "head"),
        P(None, ("req", "head")),
    )
    return jax.shard_map(
        on_device,
        mesh=mesh,
        in_specs=placed,
        out_specs=(P("req", None, "head"), P("req", "head", None, None), P("req"), P("req")),
        check_vma=False,
    )
```

```python
import functools

import jax
import jax.numpy as jnp
import numpy as np
from jax import lax
from jax.experimental import pallas as pl
from jax.experimental.pallas import tpu as pltpu
from jax.sharding import PartitionSpec as P

D = 2048
HEAD_DIM = 128
epsilon = 1e-06
F32 = jnp.float32
BF16 = jnp.bfloat16
VMEM = pltpu.VMEM
SMEM = pltpu.SMEM


def swap(x, axis, size, offset):
    return lax.ppermute(x, axis, [(i, i ^ offset) for i in range(size)])


def bf16_parts(x):
    high = lax.reduce_precision(x, 8, 7)
    return high.astype(BF16), (x - high).astype(BF16)


def sort_kernel(sends, order_ref, old_ref, *rest):
    outs, (held, in_sems, out_sems) = rest[:-3], rest[-3:]
    owners = held.shape[0]
    spans, first = [], 0
    for out in outs:
        spans.append((first, out.shape[1]))
        first += out.shape[1]

    def load(owner, rank):
        at = owner * sends + rank
        return pltpu.make_async_copy(
            old_ref.at[order_ref[at]], held.at[owner, rank], in_sems.at[owner, rank]
        )

    def store(part):
        first, count = spans[part]
        return pltpu.make_async_copy(
            held.at[:, pl.ds(first, count)], outs[part], out_sems.at[part]
        )

    for first, count in spans:
        for owner in range(owners):
            for rank in range(first, first + count):
                load(owner, rank).start()
    for part, (first, count) in enumerate(spans):
        for owner in range(owners):
            for rank in range(first, first + count):
                load(owner, rank).wait()
        store(part).start()
    for part in range(len(outs)):
        store(part).wait()


def sort_states(order, old_states, owners, counts):
    sends = sum(counts)
    state = old_states.shape[1:]
    return pl.pallas_call(
        functools.partial(sort_kernel, sends),
        out_shape=[
            jax.ShapeDtypeStruct((owners, count) + state, old_states.dtype) for count in counts
        ],
        in_specs=[pl.BlockSpec(memory_space=SMEM), pl.BlockSpec(memory_space=pl.ANY)],
        out_specs=[pl.BlockSpec(memory_space=pl.ANY)] * len(counts),
        scratch_shapes=[
            VMEM((owners, sends) + state, old_states.dtype),
            pltpu.SemaphoreType.DMA((owners, sends)),
            pltpu.SemaphoreType.DMA((len(counts),)),
        ],
        compiler_params=pltpu.CompilerParams(vmem_limit_bytes=56 << 20),
    )(order, old_states)


def hand_on(*refs):
    pass


def after(x, *others, flops=0):
    anywhere = pl.BlockSpec(memory_space=pl.ANY)
    return pl.pallas_call(
        hand_on,
        out_shape=jax.ShapeDtypeStruct(x.shape, x.dtype),
        in_specs=[anywhere] * (1 + len(others)),
        out_specs=anywhere,
        input_output_aliases={0: 0},
        cost_estimate=pl.CostEstimate(flops=flops, bytes_accessed=0, transcendentals=0),
    )(x, *others)


def roll(x, by):
    return pltpu.roll(x, by % x.shape[0], 0)


def mixer_kernel(
    counts, owners, heads, classes, steps,
    me_ref, emb_ref, live_ref, gain_ref, floor_ref, ggain_ref, qw_hbm, fw_hbm, iw_hbm, ow_hbm,
    *rest,
):
    pieces, sends = len(counts), sum(counts)
    states_hbm = rest[:pieces]
    own_ref, kv_ref = rest[pieces : pieces + 2]
    parts = rest[pieces + 2 : pieces + 2 + classes]
    (qw_ref, fw_ref, iw_ref, ow_ref, states, qhi_ref, qlo_ref, mixed_ref, part_ref, sems) = rest[
        pieces + 2 + classes :
    ]
    weight_pairs = ((qw_hbm, qw_ref), (fw_hbm, fw_ref), (iw_hbm, iw_ref), (ow_hbm, ow_ref))
    loads = [
        pltpu.make_async_copy(there, here, sems.at[i]) for i, (there, here) in enumerate(weight_pairs)
    ]
    state_loads = [
        pltpu.make_async_copy(
            states_hbm[i], states.at[:, pl.ds(sum(counts[:i]), counts[i])], sems.at[4 + i]
        )
        for i in range(pieces)
    ]
    for load in loads[:3] + state_loads + loads[3:]:
        load.start()
    tokens = live_ref.shape[0]
    requests = tokens // steps
    group = requests // classes
    rows = group * steps
    stream = emb_ref[0:tokens, :].astype(F32)
    scale = lax.rsqrt(jnp.mean(stream * stream, axis=1, keepdims=True) + epsilon)
    normed = (stream * scale * gain_ref[...]).astype(BF16)
    loads[0].wait()
    query = jnp.dot(normed, qw_ref[...], preferred_element_type=F32)
    query = query * jax.nn.sigmoid(query) * HEAD_DIM ** (-0.5)
    loads[1].wait()
    forget_raw = jnp.dot(normed, fw_ref[...], preferred_element_type=F32)
    loads[2].wait()
    value = jnp.dot(normed, iw_ref[...], preferred_element_type=F32)
    floor = floor_ref[...]
    forget = jnp.where(
        live_ref[...] > 0.0, floor + (1.0 - floor) * jax.nn.sigmoid(forget_raw), 1.0
    )
    key = 1.0 - forget
    step = lax.broadcasted_iota(jnp.int32, forget.shape, 0) % steps
    upto = forget * jnp.where(step >= 1, roll(forget, 1), 1.0)
    upto = upto * jnp.where(step >= 2, roll(upto, 2), 1.0)
    after = jnp.where(step <= steps - 2, roll(forget, -1), 1.0)
    after = after * jnp.where(step <= steps - 3, roll(forget, -2), 1.0)
    after = after * jnp.where(step <= steps - 4, roll(forget, -3), 1.0)
    carried = query * upto
    high = carried.astype(BF16).astype(F32)
    qhi_ref[...] = high
    qlo_ref[...] = carried - high
    lag_key, lag_value = key, value
    local = [jnp.zeros((tokens, HEAD_DIM), F32) for _ in range(heads)]
    for lag in range(steps):
        if lag:
            lag_key = roll(lag_key, 1) * forget
            lag_value = roll(lag_value, 1)
        product = jnp.where(step >= lag, query * lag_key, 0.0)
        for head in range(heads):
            cols = slice(head * HEAD_DIM, (head + 1) * HEAD_DIM)
            weight = jnp.sum(product[:, cols], axis=1, keepdims=True)
            local[head] = local[head] + weight * lag_value[:, cols]
    for head in range(heads):
        mixed_ref[:, head * HEAD_DIM : (head + 1) * HEAD_DIM] = local[head]
    for load in state_loads:
        load.wait()
    here = me_ref[0]
    upper = lax.broadcasted_iota(jnp.int32, (8, HEAD_DIM), 0) < steps
    for tile in range(tokens // 8):
        for head in range(heads):
            cols = slice(head * HEAD_DIM, (head + 1) * HEAD_DIM)
            at = slice(tile * 8, tile * 8 + 8)
            left = jnp.concatenate([qhi_ref[at, cols], qlo_ref[at, cols]], axis=0).astype(BF16)
            got = []
            for request in (2 * tile, 2 * tile + 1):
                place = (request % group) * classes + request // group
                old = states[here ^ (place // sends), place % sends, head]
                product = jnp.dot(left, old, preferred_element_type=F32)
                got.append(product[0:8] + product[8:16])
            mixed_ref[at, cols] += jnp.where(upper, got[0], got[1])
    mixed = mixed_ref[...]
    square = jnp.sum(mixed * mixed, axis=1, keepdims=True)
    loads[3].wait()
    part_ref[:, 0:D] = jnp.dot(
        (mixed * ggain_ref[...]).astype(BF16), ow_ref[...], preferred_element_type=F32
    )
    square_high = square.astype(BF16).astype(F32)
    lane = lax.broadcasted_iota(jnp.int32, (tokens, 128), 1)
    part_ref[:, D : D + 128] = jnp.where(lane < 64, square_high, square - square_high)
    for e in range(classes):
        first = pl.multiple_of((me_ref[1] ^ e) * rows, rows)
        parts[e][...] = part_ref[pl.ds(first, rows), :].astype(BF16)
    own_ref[...] = emb_ref[pl.ds(pl.multiple_of(me_ref[1] * rows, rows), rows), :]
    both = jnp.concatenate([(key * after).astype(BF16), value.astype(BF16)], axis=0)
    shape = (2 * tokens, 2 * tokens)
    target = lax.broadcasted_iota(jnp.int32, shape, 0)
    source = lax.broadcasted_iota(jnp.int32, shape, 1)
    slot, within = target // (2 * steps), target % (2 * steps)
    place = ((slot // sends) ^ here) * sends + slot % sends
    request = (place % classes) * group + place // classes
    wanted = request * steps + within % steps + jnp.where(within >= steps, tokens, 0)
    pick = jnp.where(source == wanted, 1.0, 0.0).astype(BF16)
    kv_ref[...] = jnp.dot(pick, both, preferred_element_type=F32).astype(BF16)


def mixer(me, emb, live, gain, floor, ggain, weights, states, steps, classes):
    tokens = live.shape[0]
    counts = tuple(piece.shape[1] for piece in states)
    owners, _, heads = states[0].shape[:3]
    width = floor.shape[1]
    rows = tokens // classes
    vmem, anywhere = pl.BlockSpec(memory_space=VMEM), pl.BlockSpec(memory_space=pl.ANY)
    return pl.pallas_call(
        functools.partial(mixer_kernel, counts, owners, heads, classes, steps),
        out_shape=[
            jax.ShapeDtypeStruct((rows, D), BF16),
            jax.ShapeDtypeStruct((2 * tokens, width), BF16),
        ]
        + [jax.ShapeDtypeStruct((rows, D + 128), BF16)] * classes,
        in_specs=[pl.BlockSpec(memory_space=SMEM)] + [vmem] * 5 + [anywhere] * (4 + len(states)),
        out_specs=[vmem] * (2 + classes),
        scratch_shapes=[VMEM(w.shape, BF16) for w in weights]
        + [
            VMEM((owners, sum(counts)) + states[0].shape[2:], BF16),
            VMEM((tokens, width), F32),
            VMEM((tokens, width), F32),
            VMEM((tokens, width), F32),
            VMEM((tokens, D + 128), F32),
            pltpu.SemaphoreType.DMA((4 + len(states),)),
        ],
        compiler_params=pltpu.CompilerParams(vmem_limit_bytes=56 << 20),
    )(me, emb, live, gain, floor, ggain, *weights, *states)


def update_kernel(steps, slot_ref, kv_ref, *rest):
    states, out_ref = rest[:-1], rest[-1]
    owners, _, heads = states[0].shape[:3]
    ranks = [(piece, i) for piece in states for i in range(piece.shape[1])]
    sends = len(ranks)
    diagonal = lax.broadcasted_iota(jnp.int32, (HEAD_DIM, HEAD_DIM), 0) == lax.broadcasted_iota(
        jnp.int32, (HEAD_DIM, HEAD_DIM), 1
    )
    first = lax.broadcasted_iota(jnp.int32, (2 * steps, HEAD_DIM), 0) < steps
    for k in range(owners):
        for rank, (piece, i) in enumerate(ranks):
            place = k * sends + rank
            slot = slot_ref[place]
            for head in range(heads):
                cols = slice(head * HEAD_DIM, (head + 1) * HEAD_DIM)
                both = kv_ref[place, :, cols]
                key = jnp.where(first, both, 0.0)
                value = jnp.where(first, roll(both, steps), 0.0)
                kept = 1.0 - jnp.sum(key, axis=0, keepdims=True)
                keep = jnp.where(diagonal, kept, 0.0).astype(BF16)
                fresh = lax.dot_general(
                    key, value, (((0,), (0,)), ((), ())), preferred_element_type=F32
                )
                old = jnp.dot(keep, piece[k, i, head], preferred_element_type=F32)
                out_ref[slot, head] = (old + fresh).astype(BF16)


def update_states(slots, kv, states, steps):
    vmem = pl.BlockSpec(memory_space=VMEM)
    return pl.pallas_call(
        functools.partial(update_kernel, steps),
        out_shape=jax.ShapeDtypeStruct((slots.shape[0],) + states[0].shape[2:], BF16),
        in_specs=[pl.BlockSpec(memory_space=SMEM)] + [vmem] * (1 + len(states)),
        out_specs=vmem,
        compiler_params=pltpu.CompilerParams(vmem_limit_bytes=56 << 20),
    )(slots, kv, *states)


def dot_rows(a, b):
    return lax.dot_general(a, b, (((1,), (1,)), ((), ())), preferred_element_type=F32)


def feed_kernel(
    x_hbm, weights_hbm, pick_ref, mine_ref, gain_ref, down_ref, kept_ref, x, weights, feed, act, sems
):
    blocks, height, depth = weights.shape
    units = height // 3
    loads = [pltpu.make_async_copy(x_hbm, x, sems.at[3])]
    for i in range(3):
        span = pl.ds(i * units, units)
        loads.append(
            pltpu.make_async_copy(weights_hbm.at[:, span], weights.at[:, span], sems.at[i])
        )
    for load in loads:
        load.start()
    loads[0].wait()
    stream = x[...].astype(F32)
    scale = lax.rsqrt(jnp.mean(stream * stream, axis=1, keepdims=True) + epsilon)
    feed[...] = (stream * scale * gain_ref[...]).astype(BF16)
    kept_ref[...] = jnp.dot(mine_ref[...], x[...], preferred_element_type=F32).astype(BF16)
    loads[1].wait()
    loads[2].wait()
    for first in range(0, units, 256):
        last = min(first + 256, units)
        gate = up = 0.0
        for b in range(blocks):
            part = feed[:, b * depth : (b + 1) * depth]
            gate += dot_rows(part, weights[b, first:last, :])
            up += dot_rows(part, weights[b, units + first : units + last, :])
        act[:, first:last] = (gate * jax.nn.sigmoid(gate) * up).astype(BF16)
    placed = jnp.dot(pick_ref[...], act[...], preferred_element_type=F32).astype(BF16)
    loads[3].wait()
    for b in range(blocks):
        down_ref[:, b * depth : (b + 1) * depth] = jnp.dot(
            placed, weights[b, 2 * units :, :], preferred_element_type=F32
        ).astype(BF16)


def feed_forward(x, weights, pick, mine, gain):
    vmem, anywhere = pl.BlockSpec(memory_space=VMEM), pl.BlockSpec(memory_space=pl.ANY)
    tokens, width = x.shape
    return pl.pallas_call(
        feed_kernel,
        out_shape=[
            jax.ShapeDtypeStruct((tokens, width), BF16),
            jax.ShapeDtypeStruct((mine.shape[0], width), BF16),
        ],
        in_specs=[anywhere] * 2 + [vmem] * 3,
        out_specs=[vmem] * 2,
        scratch_shapes=[
            VMEM(x.shape, BF16),
            VMEM(weights.shape, BF16),
            VMEM(x.shape, BF16),
            VMEM((tokens, weights.shape[1] // 3), BF16),
            pltpu.SemaphoreType.DMA((4,)),
        ],
        cost_estimate=pl.CostEstimate(
            flops=32 * tokens * weights.size, bytes_accessed=2 * weights.size, transcendentals=0
        ),
        compiler_params=pltpu.CompilerParams(vmem_limit_bytes=58 << 20),
    )(x, weights, pick, mine, gain)


def greatest_kernel(me_ref, full_hbm, own_hbm, other_hbm, best_ref, full, own, other, sems):
    loads = [
        pltpu.make_async_copy(there, here, sems.at[i])
        for i, (there, here) in enumerate(((full_hbm, full), (own_hbm, own), (other_hbm, other)))
    ]
    for load in loads:
        load.start()
    loads[0].wait()
    best = None
    for i, table in enumerate((own, other)):
        loads[1 + i].wait()
        height = table.shape[0]
        for first in range(0, height, 256):
            entries = dot_rows(table[first : min(first + 256, height), :], full[...])
            top = jnp.max(entries, axis=0, keepdims=True)
            best = top if best is None else jnp.maximum(best, top)
    width = best_ref.shape[1]
    for k in range(best_ref.shape[0]):
        best_ref[pl.ds(me_ref[0] ^ k, 1), :] = best[:, k * width : (k + 1) * width]


def greatest_entries(me, blocks, full, own, other):
    anywhere = pl.BlockSpec(memory_space=pl.ANY)
    return pl.pallas_call(
        greatest_kernel,
        out_shape=jax.ShapeDtypeStruct((blocks, full.shape[0] // blocks), F32),
        in_specs=[pl.BlockSpec(memory_space=SMEM)] + [anywhere] * 3,
        out_specs=pl.BlockSpec(memory_space=VMEM),
        scratch_shapes=[VMEM(x.shape, BF16) for x in (full, own, other)]
        + [pltpu.SemaphoreType.DMA((3,))],
        cost_estimate=pl.CostEstimate(
            flops=8 * full.shape[0] * own.size, bytes_accessed=4 * own.size, transcendentals=0
        ),
        compiler_params=pltpu.CompilerParams(vmem_limit_bytes=58 << 20),
    )(me, full, own, other)


def exchange(block, dim, n, n_head):
    if dim == "outer":
        got = [swap(block, "req", n, 2 * j) for j in range(1, n // 2)]
    elif dim == "inner":
        got = [swap(block, "req", n, 1)]
    else:
        got = [swap(block, "head", n_head, 2)]
    return jnp.stack([block] + got)


def gather_by(block, dims, n, n_head):
    rank = block.ndim
    for dim in dims:
        block = exchange(block, dim, n, n_head)
    at = [dims[::-1].index(dim) for dim in ("outer", "inner", "cross")]
    return block.transpose(at + list(range(len(dims), len(dims) + rank)))


def to_all(x, axis):
    return lax.all_to_all(x, axis, split_axis=0, concat_axis=0, tiled=True)


def on_device(
    token_ids, state_perm, token_count, tenant_bounds, old_states, embedding, mixer_gain,
    query_weight, forget_weight, input_weight, forget_floor, group_gain, output_weight, feed_gain,
    gate_weight, up_weight, down_weight, final_gain, tenant_gain, vocab_weight,
):
    requests, steps = token_ids.shape
    n = lax.axis_size("req")
    n_head = lax.axis_size("head")
    r = lax.axis_index("req")
    h = lax.axis_index("head")
    tokens = requests * steps
    everyone = requests * n
    sends = requests // n
    group = requests // n_head
    rows = group * steps
    width = D // n_head

    feed_weights = jnp.concatenate([gate_weight.T, up_weight.T, down_weight], axis=0)
    feed_weights = lax.all_gather(feed_weights, "head", axis=0)

    packed = jnp.concatenate([token_ids.T, state_perm[None], token_count[None]], axis=0)
    packed = to_all(jnp.broadcast_to(packed[None], (n,) + packed.shape), "req").transpose(1, 0, 2).reshape(steps + 2, everyone)
    every = jnp.arange(everyone, dtype=jnp.int32)
    source = packed[steps] // requests
    rank = jnp.sum(
        ((source[None, :] == source[:, None]) & (every[None, :] < every[:, None])).astype(jnp.int32),
        axis=1,
    )
    place = ((every // requests) ^ source) * sends + rank % sends
    at = source * requests + (place % n_head) * group + place // n_head
    chosen = (at[:, None] == every[None, :]).astype(F32)
    ordered = jnp.dot(packed.astype(F32), chosen, precision=lax.Precision.HIGHEST)
    ordered = (ordered + 0.5).astype(jnp.int32)

    ids = ordered[:steps].T.reshape(n, tokens)
    table = embedding.shape[0]
    room = tokens * 3 // 8
    holder = lax.div(ids, jnp.int32(table))
    held = holder == r
    earlier = jnp.triu(jnp.ones((tokens, tokens), BF16), 1)
    turn = jnp.dot(held.astype(BF16), earlier, preferred_element_type=F32).astype(jnp.int32)
    local_ids = jnp.where(held, ids - r * table, 0)
    seat = held[:, None] & (turn[:, None] == jnp.arange(room, dtype=jnp.int32)[None, :, None])
    wanted = jnp.sum(jnp.where(seat, local_ids[:, None], 0), axis=2).reshape(n * room)
    got = to_all(jnp.take(embedding, wanted, axis=0, mode="clip").reshape(n, room, width), "req")
    own_holder = lax.dynamic_index_in_dim(holder, r, 0, keepdims=False)
    order = jnp.arange(tokens, dtype=jnp.int32)
    own_turn = jnp.sum(
        ((own_holder[None, :] == own_holder[:, None]) & (order[None, :] < order[:, None])).astype(
            jnp.int32
        ),
        axis=1,
    )
    seat = jnp.where(own_turn < room, own_holder * room + own_turn, -1)
    pick = (seat[:, None] == jnp.arange(n * room, dtype=jnp.int32)[None, :]).astype(BF16)
    embed_part = jnp.dot(
        pick, got.reshape(n * room, width), preferred_element_type=F32
    ).astype(BF16)
    owners = jnp.arange(n, dtype=jnp.int32)
    load = jnp.sum((holder[:, None] == owners[None, :, None]).astype(jnp.int32), axis=2)

    def with_rest(part):
        rows = jnp.take(embedding, local_ids.reshape(n * tokens), axis=0, mode="clip")
        rest = (held & (turn >= room)).reshape(n * tokens, 1)
        rows = jnp.where(rest, rows, jnp.zeros((), BF16)).reshape(n, tokens, width)
        return (part.astype(F32) + jnp.sum(to_all(rows, "req").astype(F32), axis=0)).astype(BF16)

    embed_part = lax.cond(jnp.max(load) > room, with_rest, lambda part: part, embed_part)
    vocab_other = swap(vocab_weight.T, "head", n_head, 1)

    gains = jnp.concatenate([final_gain[None], tenant_gain], axis=0)
    gains_high, gains_low = bf16_parts(gains)
    extra = jnp.zeros((16 - 2 * gains.shape[0], width), BF16)
    embedded = lax.all_gather(
        jnp.concatenate([embed_part, gains_high, gains_low, extra], axis=0), "head", axis=1, tiled=True
    )
    gains = embedded[tokens : tokens + 5].astype(F32) + embedded[tokens + 5 : tokens + 10].astype(F32)

    ordered = lax.dynamic_slice_in_dim(ordered, r * requests, requests, 1)
    old_order = (ordered[steps] - r * requests).reshape(n_head, group).T.reshape(n, sends)
    old_order = jnp.take(old_order, jnp.arange(n) ^ r, axis=0).reshape(requests)
    counts = (2, 2) if sends == 4 else (sends,)
    pieces = sort_states(old_order, old_states, n, counts)
    live = (jnp.arange(steps)[None, :] < ordered[steps + 1][:, None]).astype(F32)
    own, kv, *parts = mixer(
        jnp.stack([r, h]), embedded, live.reshape(tokens, 1), mixer_gain[None], forget_floor[None],
        group_gain[None], (query_weight, forget_weight, input_weight, output_weight), pieces,
        steps, n_head,
    )
    arrived = [to_all(pieces[0], "req")]

    total = parts[0].astype(F32)
    for e in range(1, n_head):
        total = total + swap(parts[e], "head", n_head, e).astype(F32)
    square = total[:, D : D + 1] + total[:, D + 127 : D + 128]
    after_mixer = own.astype(F32) + total[:, :D] * lax.rsqrt(square / D + epsilon)
    after_mixer = after(after_mixer.astype(BF16), feed_weights)
    everything = lax.all_gather(after_mixer, "req", axis=0, tiled=True)
    for piece in pieces[1:]:
        piece = after(piece, after_mixer, *arrived, flops=50_000_000_000)
        arrived += [to_all(piece, "req")]

    row = jnp.arange(n * rows, dtype=jnp.int32)
    by_owner, by_group, by_step = row // rows, (row % rows) // steps, row % steps
    if sends % n_head == 0:
        offset = by_group * n_head // sends
    else:
        offset = (by_group * n_head + h) // sends
    wanted = (by_owner ^ offset) * rows + by_group * steps + by_step
    pick = (wanted[None, :] == row[:, None]).astype(BF16)
    mine = (wanted[None, :] == (r * rows + row[:rows])[:, None]).astype(BF16)
    down, kept = feed_forward(everything, feed_weights, pick, mine, feed_gain[None])
    down = after(down, *arrived)
    hidden = kept.astype(F32) + jnp.sum(to_all(down.reshape(n, rows, D), "req").astype(F32), axis=0)
    mean_square = jnp.mean(hidden * hidden, axis=1, keepdims=True)

    slots = jnp.arange(requests, dtype=jnp.int32)
    source = state_perm // requests
    rank = jnp.sum(
        ((source[None, :] == source[:, None]) & (slots[None, :] < slots[:, None])).astype(jnp.int32),
        axis=1,
    )
    place = (source ^ r) * sends + rank
    natural = source * sends + rank
    slot_of = jnp.sum(jnp.where(natural[None, :] == slots[:, None], slots[None, :], 0), axis=1)
    mine = jnp.sum(
        jnp.where(
            place[None, :] == (jnp.arange(group, dtype=jnp.int32) * n_head + h)[:, None],
            slots[None, :],
            0,
        ),
        axis=1,
    )
    tenant = jnp.sum(
        ((mine + r * requests)[:, None] >= tenant_bounds[None, 1:-1]).astype(jnp.int32), axis=1
    )
    tenant_rows = sum(
        jnp.where((tenant == t)[:, None], gains[1 + t][None, :], 0.0)
        for t in range(tenant_gain.shape[0])
    )
    token_gain = jnp.repeat(tenant_rows * gains[0][None, :], steps, axis=0)
    final = (hidden * lax.rsqrt(mean_square + epsilon) * token_gain).astype(BF16)

    c1, c2 = D * 7 // 16, D * 13 // 16
    full = jnp.concatenate(
        [
            gather_by(final[:, :c1], ("outer", "inner", "cross"), n, n_head),
            gather_by(final[:, c1:c2], ("cross", "outer", "inner"), n, n_head),
            gather_by(final[:, c2:], ("inner", "cross", "outer"), n, n_head),
        ],
        axis=-1,
    ).reshape(n * 2 * rows, D)
    arrived_kv = to_all(after(kv, full).reshape(n, -1, width), "req")
    new_states = update_states(
        slot_of, arrived_kv.reshape(requests, 2 * steps, width).astype(F32), arrived, steps
    )
    best = greatest_entries(r[None], n, full, vocab_weight.T, vocab_other)
    got = jnp.max(to_all(after(best, arrived_kv), "req"), axis=0)
    got = lax.all_gather(got, "head", axis=0).reshape(n_head, 2, rows)
    crossed = jnp.stack([got[i ^ 2, 1] for i in range(n_head)])
    best = jnp.maximum(got[:, 0], crossed).reshape(requests, steps)
    index = (place % n_head) * group + place // n_head
    match = (index[:, None] == slots[None, :])[:, :, None]
    best = jnp.sum(jnp.where(match, best[None], 0.0), axis=1)
    live = jnp.arange(steps)[None, :] < token_count[:, None]
    greatest = jnp.max(jnp.where(live, best, -1e30), axis=1)

    blocks = hidden.reshape(rows, n_head, width).transpose(1, 0, 2)
    tail = jnp.broadcast_to(mean_square, (rows, 128))
    whole = []
    for e in range(n_head):
        block = lax.dynamic_index_in_dim(blocks, h ^ e, 0, keepdims=False)
        block = jnp.concatenate([block, tail], axis=1)
        whole.append(block if e == 0 else swap(block, "head", n_head, e))
    whole = jnp.stack(whole).reshape(requests, steps, width + 128)
    index = ((place % n_head) ^ h) * group + place // n_head
    whole = jnp.take(whole, index, axis=0, mode="clip")
    last = jnp.arange(steps)[None, :] == (token_count - 1)[:, None]
    last_norm = jnp.sqrt(jnp.sum(jnp.where(last, whole[:, :, width], 0.0), axis=1) + epsilon)

    return whole[:, :, :width], new_states, last_norm, greatest


def solution(mesh):
    placed = (
        P("req", None),
        P("req"),
        P("req"),
        P(),
        P("req", "head", None, None),
        P("req", "head"),
        P(),
        P(None, "head"),
        P(None, "head"),
        P(None, "head"),
        P("head"),
        P("head"),
        P("head", None),
        P(),
        P("head", "req"),
        P("head", "req"),
        P("req", "head"),
        P("head"),
        P(None, "head"),
        P(None, ("req", "head")),
    )
    return jax.shard_map(
        on_device,
        mesh=mesh,
        in_specs=placed,
        out_specs=(P("req", None, "head"), P("req", "head", None, None), P("req"), P("req")),
        check_vma=False,
    )
```

```python
import functools

import jax
import jax.numpy as jnp
import numpy as np
from jax import lax
from jax.experimental import pallas as pl
from jax.experimental.pallas import tpu as pltpu
from jax.sharding import PartitionSpec as P

D = 2048
HEAD_DIM = 128
epsilon = 1e-06
F32 = jnp.float32
BF16 = jnp.bfloat16
VMEM = pltpu.VMEM
SMEM = pltpu.SMEM


def swap(x, axis, size, offset):
    return lax.ppermute(x, axis, [(i, i ^ offset) for i in range(size)])


def bf16_parts(x):
    high = lax.reduce_precision(x, 8, 7)
    return high.astype(BF16), (x - high).astype(BF16)


def sort_kernel(sends, order_ref, old_ref, *rest):
    outs, (held, in_sems, out_sems) = rest[:-3], rest[-3:]
    owners = held.shape[0]
    spans, first = [], 0
    for out in outs:
        spans.append((first, out.shape[1]))
        first += out.shape[1]

    def load(owner, rank):
        at = owner * sends + rank
        return pltpu.make_async_copy(
            old_ref.at[order_ref[at]], held.at[owner, rank], in_sems.at[owner, rank]
        )

    def store(part):
        first, count = spans[part]
        return pltpu.make_async_copy(
            held.at[:, pl.ds(first, count)], outs[part], out_sems.at[part]
        )

    for first, count in spans:
        for owner in range(owners):
            for rank in range(first, first + count):
                load(owner, rank).start()
    for part, (first, count) in enumerate(spans):
        for owner in range(owners):
            for rank in range(first, first + count):
                load(owner, rank).wait()
        store(part).start()
    for part in range(len(outs)):
        store(part).wait()


def sort_states(order, old_states, owners, counts):
    sends = sum(counts)
    state = old_states.shape[1:]
    return pl.pallas_call(
        functools.partial(sort_kernel, sends),
        out_shape=[
            jax.ShapeDtypeStruct((owners, count) + state, old_states.dtype) for count in counts
        ],
        in_specs=[pl.BlockSpec(memory_space=SMEM), pl.BlockSpec(memory_space=pl.ANY)],
        out_specs=[pl.BlockSpec(memory_space=pl.ANY)] * len(counts),
        scratch_shapes=[
            VMEM((owners, sends) + state, old_states.dtype),
            pltpu.SemaphoreType.DMA((owners, sends)),
            pltpu.SemaphoreType.DMA((len(counts),)),
        ],
        compiler_params=pltpu.CompilerParams(vmem_limit_bytes=56 << 20),
    )(order, old_states)


def hand_on(*refs):
    pass


def after(x, *others, flops=0):
    anywhere = pl.BlockSpec(memory_space=pl.ANY)
    return pl.pallas_call(
        hand_on,
        out_shape=jax.ShapeDtypeStruct(x.shape, x.dtype),
        in_specs=[anywhere] * (1 + len(others)),
        out_specs=anywhere,
        input_output_aliases={0: 0},
        cost_estimate=pl.CostEstimate(flops=flops, bytes_accessed=0, transcendentals=0),
    )(x, *others)


def roll(x, by):
    return pltpu.roll(x, by % x.shape[0], 0)


def mixer_kernel(
    counts, owners, heads, classes, steps,
    me_ref, emb_ref, live_ref, gain_ref, floor_ref, ggain_ref, qw_hbm, fw_hbm, iw_hbm, ow_hbm,
    *rest,
):
    pieces, sends = len(counts), sum(counts)
    states_hbm = rest[:pieces]
    own_ref, kv_ref = rest[pieces : pieces + 2]
    parts = rest[pieces + 2 : pieces + 2 + classes]
    (qw_ref, fw_ref, iw_ref, ow_ref, states, qhi_ref, qlo_ref, mixed_ref, part_ref, sems) = rest[
        pieces + 2 + classes :
    ]
    weight_pairs = ((qw_hbm, qw_ref), (fw_hbm, fw_ref), (iw_hbm, iw_ref), (ow_hbm, ow_ref))
    loads = [
        pltpu.make_async_copy(there, here, sems.at[i]) for i, (there, here) in enumerate(weight_pairs)
    ]
    state_loads = [
        pltpu.make_async_copy(
            states_hbm[i], states.at[:, pl.ds(sum(counts[:i]), counts[i])], sems.at[4 + i]
        )
        for i in range(pieces)
    ]
    for load in loads[:3] + state_loads + loads[3:]:
        load.start()
    tokens = live_ref.shape[0]
    requests = tokens // steps
    group = requests // classes
    rows = group * steps
    stream = emb_ref[0:tokens, :].astype(F32)
    scale = lax.rsqrt(jnp.mean(stream * stream, axis=1, keepdims=True) + epsilon)
    normed = (stream * scale * gain_ref[...]).astype(BF16)
    loads[0].wait()
    query = jnp.dot(normed, qw_ref[...], preferred_element_type=F32)
    query = query * jax.nn.sigmoid(query) * HEAD_DIM ** (-0.5)
    loads[1].wait()
    forget_raw = jnp.dot(normed, fw_ref[...], preferred_element_type=F32)
    loads[2].wait()
    value = jnp.dot(normed, iw_ref[...], preferred_element_type=F32)
    floor = floor_ref[...]
    forget = jnp.where(
        live_ref[...] > 0.0, floor + (1.0 - floor) * jax.nn.sigmoid(forget_raw), 1.0
    )
    key = 1.0 - forget
    step = lax.broadcasted_iota(jnp.int32, forget.shape, 0) % steps
    upto = forget * jnp.where(step >= 1, roll(forget, 1), 1.0)
    upto = upto * jnp.where(step >= 2, roll(upto, 2), 1.0)
    after = jnp.where(step <= steps - 2, roll(forget, -1), 1.0)
    after = after * jnp.where(step <= steps - 3, roll(forget, -2), 1.0)
    after = after * jnp.where(step <= steps - 4, roll(forget, -3), 1.0)
    carried = query * upto
    high = carried.astype(BF16).astype(F32)
    qhi_ref[...] = high
    qlo_ref[...] = carried - high
    lag_key, lag_value = key, value
    local = [jnp.zeros((tokens, HEAD_DIM), F32) for _ in range(heads)]
    for lag in range(steps):
        if lag:
            lag_key = roll(lag_key, 1) * forget
            lag_value = roll(lag_value, 1)
        product = jnp.where(step >= lag, query * lag_key, 0.0)
        for head in range(heads):
            cols = slice(head * HEAD_DIM, (head + 1) * HEAD_DIM)
            weight = jnp.sum(product[:, cols], axis=1, keepdims=True)
            local[head] = local[head] + weight * lag_value[:, cols]
    for head in range(heads):
        mixed_ref[:, head * HEAD_DIM : (head + 1) * HEAD_DIM] = local[head]
    for load in state_loads:
        load.wait()
    here = me_ref[0]
    upper = lax.broadcasted_iota(jnp.int32, (8, HEAD_DIM), 0) < steps
    for tile in range(tokens // 8):
        for head in range(heads):
            cols = slice(head * HEAD_DIM, (head + 1) * HEAD_DIM)
            at = slice(tile * 8, tile * 8 + 8)
            left = jnp.concatenate([qhi_ref[at, cols], qlo_ref[at, cols]], axis=0).astype(BF16)
            got = []
            for request in (2 * tile, 2 * tile + 1):
                place = (request % group) * classes + request // group
                old = states[here ^ (place // sends), place % sends, head]
                product = jnp.dot(left, old, preferred_element_type=F32)
                got.append(product[0:8] + product[8:16])
            mixed_ref[at, cols] += jnp.where(upper, got[0], got[1])
    mixed = mixed_ref[...]
    square = jnp.sum(mixed * mixed, axis=1, keepdims=True)
    loads[3].wait()
    part_ref[:, 0:D] = jnp.dot(
        (mixed * ggain_ref[...]).astype(BF16), ow_ref[...], preferred_element_type=F32
    )
    square_high = square.astype(BF16).astype(F32)
    lane = lax.broadcasted_iota(jnp.int32, (tokens, 128), 1)
    part_ref[:, D : D + 128] = jnp.where(lane < 64, square_high, square - square_high)
    for e in range(classes):
        first = pl.multiple_of((me_ref[1] ^ e) * rows, rows)
        parts[e][...] = part_ref[pl.ds(first, rows), :].astype(BF16)
    own_ref[...] = emb_ref[pl.ds(pl.multiple_of(me_ref[1] * rows, rows), rows), :]
    both = jnp.concatenate([(key * after).astype(BF16), value.astype(BF16)], axis=0)
    shape = (2 * tokens, 2 * tokens)
    target = lax.broadcasted_iota(jnp.int32, shape, 0)
    source = lax.broadcasted_iota(jnp.int32, shape, 1)
    place, within = target // (2 * steps), target % (2 * steps)
    request = (place % classes) * group + place // classes
    wanted = request * steps + within % steps + jnp.where(within >= steps, tokens, 0)
    pick = jnp.where(source == wanted, 1.0, 0.0).astype(BF16)
    kv_ref[...] = jnp.dot(pick, both, preferred_element_type=F32).astype(BF16)


def mixer(me, emb, live, gain, floor, ggain, weights, states, steps, classes):
    tokens = live.shape[0]
    counts = tuple(piece.shape[1] for piece in states)
    owners, _, heads = states[0].shape[:3]
    width = floor.shape[1]
    rows = tokens // classes
    vmem, anywhere = pl.BlockSpec(memory_space=VMEM), pl.BlockSpec(memory_space=pl.ANY)
    return pl.pallas_call(
        functools.partial(mixer_kernel, counts, owners, heads, classes, steps),
        out_shape=[
            jax.ShapeDtypeStruct((rows, D), BF16),
            jax.ShapeDtypeStruct((2 * tokens, width), BF16),
        ]
        + [jax.ShapeDtypeStruct((rows, D + 128), BF16)] * classes,
        in_specs=[pl.BlockSpec(memory_space=SMEM)] + [vmem] * 5 + [anywhere] * (4 + len(states)),
        out_specs=[vmem] * (2 + classes),
        scratch_shapes=[VMEM(w.shape, BF16) for w in weights]
        + [
            VMEM((owners, sum(counts)) + states[0].shape[2:], BF16),
            VMEM((tokens, width), F32),
            VMEM((tokens, width), F32),
            VMEM((tokens, width), F32),
            VMEM((tokens, D + 128), F32),
            pltpu.SemaphoreType.DMA((4 + len(states),)),
        ],
        compiler_params=pltpu.CompilerParams(vmem_limit_bytes=56 << 20),
    )(me, emb, live, gain, floor, ggain, *weights, *states)


def update_kernel(steps, me_ref, slot_ref, kv_ref, *rest):
    states, out_ref = rest[:-1], rest[-1]
    owners, _, heads = states[0].shape[:3]
    ranks = [(piece, i) for piece in states for i in range(piece.shape[1])]
    sends = len(ranks)
    diagonal = lax.broadcasted_iota(jnp.int32, (HEAD_DIM, HEAD_DIM), 0) == lax.broadcasted_iota(
        jnp.int32, (HEAD_DIM, HEAD_DIM), 1
    )
    first = lax.broadcasted_iota(jnp.int32, (2 * steps, HEAD_DIM), 0) < steps
    for k in range(owners):
        for rank, (piece, i) in enumerate(ranks):
            place = k * sends + rank
            slot = slot_ref[place]
            for head in range(heads):
                cols = slice(head * HEAD_DIM, (head + 1) * HEAD_DIM)
                both = kv_ref[(k ^ me_ref[0]) * sends + rank, :, cols]
                key = jnp.where(first, both, 0.0)
                value = jnp.where(first, roll(both, steps), 0.0)
                kept = 1.0 - jnp.sum(key, axis=0, keepdims=True)
                keep = jnp.where(diagonal, kept, 0.0).astype(BF16)
                fresh = lax.dot_general(
                    key, value, (((0,), (0,)), ((), ())), preferred_element_type=F32
                )
                old = jnp.dot(keep, piece[k, i, head], preferred_element_type=F32)
                out_ref[slot, head] = (old + fresh).astype(BF16)


def update_states(me, slots, kv, states, steps):
    vmem = pl.BlockSpec(memory_space=VMEM)
    return pl.pallas_call(
        functools.partial(update_kernel, steps),
        out_shape=jax.ShapeDtypeStruct((slots.shape[0],) + states[0].shape[2:], BF16),
        in_specs=[pl.BlockSpec(memory_space=SMEM)] * 2 + [vmem] * (1 + len(states)),
        out_specs=vmem,
        compiler_params=pltpu.CompilerParams(vmem_limit_bytes=56 << 20),
    )(me, slots, kv, *states)


def dot_rows(a, b):
    return lax.dot_general(a, b, (((1,), (1,)), ((), ())), preferred_element_type=F32)


def feed_kernel(
    x_hbm, weights_hbm, pick_ref, mine_ref, gain_ref, down_ref, kept_ref, x, weights, feed, act, sems
):
    blocks, height, depth = weights.shape
    units = height // 3
    loads = [pltpu.make_async_copy(x_hbm, x, sems.at[3])]
    for i in range(3):
        span = pl.ds(i * units, units)
        loads.append(
            pltpu.make_async_copy(weights_hbm.at[:, span], weights.at[:, span], sems.at[i])
        )
    for load in loads:
        load.start()
    loads[0].wait()
    stream = x[...].astype(F32)
    scale = lax.rsqrt(jnp.mean(stream * stream, axis=1, keepdims=True) + epsilon)
    feed[...] = (stream * scale * gain_ref[...]).astype(BF16)
    kept_ref[...] = jnp.dot(mine_ref[...], x[...], preferred_element_type=F32).astype(BF16)
    loads[1].wait()
    loads[2].wait()
    for first in range(0, units, 256):
        last = min(first + 256, units)
        gate = up = 0.0
        for b in range(blocks):
            part = feed[:, b * depth : (b + 1) * depth]
            gate += dot_rows(part, weights[b, first:last, :])
            up += dot_rows(part, weights[b, units + first : units + last, :])
        act[:, first:last] = (gate * jax.nn.sigmoid(gate) * up).astype(BF16)
    placed = jnp.dot(pick_ref[...], act[...], preferred_element_type=F32).astype(BF16)
    loads[3].wait()
    for b in range(blocks):
        down_ref[:, b * depth : (b + 1) * depth] = jnp.dot(
            placed, weights[b, 2 * units :, :], preferred_element_type=F32
        ).astype(BF16)


def feed_forward(x, weights, pick, mine, gain):
    vmem, anywhere = pl.BlockSpec(memory_space=VMEM), pl.BlockSpec(memory_space=pl.ANY)
    tokens, width = x.shape
    return pl.pallas_call(
        feed_kernel,
        out_shape=[
            jax.ShapeDtypeStruct((tokens, width), BF16),
            jax.ShapeDtypeStruct((mine.shape[0], width), BF16),
        ],
        in_specs=[anywhere] * 2 + [vmem] * 3,
        out_specs=[vmem] * 2,
        scratch_shapes=[
            VMEM(x.shape, BF16),
            VMEM(weights.shape, BF16),
            VMEM(x.shape, BF16),
            VMEM((tokens, weights.shape[1] // 3), BF16),
            pltpu.SemaphoreType.DMA((4,)),
        ],
        cost_estimate=pl.CostEstimate(
            flops=32 * tokens * weights.size, bytes_accessed=2 * weights.size, transcendentals=0
        ),
        compiler_params=pltpu.CompilerParams(vmem_limit_bytes=58 << 20),
    )(x, weights, pick, mine, gain)


def greatest_kernel(me_ref, full_hbm, own_hbm, other_hbm, best_ref, full, own, other, sems):
    loads = [
        pltpu.make_async_copy(there, here, sems.at[i])
        for i, (there, here) in enumerate(((full_hbm, full), (own_hbm, own), (other_hbm, other)))
    ]
    for load in loads:
        load.start()
    loads[0].wait()
    best = None
    for i, table in enumerate((own, other)):
        loads[1 + i].wait()
        height = table.shape[0]
        for first in range(0, height, 256):
            entries = dot_rows(table[first : min(first + 256, height), :], full[...])
            top = jnp.max(entries, axis=0, keepdims=True)
            best = top if best is None else jnp.maximum(best, top)
    width = best_ref.shape[1]
    for k in range(best_ref.shape[0]):
        best_ref[pl.ds(me_ref[0] ^ k, 1), :] = best[:, k * width : (k + 1) * width]


def greatest_entries(me, blocks, full, own, other):
    anywhere = pl.BlockSpec(memory_space=pl.ANY)
    return pl.pallas_call(
        greatest_kernel,
        out_shape=jax.ShapeDtypeStruct((blocks, full.shape[0] // blocks), F32),
        in_specs=[pl.BlockSpec(memory_space=SMEM)] + [anywhere] * 3,
        out_specs=pl.BlockSpec(memory_space=VMEM),
        scratch_shapes=[VMEM(x.shape, BF16) for x in (full, own, other)]
        + [pltpu.SemaphoreType.DMA((3,))],
        cost_estimate=pl.CostEstimate(
            flops=8 * full.shape[0] * own.size, bytes_accessed=4 * own.size, transcendentals=0
        ),
        compiler_params=pltpu.CompilerParams(vmem_limit_bytes=58 << 20),
    )(me, full, own, other)


def exchange(block, dim, n, n_head):
    if dim == "outer":
        got = [swap(block, "req", n, 2 * j) for j in range(1, n // 2)]
    elif dim == "inner":
        got = [swap(block, "req", n, 1)]
    else:
        got = [swap(block, "head", n_head, 2)]
    return jnp.stack([block] + got)


def gather_by(block, dims, n, n_head):
    rank = block.ndim
    for dim in dims:
        block = exchange(block, dim, n, n_head)
    at = [dims[::-1].index(dim) for dim in ("outer", "inner", "cross")]
    return block.transpose(at + list(range(len(dims), len(dims) + rank)))


def to_all(x, axis):
    return lax.all_to_all(x, axis, split_axis=0, concat_axis=0, tiled=True)


def on_device(
    token_ids, state_perm, token_count, tenant_bounds, old_states, embedding, mixer_gain,
    query_weight, forget_weight, input_weight, forget_floor, group_gain, output_weight, feed_gain,
    gate_weight, up_weight, down_weight, final_gain, tenant_gain, vocab_weight,
):
    requests, steps = token_ids.shape
    n = lax.axis_size("req")
    n_head = lax.axis_size("head")
    r = lax.axis_index("req")
    h = lax.axis_index("head")
    tokens = requests * steps
    everyone = requests * n
    sends = requests // n
    group = requests // n_head
    rows = group * steps
    width = D // n_head

    feed_weights = jnp.concatenate([gate_weight.T, up_weight.T, down_weight], axis=0)
    feed_weights = lax.all_gather(feed_weights, "head", axis=0)

    packed = jnp.concatenate([token_ids.T, state_perm[None], token_count[None]], axis=0)
    packed = to_all(jnp.broadcast_to(packed[None], (n,) + packed.shape), "req").transpose(1, 0, 2).reshape(steps + 2, everyone)
    every = jnp.arange(everyone, dtype=jnp.int32)
    source = packed[steps] // requests
    rank = jnp.sum(
        ((source[None, :] == source[:, None]) & (every[None, :] < every[:, None])).astype(jnp.int32),
        axis=1,
    )
    place = ((every // requests) ^ source) * sends + rank % sends
    at = source * requests + (place % n_head) * group + place // n_head
    chosen = (at[:, None] == every[None, :]).astype(F32)
    ordered = jnp.dot(packed.astype(F32), chosen, precision=lax.Precision.HIGHEST)
    ordered = (ordered + 0.5).astype(jnp.int32)

    ids = ordered[:steps].T.reshape(n, tokens)
    table = embedding.shape[0]
    room = tokens * 3 // 8
    holder = lax.div(ids, jnp.int32(table))
    held = holder == r
    earlier = jnp.triu(jnp.ones((tokens, tokens), BF16), 1)
    turn = jnp.dot(held.astype(BF16), earlier, preferred_element_type=F32).astype(jnp.int32)
    local_ids = jnp.where(held, ids - r * table, 0)
    seat = held[:, None] & (turn[:, None] == jnp.arange(room, dtype=jnp.int32)[None, :, None])
    wanted = jnp.sum(jnp.where(seat, local_ids[:, None], 0), axis=2).reshape(n * room)
    got = to_all(jnp.take(embedding, wanted, axis=0, mode="clip").reshape(n, room, width), "req")
    own_holder = lax.dynamic_index_in_dim(holder, r, 0, keepdims=False)
    order = jnp.arange(tokens, dtype=jnp.int32)
    own_turn = jnp.sum(
        ((own_holder[None, :] == own_holder[:, None]) & (order[None, :] < order[:, None])).astype(
            jnp.int32
        ),
        axis=1,
    )
    seat = jnp.where(own_turn < room, own_holder * room + own_turn, -1)
    pick = (seat[:, None] == jnp.arange(n * room, dtype=jnp.int32)[None, :]).astype(BF16)
    embed_part = jnp.dot(
        pick, got.reshape(n * room, width), preferred_element_type=F32
    ).astype(BF16)
    owners = jnp.arange(n, dtype=jnp.int32)
    load = jnp.sum((holder[:, None] == owners[None, :, None]).astype(jnp.int32), axis=2)

    def with_rest(part):
        rows = jnp.take(embedding, local_ids.reshape(n * tokens), axis=0, mode="clip")
        rest = (held & (turn >= room)).reshape(n * tokens, 1)
        rows = jnp.where(rest, rows, jnp.zeros((), BF16)).reshape(n, tokens, width)
        return (part.astype(F32) + jnp.sum(to_all(rows, "req").astype(F32), axis=0)).astype(BF16)

    embed_part = lax.cond(jnp.max(load) > room, with_rest, lambda part: part, embed_part)
    vocab_other = swap(vocab_weight.T, "head", n_head, 1)

    gains = jnp.concatenate([final_gain[None], tenant_gain], axis=0)
    gains_high, gains_low = bf16_parts(gains)
    extra = jnp.zeros((16 - 2 * gains.shape[0], width), BF16)
    embedded = lax.all_gather(
        jnp.concatenate([embed_part, gains_high, gains_low, extra], axis=0), "head", axis=1, tiled=True
    )
    gains = embedded[tokens : tokens + 5].astype(F32) + embedded[tokens + 5 : tokens + 10].astype(F32)

    ordered = lax.dynamic_slice_in_dim(ordered, r * requests, requests, 1)
    old_order = (ordered[steps] - r * requests).reshape(n_head, group).T.reshape(n, sends)
    old_order = jnp.take(old_order, jnp.arange(n) ^ r, axis=0).reshape(requests)
    counts = (2, 2) if sends == 4 else (sends,)
    pieces = sort_states(old_order, old_states, n, counts)
    live = (jnp.arange(steps)[None, :] < ordered[steps + 1][:, None]).astype(F32)
    own, kv, *parts = mixer(
        jnp.stack([r, h]), embedded, live.reshape(tokens, 1), mixer_gain[None], forget_floor[None],
        group_gain[None], (query_weight, forget_weight, input_weight, output_weight), pieces,
        steps, n_head,
    )
    arrived = [to_all(pieces[0], "req")]

    total = parts[0].astype(F32)
    for e in range(1, n_head):
        total = total + swap(parts[e], "head", n_head, e).astype(F32)
    square = total[:, D : D + 1] + total[:, D + 127 : D + 128]
    after_mixer = own.astype(F32) + total[:, :D] * lax.rsqrt(square / D + epsilon)
    after_mixer = after(after_mixer.astype(BF16), feed_weights)
    everything = lax.all_gather(after_mixer, "req", axis=0, tiled=True)
    for piece in pieces[1:]:
        piece = after(piece, after_mixer, *arrived, flops=50_000_000_000)
        arrived += [to_all(piece, "req")]

    row = jnp.arange(n * rows, dtype=jnp.int32)
    by_owner, by_group, by_step = row // rows, (row % rows) // steps, row % steps
    if sends % n_head == 0:
        offset = by_group * n_head // sends
    else:
        offset = (by_group * n_head + h) // sends
    wanted = (by_owner ^ offset) * rows + by_group * steps + by_step
    pick = (wanted[None, :] == row[:, None]).astype(BF16)
    mine = (wanted[None, :] == (r * rows + row[:rows])[:, None]).astype(BF16)
    down, kept = feed_forward(everything, feed_weights, pick, mine, feed_gain[None])
    down = after(down, *arrived)
    hidden = kept.astype(F32) + jnp.sum(to_all(down.reshape(n, rows, D), "req").astype(F32), axis=0)
    mean_square = jnp.mean(hidden * hidden, axis=1, keepdims=True)

    slots = jnp.arange(requests, dtype=jnp.int32)
    source = state_perm // requests
    rank = jnp.sum(
        ((source[None, :] == source[:, None]) & (slots[None, :] < slots[:, None])).astype(jnp.int32),
        axis=1,
    )
    place = (source ^ r) * sends + rank
    natural = source * sends + rank
    slot_of = jnp.sum(jnp.where(natural[None, :] == slots[:, None], slots[None, :], 0), axis=1)
    mine = jnp.sum(
        jnp.where(
            place[None, :] == (jnp.arange(group, dtype=jnp.int32) * n_head + h)[:, None],
            slots[None, :],
            0,
        ),
        axis=1,
    )
    tenant = jnp.sum(
        ((mine + r * requests)[:, None] >= tenant_bounds[None, 1:-1]).astype(jnp.int32), axis=1
    )
    tenant_rows = sum(
        jnp.where((tenant == t)[:, None], gains[1 + t][None, :], 0.0)
        for t in range(tenant_gain.shape[0])
    )
    token_gain = jnp.repeat(tenant_rows * gains[0][None, :], steps, axis=0)
    final = (hidden * lax.rsqrt(mean_square + epsilon) * token_gain).astype(BF16)

    kv = kv.reshape(n, -1, width)
    kv = jnp.stack([kv[0]] + [swap(kv[k], "req", n, k) for k in range(1, n)])
    new_states = update_states(
        r[None], slot_of, kv.reshape(requests, 2 * steps, width).astype(F32), arrived, steps
    )
    final = after(final, new_states)
    c1, c2 = D * 7 // 16, D * 13 // 16
    full = jnp.concatenate(
        [
            gather_by(final[:, :c1], ("outer", "inner", "cross"), n, n_head),
            gather_by(final[:, c1:c2], ("cross", "outer", "inner"), n, n_head),
            gather_by(final[:, c2:], ("inner", "cross", "outer"), n, n_head),
        ],
        axis=-1,
    ).reshape(n * 2 * rows, D)
    best = greatest_entries(r[None], n, full, vocab_weight.T, vocab_other)
    got = jnp.max(to_all(best, "req"), axis=0)
    got = lax.all_gather(got, "head", axis=0).reshape(n_head, 2, rows)
    crossed = jnp.stack([got[i ^ 2, 1] for i in range(n_head)])
    best = jnp.maximum(got[:, 0], crossed).reshape(requests, steps)
    index = (place % n_head) * group + place // n_head
    match = (index[:, None] == slots[None, :])[:, :, None]
    best = jnp.sum(jnp.where(match, best[None], 0.0), axis=1)
    live = jnp.arange(steps)[None, :] < token_count[:, None]
    greatest = jnp.max(jnp.where(live, best, -1e30), axis=1)

    blocks = hidden.reshape(rows, n_head, width).transpose(1, 0, 2)
    tail = jnp.broadcast_to(mean_square, (rows, 128))
    whole = []
    for e in range(n_head):
        block = lax.dynamic_index_in_dim(blocks, h ^ e, 0, keepdims=False)
        block = jnp.concatenate([block, tail], axis=1)
        whole.append(block if e == 0 else swap(block, "head", n_head, e))
    whole = jnp.stack(whole).reshape(requests, steps, width + 128)
    index = ((place % n_head) ^ h) * group + place // n_head
    whole = jnp.take(whole, index, axis=0, mode="clip")
    last = jnp.arange(steps)[None, :] == (token_count - 1)[:, None]
    last_norm = jnp.sqrt(jnp.sum(jnp.where(last, whole[:, :, width], 0.0), axis=1) + epsilon)

    return whole[:, :, :width], new_states, last_norm, greatest


def solution(mesh):
    placed = (
        P("req", None),
        P("req"),
        P("req"),
        P(),
        P("req", "head", None, None),
        P("req", "head"),
        P(),
        P(None, "head"),
        P(None, "head"),
        P(None, "head"),
        P("head"),
        P("head"),
        P("head", None),
        P(),
        P("head", "req"),
        P("head", "req"),
        P("req", "head"),
        P("head"),
        P(None, "head"),
        P(None, ("req", "head")),
    )
    return jax.shard_map(
        on_device,
        mesh=mesh,
        in_specs=placed,
        out_specs=(P("req", None, "head"), P("req", "head", None, None), P("req"), P("req")),
        check_vma=False,
    )
```
